512 devices in a mesh: row: 16 (over x, z_hi), col: 32 (over y, z_lo, core).
Axes of the slice: x: 4, y: 4, z: 16 (z_hi: 4, z_lo: 4; z = z_hi * 4 + z_lo), core: 2. Of those that a mesh axis runs over, the one named last changes fastest.
Arguments:
- momentum: bfloat16 [3584, 18432], P('row', 'col'), may hold values from -0.0390625 to 0.0390625
Outputs:
- update: bfloat16 [3584, 18432], P('row', 'col')
The draws below stay inside these ranges and needn't reach their ends.
All inputs are finite; a program needn't handle non-finite values.
Results may differ from the reference program's by a relative error of at most 0.0088.
Values may be sent and summed in bfloat16 or wider, within the bound.
A program may use at most 64 MiB of HBM per device.

```python
import jax
import jax.numpy as jnp

NR = 3584
NC = 18432


def levels(own_key, shape, cuts, low, largest):
    factor_of = 1.0
    for position, shards_of in cuts:
        heights = jax.random.uniform(jax.random.fold_in(jax.random.fold_in(own_key, 6), position), (shards_of,), jnp.float32, low / len(cuts), largest / len(cuts))
        factor_of = factor_of * jnp.repeat(jnp.exp(heights), shape[position] // shards_of).reshape((-1,) + (1,) * (len(shape) - 1 - position))
    return factor_of


def scatter_about(key, extent, scale, reach, split=(), dtype=jnp.bfloat16):
    values = scale * jax.random.normal(key, extent, jnp.float32)
    if split:
        values = values * levels(key, extent, split, -0.22, 0.18)
    return jnp.clip(values, -reach, reach).astype(dtype)


def setup_inputs(seed: int = 0) -> dict:
    streams_of = jax.random.split(jax.random.key(seed), 2)
    momentum = scatter_about(streams_of[0], (NR, NC), (NR + NC) ** -0.5, 0.0390625, ((0, 16), (1, 32)))
    return dict(momentum=momentum)


coef_a = 3.4445
coef_b = -4.7750
coef_c = 2.0315


def reference(momentum):
    gram = jnp.dot(momentum, momentum.T, preferred_element_type=jnp.float32).astype(jnp.bfloat16)
    square = jnp.dot(gram, gram, preferred_element_type=jnp.float32)
    poly = (coef_b * gram.astype(jnp.float32) + coef_c * square).astype(jnp.bfloat16)
    product = jnp.dot(poly, momentum, preferred_element_type=jnp.float32)
    factor = 0.2 * (max(NR, NC) ** 0.5)
    return (factor * (coef_a * momentum.astype(jnp.float32) + product)).astype(jnp.bfloat16)
```

```python
import jax
import jax.numpy as jnp
from jax import lax
from jax.experimental import pallas as pl
from jax.experimental.pallas import tpu as pltpu
from jax.sharding import PartitionSpec as P

NR = 3584
NC = 18432

coef_a = 3.4445
coef_b = -4.775
coef_c = 2.0315
factor = 0.2 * max(NR, NC) ** 0.5

MESH = pl.DeviceIdType.MESH

B = 224
H = 112
W = 576
TILES = 4
PACK = TILES * B + H
CUTS = ((0, 256), (256, 256), (512, 256), (768, 240))
UP = (0, 1)
DOWN = (2, 3)


def nt_dot(a, b):
    return lax.dot_general(a, b, (((1,), (1,)), ((), ())), preferred_element_type=jnp.float32)


def nn_dot(a, b):
    return lax.dot_general(a, b, (((1,), (0,)), ((), ())), preferred_element_type=jnp.float32)


def kernel(
    x_ref,
    o_ref,
    xs,
    part,
    send1,
    recv1,
    send2,
    recv2,
    sum2,
    send3,
    recv3,
    gr,
    gc,
    pr,
    acc,
    xsend,
    xrecv,
    rsend,
    rrecv,
    gsend,
    grecv,
    psend,
    precv,
):
    row = lax.axis_index("row")
    col = lax.axis_index("col")
    x, zh = row // 4, row % 4
    y, zl, k = col // 8, (col // 2) % 4, col % 2

    def at(dx=0, dzh=0, dy=0, dzl=0, dk=0):
        return (
            ((x + dx) % 4) * 4 + (zh + dzh) % 4,
            ((y + dy) % 4) * 8 + ((zl + dzl) % 4) * 2 + (k + dk) % 2,
        )

    started = []

    def send(src, dst, ssem, rsem, device):
        copy = pltpu.make_async_remote_copy(
            src_ref=src, dst_ref=dst, send_sem=ssem, recv_sem=rsem, device_id=device, device_id_type=MESH
        )
        copy.start()
        started.append(copy)

    def arrived(dst, rsem):
        pltpu.make_async_copy(dst, dst, rsem).wait()

    def unpack(zp, xp):
        tiles = [xs[zp, xp, pl.ds(t * B, B), :] for t in range(TILES)]
        last = xs[zp, xp, pl.ds(TILES * B, H), :]
        tiles.append(jnp.concatenate([last[:, :64], last[:, 64:]], axis=0))
        return jnp.concatenate(tiles, axis=1)

    for t in range(TILES):
        xs[zh, x, pl.ds(t * B, B), :] = x_ref[:, pl.ds(t * 128, 128)]
    xs[zh, x, pl.ds(TILES * B, H), :] = jnp.concatenate(
        [x_ref[pl.ds(0, H), pl.ds(TILES * 128, 64)], x_ref[pl.ds(H, H), pl.ds(TILES * 128, 64)]], axis=1
    )

    barrier = pltpu.get_barrier_semaphore()
    peers = [at(dx=d) for d in (1, 2, 3)] + [at(dzh=d) for d in (1, 2, 3)]
    peers += [at(dy=d) for d in (1, 2, 3)] + [at(dzl=d) for d in (1, 2, 3)] + [at(dk=1)]
    for peer in peers:
        pl.semaphore_signal(barrier, 1, device_id=peer, device_id_type=MESH)
    pl.semaphore_wait(barrier, len(peers))

    def xpiece(dz, dx, ch):
        start, size = CUTS[ch]
        return xs.at[(zh + dz) % 4, (x + dx) % 4, pl.ds(start, size)]

    def xmove(kind, dz, dx, ch, hop_z, hop_x):
        there = ((dz - hop_z) % 4, (dx - hop_x) % 4)
        piece = xpiece(dz, dx, ch)
        send(piece, piece, xsend.at[kind, dz, ch], xrecv.at[there[0], there[1], ch], at(dx=hop_x, dzh=hop_z))

    def xwait(dz, dx, ch):
        arrived(xpiece(dz, dx, ch), xrecv.at[dz, dx, ch])

    def x_spread(dz, ch):
        xmove(0, dz, 0, ch, 0, 1)
        xmove(1, dz, 0, ch, 0, 3)

    def x_forward(dz, ch):
        if ch in UP:
            xwait(dz, 3, ch)
            xmove(2, dz, 3, ch, 0, 1)
        else:
            xwait(dz, 1, ch)
            xmove(2, dz, 1, ch, 0, 3)

    def x_rest(dz):
        for ch in range(4):
            xwait(dz, 1 if ch in UP else 3, ch)
            xwait(dz, 2, ch)

    def z_forward(ch):
        if ch in UP:
            xwait(3, 0, ch)
            xmove(4, 3, 0, ch, 1, 0)
            x_spread(3, ch)
        else:
            xwait(1, 0, ch)
            xmove(4, 1, 0, ch, 3, 0)
            x_spread(1, ch)

    def z_last(ch):
        dz = 1 if ch in UP else 3
        xwait(dz, 0, ch)
        x_spread(dz, ch)

    def gram(dz):
        zp = (zh + dz) % 4

        def step(xp, carry):
            part[dz, xp] = nt_dot(x_ref[...], unpack(zp, xp))
            send1[dz, xp] = part[dz, xp, pl.ds((1 - k) * H, H), :].astype(jnp.bfloat16)
            return carry

        lax.fori_loop(0, 4, step, 0)
        send(send1.at[dz], recv1.at[dz], rsend.at[0, dz], rrecv.at[0, dz], at(dk=1))

    def reduce_core(dz):
        arrived(recv1.at[dz], rrecv.at[0, dz])

        def both(xp):
            return part[dz, xp, pl.ds(k * H, H), :] + recv1[dz, xp].astype(jnp.float32)

        for dy in (1, 2, 3):
            send2[dz, dy - 1] = both((y + dy) % 4).astype(jnp.bfloat16)
            send(send2.at[dz, dy - 1], recv2.at[dz, dy - 1], rsend.at[dy, dz], rrecv.at[dy, dz], at(dy=dy))
        sum2[dz] = both(y)

    def reduce_y(dz):
        for dy in (1, 2, 3):
            arrived(recv2.at[dz, dy - 1], rrecv.at[dy, dz])
        total = sum2[dz]
        for dy in (1, 2, 3):
            total = total + recv2[dz, dy - 1].astype(jnp.float32)
        sum2[dz] = total

    for n in range(2):
        xmove(3, 0, 0, UP[n], 1, 0)
        xmove(5, 0, 0, DOWN[n], 3, 0)
        xmove(0, 0, 0, UP[n], 0, 1)
        xmove(1, 0, 0, DOWN[n], 0, 3)
    for n in range(2):
        xmove(3, 0, 0, DOWN[n], 1, 0)
        xmove(5, 0, 0, UP[n], 3, 0)
        xmove(0, 0, 0, DOWN[n], 0, 1)
        xmove(1, 0, 0, UP[n], 0, 3)
    for n in range(2):
        x_forward(0, UP[n])
        x_forward(0, DOWN[n])
    z_forward(UP[0])
    z_forward(DOWN[0])
    x_rest(0)
    gram(0)
    z_forward(UP[1])
    z_forward(DOWN[1])
    reduce_core(0)
    x_forward(3, UP[0])
    x_forward(1, DOWN[0])
    x_forward(3, UP[1])
    x_forward(1, DOWN[1])
    z_last(DOWN[0])
    z_last(UP[0])
    reduce_y(0)
    z_last(DOWN[1])
    z_last(UP[1])
    x_forward(3, DOWN[0])
    x_forward(1, UP[0])
    xwait(2, 0, UP[0])
    x_spread(2, UP[0])
    xwait(2, 0, DOWN[0])
    x_spread(2, DOWN[0])
    x_forward(3, DOWN[1])
    x_forward(1, UP[1])
    x_rest(3)
    gram(3)
    x_rest(1)
    gram(1)
    x_forward(2, UP[0])
    x_forward(2, DOWN[0])
    reduce_core(3)
    reduce_core(1)
    xwait(2, 0, UP[1])
    x_spread(2, UP[1])
    xwait(2, 0, DOWN[1])
    x_spread(2, DOWN[1])
    reduce_y(3)
    reduce_y(1)
    x_forward(2, UP[1])
    x_forward(2, DOWN[1])
    x_rest(2)
    gram(2)
    reduce_core(2)
    reduce_y(2)

    for d in (1, 2, 3):
        send3[d - 1] = sum2[(zl + d - zh + 4) % 4].astype(jnp.bfloat16)
        send(send3.at[d - 1], recv3.at[d - 1], rsend.at[4, d], rrecv.at[4, d], at(dzl=d))
    total = sum2[(zl - zh + 4) % 4]
    for d in (1, 2, 3):
        arrived(recv3.at[d - 1], rrecv.at[4, d])
        total = total + recv3[d - 1].astype(jnp.float32)
    tile = total.astype(jnp.bfloat16)

    gr[zl, y] = tile
    gc[zh, k, x] = tile

    def row_move(buf, ssem, rsem, dzl, hop_zl, hop_y):
        piece = buf((zl + dzl) % 4, y)
        kind = hop_zl if hop_zl else 3 + hop_y
        there = ((dzl - hop_zl) % 4, (0 - hop_y) % 4)
        send(piece, piece, ssem.at[kind, dzl], rsem.at[there[0], there[1]], at(dzl=hop_zl, dy=hop_y))

    def gr_at(zp, yp):
        return gr.at[zp, yp]

    def gc_move(dz, hop_z, hop_x):
        piece = gc.at[(zh + dz) % 4, k, x]
        kind = 7 + (hop_z if hop_z else 3 + hop_x)
        there = ((dz - hop_z) % 4, (0 - hop_x) % 4)
        send(piece, piece, gsend.at[kind, dz], grecv.at[4 + there[0], there[1]], at(dzh=hop_z, dx=hop_x))

    for d in (1, 3, 2):
        gc_move(0, d, 0)
        row_move(gr_at, gsend, grecv, 0, d, 0)
    for d in (1, 3, 2):
        gc_move(0, 0, d)
        row_move(gr_at, gsend, grecv, 0, 0, d)
    for n in (3, 1, 2):
        arrived(gr.at[(zl + n) % 4, y], grecv.at[n, 0])
        for d in (1, 3, 2):
            row_move(gr_at, gsend, grecv, n, 0, d)
    for n in (3, 1, 2):
        arrived(gc.at[(zh + n) % 4, k, x], grecv.at[4 + n, 0])
        for d in (1, 3, 2):
            gc_move(n, 0, d)
    for n in (0, 3, 1, 2):
        zp = (zh + n) % 4
        for d in (1, 3, 2):
            arrived(gc.at[zp, k, (x + d) % 4], grecv.at[4 + n, d])
        send(gc.at[zp, k], gc.at[zp, k], gsend.at[14, n], grecv.at[8, n], at(dk=1))
    for n in range(4):
        for d in (1, 3, 2):
            arrived(gr.at[(zl + n) % 4, (y + d) % 4], grecv.at[n, d])
    for n in range(4):
        zp = (zh + n) % 4
        arrived(gc.at[zp, 1 - k], grecv.at[8, n])

    square = jnp.zeros((H, B), jnp.float32)
    for zp in range(4):
        for xp in range(4):
            right = jnp.concatenate([gc[zp, 0, xp], gc[zp, 1, xp]], axis=0)
            square = square + nn_dot(gr[zp, xp], right)
    pr[zl, k, y] = (coef_b * gr[zl, y].astype(jnp.float32) + coef_c * square).astype(jnp.bfloat16)

    def pr_at(zp, yp):
        return pr.at[zp, k, yp]

    for d in (1, 3, 2):
        row_move(pr_at, psend, precv, 0, d, 0)
    for d in (1, 3, 2):
        row_move(pr_at, psend, precv, 0, 0, d)
    for n in (3, 1, 2):
        arrived(pr_at((zl + n) % 4, y), precv.at[n, 0])
        for d in (1, 3, 2):
            row_move(pr_at, psend, precv, n, 0, d)
    for n in (0, 3, 1, 2):
        zp = (zl + n) % 4
        for d in (1, 3, 2):
            arrived(pr_at(zp, (y + d) % 4), precv.at[n, d])
        send(pr.at[zp, k], pr.at[zp, k], psend.at[7, n], precv.at[4, n], at(dk=1))

    for n, d in enumerate((0, 3, 1, 2)):
        zp = (zl + d) % 4
        arrived(pr.at[zp, 1 - k], precv.at[4, d])

        def step(xp, carry, zp=zp, first=n == 0):
            left = jnp.concatenate([pr[zp, 0, xp], pr[zp, 1, xp]], axis=0)
            acc[...] += nn_dot(left, unpack(zp, xp))
            return carry

        if n == 0:
            acc[...] = coef_a * x_ref[...].astype(jnp.float32)
        lax.fori_loop(0, 4, step, 0)
    o_ref[...] = (factor * acc[...]).astype(jnp.bfloat16)

    for copy in started:
        copy.wait_send()


def on_device(momentum):
    bf16, f32 = jnp.bfloat16, jnp.float32
    dma = pltpu.SemaphoreType.DMA
    return pl.pallas_call(
        kernel,
        out_shape=jax.ShapeDtypeStruct((B, W), bf16),
        in_specs=[pl.BlockSpec(memory_space=pltpu.VMEM)],
        out_specs=pl.BlockSpec(memory_space=pltpu.VMEM),
        scratch_shapes=[
            pltpu.VMEM((4, 4, PACK, 128), bf16),
            pltpu.VMEM((4, 4, B, B), f32),
            pltpu.VMEM((4, 4, H, B), bf16),
            pltpu.VMEM((4, 4, H, B), bf16),
            pltpu.VMEM((4, 3, H, B), bf16),
            pltpu.VMEM((4, 3, H, B), bf16),
            pltpu.VMEM((4, H, B), f32),
            pltpu.VMEM((3, H, B), bf16),
            pltpu.VMEM((3, H, B), bf16),
            pltpu.VMEM((4, 4, H, B), bf16),
            pltpu.VMEM((4, 2, 4, H, B), bf16),
            pltpu.VMEM((4, 2, 4, H, B), bf16),
            pltpu.VMEM((B, W), f32),
            dma((6, 4, 4)),
            dma((4, 4, 4)),
            dma((5, 4)),
            dma((5, 4)),
            dma((15, 4)),
            dma((9, 4)),
            dma((8, 4)),
            dma((5, 4)),
        ],
        compiler_params=pltpu.CompilerParams(
            collective_id=0, has_side_effects=True, vmem_limit_bytes=48 * 2**20
        ),
        cost_estimate=pl.CostEstimate(flops=4 * 10**9, bytes_accessed=2 * 10**7, transcendentals=0),
    )(momentum)


def solution(mesh):
    return jax.shard_map(
        on_device, mesh=mesh, in_specs=(P("row", "col"),), out_specs=P("row", "col"), check_vma=False
    )
```

```python
import jax
import jax.numpy as jnp
from jax import lax
from jax.experimental import pallas as pl
from jax.experimental.pallas import tpu as pltpu
from jax.sharding import PartitionSpec as P

NR = 3584
NC = 18432

coef_a = 3.4445
coef_b = -4.775
coef_c = 2.0315
factor = 0.2 * max(NR, NC) ** 0.5

MESH = pl.DeviceIdType.MESH

B = 224
H = 112
W = 576
TILES = 4
PACK = TILES * B + H
LOW = (0, 2 * B)
HIGH = (2 * B, 2 * B + H)
REST = (TILES * B, H)


def nt_dot(a, b):
    return lax.dot_general(a, b, (((1,), (1,)), ((), ())), preferred_element_type=jnp.float32)


def nn_dot(a, b):
    return lax.dot_general(a, b, (((1,), (0,)), ((), ())), preferred_element_type=jnp.float32)


def kernel(
    x_ref,
    o_ref,
    xs,
    part,
    send1,
    recv1,
    send2,
    recv2,
    sum2,
    send3,
    recv3,
    swap_send,
    swap_recv,
    flip_send,
    flip_recv,
    swap_sum,
    flip_sum,
    gr,
    gc,
    pr,
    acc,
    zsend,
    zrecv,
    xsend,
    xrecv,
    rsend,
    rrecv,
    tsend,
    trecv,
    gsend,
    grecv,
    psend,
    precv,
):
    row = lax.axis_index("row")
    col = lax.axis_index("col")
    x, zh = row // 4, row % 4
    y, zl, k = col // 8, (col // 2) % 4, col % 2
    sign = 1 + 2 * (zl % 2)

    def place(x_, zh_, y_, zl_, k_):
        return (x_ * 4 + zh_, y_ * 8 + zl_ * 2 + k_)

    def at(dx=0, dzh=0, dy=0, dzl=0, dk=0):
        return place((x + dx) % 4, (zh + dzh) % 4, (y + dy) % 4, (zl + dzl) % 4, (k + dk) % 2)

    def station(dz):
        return (zh + sign * dz) % 4

    started = []

    def send(src, dst, ssem, rsem, device):
        copy = pltpu.make_async_remote_copy(
            src_ref=src, dst_ref=dst, send_sem=ssem, recv_sem=rsem, device_id=device, device_id_type=MESH
        )
        copy.start()
        started.append(copy)

    def arrived(dst, rsem):
        pltpu.make_async_copy(dst, dst, rsem).wait()

    def rest(zp, xp):
        last = xs[zp, xp, pl.ds(TILES * B, H), :]
        return jnp.concatenate([last[:, :64], last[:, 64:]], axis=0)

    def tile_of(zp, xp, t):
        return xs[zp, xp, pl.ds(pl.multiple_of(t * B, 16), B), :]

    def unpack(zp, xp):
        return jnp.concatenate([tile_of(zp, xp, t) for t in range(TILES)] + [rest(zp, xp)], axis=1)

    for t in range(TILES):
        xs[zh, x, pl.ds(t * B, B), :] = x_ref[:, pl.ds(t * 128, 128)]
    xs[zh, x, pl.ds(TILES * B, H), :] = jnp.concatenate(
        [x_ref[pl.ds(0, H), pl.ds(TILES * 128, 64)], x_ref[pl.ds(H, H), pl.ds(TILES * 128, 64)]], axis=1
    )

    barrier = pltpu.get_barrier_semaphore()
    peers = [at(dx=d) for d in (1, 2, 3)] + [at(dzh=d) for d in (1, 2, 3)]
    peers += [at(dy=d) for d in (1, 2, 3)] + [at(dzl=d) for d in (1, 2, 3)] + [at(dk=1)]
    swap_peer = place(y, zh, x, zl, k)
    flip_peers = [place(x, zl, y, zh, n) for n in range(2)]
    for peer in peers:
        pl.semaphore_signal(barrier, 1, device_id=peer, device_id_type=MESH)

    @pl.when(x != y)
    def _():
        pl.semaphore_signal(barrier, 1, device_id=swap_peer, device_id_type=MESH)

    @pl.when(zh != zl)
    def _():
        for peer in flip_peers:
            pl.semaphore_signal(barrier, 1, device_id=peer, device_id_type=MESH)

    pl.semaphore_wait(barrier, len(peers) + jnp.where(x != y, 1, 0) + jnp.where(zh != zl, 2, 0))

    def rows(dz, dx, start, size):
        return xs.at[station(dz), (x + dx) % 4, pl.ds(start, size)]

    def zmove(sem, dz, start, size, hop, rsem):
        piece = rows(dz, 0, start, size)
        send(piece, piece, zsend.at[sem], rsem, at(dzh=sign * hop))

    def xmove(kind, dz, dx, part_, hop):
        piece = rows(dz, dx, *(LOW, HIGH)[part_])
        send(piece, piece, xsend.at[kind, dz, part_], xrecv.at[dz, (dx - hop) % 4, part_], at(dx=hop))

    def xwait(dz, dx, part_):
        arrived(rows(dz, dx, *(LOW, HIGH)[part_]), xrecv.at[dz, dx, part_])

    def x_spread(dz, part_):
        xmove(0, dz, 0, part_, 1)
        xmove(1, dz, 0, part_, 3)

    def x_forward(dz, part_):
        source, hop = ((3, 1), (1, 3))[part_]
        xwait(dz, source, part_)
        xmove(2, dz, source, part_, hop)

    def x_rest(dz):
        for part_, source in ((0, 1), (1, 3)):
            xwait(dz, source, part_)
            xwait(dz, 2, part_)

    def tile_rows(t):
        return pl.multiple_of(t * B, 16)

    def zwait(dz, t):
        arrived(rows(dz, 0, tile_rows(t), B), zrecv.at[dz, t])

    def zwait_rest(dz):
        arrived(rows(dz, 0, *REST), zrecv.at[dz, 4])

    half = zh // 2
    half_before = ((zh + 4 - sign) % 4) // 2
    half_after = ((zh + sign) % 4) // 2

    def gram(dz):
        zp = station(dz)

        def step(xp, carry):
            if dz == 0:
                left, right = unpack(zh, xp), unpack(zh, x)
                value = 0.5 * nt_dot(left, right)
            elif dz == 1:
                left, right = [jnp.concatenate([tile_of(*b, t) for t in (0, 1)], axis=1) for b in ((zh, xp), (zp, x))]
                value = nt_dot(left, right)
            elif dz == 3:
                left, right = [
                    jnp.concatenate([tile_of(*b, t) for t in (2, 3)] + [rest(*b)], axis=1) for b in ((zh, xp), (zp, x))
                ]
                value = nt_dot(left, right)
            else:
                left, right = [
                    jnp.concatenate([tile_of(*b, half), tile_of(*b, 2 + half)], axis=1) for b in ((zh, xp), (zp, x))
                ]
                value = nt_dot(left, right) + 0.5 * nt_dot(rest(zh, xp), rest(zp, x))
            part[dz, xp] = value
            send1[dz, xp] = part[dz, xp, pl.ds(pl.multiple_of((1 - k) * H, 16), H), :].astype(jnp.bfloat16)
            return carry

        lax.fori_loop(0, 4, step, 0)
        send(send1.at[dz], recv1.at[dz], rsend.at[0, dz], rrecv.at[0, dz], at(dk=1))

    def reduce_core(dz):
        arrived(recv1.at[dz], rrecv.at[0, dz])

        def both(xp):
            return part[dz, xp, pl.ds(pl.multiple_of(k * H, 16), H), :] + recv1[dz, xp].astype(jnp.float32)

        for dy in (2, 1, 3):
            send2[dz, dy - 1] = both((y + dy) % 4).astype(jnp.bfloat16)
            send(send2.at[dz, dy - 1], recv2.at[dz, dy - 1], rsend.at[dy, dz], rrecv.at[dy, dz], at(dy=dy))
        sum2[dz] = both(y)

    def sum3(dz):
        owner = station(dz)
        d = (owner + 4 - zl) % 4
        copy = pltpu.make_async_remote_copy(
            src_ref=send3.at[dz],
            dst_ref=recv3.at[d],
            send_sem=rsend.at[4, dz],
            recv_sem=rrecv.at[4, d],
            device_id=place(x, zh, y, owner, k),
            device_id_type=MESH,
        )
        return d, copy

    def reduce_y(dz):
        for dy in (1, 3, 2):
            arrived(recv2.at[dz, dy - 1], rrecv.at[dy, dz])
        total = sum2[dz]
        for dy in (1, 2, 3):
            total = total + recv2[dz, dy - 1].astype(jnp.float32)
        sum2[dz] = total
        send3[dz] = total.astype(jnp.bfloat16)
        d, copy = sum3(dz)

        @pl.when(d != 0)
        def _():
            copy.start()

    for t in (0, 1):
        zmove((0, t), 0, t * B, B, 3, zrecv.at[1, t])
        zmove((0, 2 + t), 0, (2 + t) * B, B, 1, zrecv.at[3, 2 + t])
        xmove(t, 0, 0, t, 1 + 2 * t)
    zmove((0, 4), 0, *REST, 1, zrecv.at[3, 4])
    for t in (0, 1):
        xmove(1 - t, 0, 0, t, 3 - 2 * t)
    x_forward(0, 0)
    x_forward(0, 1)
    zwait(1, half_before)
    zmove((2, 0), 1, tile_rows(half_before), B, 3, zrecv.at[2, half_before])
    zwait(3, 2 + half_after)
    zmove((2, 1), 3, tile_rows(2 + half_after), B, 1, zrecv.at[2, 2 + half_after])
    zwait_rest(3)
    zmove((2, 2), 3, *REST, 1, zrecv.at[2, 4])
    x_rest(0)
    gram(0)
    zwait(1, 1 - half_before)
    gram(1)
    x_spread(1, 0)
    zwait(3, 3 - half_after)
    gram(3)
    x_spread(3, 1)
    reduce_core(0)
    reduce_core(1)
    reduce_core(3)
    reduce_y(0)
    zwait(2, half)
    zwait(2, 2 + half)
    zwait_rest(2)
    gram(2)
    zmove((1, 0), 0, *HIGH, 3, zrecv.at[1, 2])
    zmove((1, 1), 0, *LOW, 1, zrecv.at[3, 0])
    zmove((3, 0), 1, tile_rows(1 - half_before), B, 3, zrecv.at[2, 1 - half_before])
    zmove((3, 1), 3, tile_rows(3 - half_after), B, 1, zrecv.at[2, 3 - half_after])
    reduce_y(1)
    reduce_y(3)
    x_forward(1, 0)
    x_forward(3, 1)
    reduce_core(2)
    reduce_y(2)

    total = sum2[(sign * (zl + 4 - zh)) % 4]
    for d in (1, 2, 3):
        arrived(recv3.at[d], rrecv.at[4, d])
        total = total + recv3[d].astype(jnp.float32)

    swap_send[...] = total.astype(jnp.bfloat16)
    flipped = total.T
    for n in range(2):
        flip_send[n] = flipped[n * H : (n + 1) * H, :].astype(jnp.bfloat16)
    swap_copy = pltpu.make_async_remote_copy(
        src_ref=swap_send,
        dst_ref=swap_recv,
        send_sem=tsend.at[0],
        recv_sem=trecv.at[0],
        device_id=swap_peer,
        device_id_type=MESH,
    )

    def flip_copy(n):
        return pltpu.make_async_remote_copy(
            src_ref=flip_send.at[n],
            dst_ref=flip_recv.at[k],
            send_sem=tsend.at[1 + n],
            recv_sem=trecv.at[1 + k],
            device_id=place(x, zl, y, zh, n),
            device_id_type=MESH,
        )

    @pl.when(x != y)
    def _():
        swap_copy.start()

    @pl.when(x == y)
    def _():
        swap_sum[...] = total

    flip_copy(1 - k).start()

    @pl.when(zh != zl)
    def _():
        flip_copy(k).start()

    @pl.when(zh == zl)
    def _():
        swap_send2 = jnp.where(k == 0, flipped[:H, :], flipped[H:, :])
        flip_sum[k] = swap_send2

    arrived(rows(1, 0, *HIGH), zrecv.at[1, 2])
    x_spread(1, 1)
    arrived(rows(3, 0, *LOW), zrecv.at[3, 0])
    x_spread(3, 0)

    @pl.when(x != y)
    def _():
        arrived(swap_recv, trecv.at[0])
        swap_sum[...] = swap_recv[...].astype(jnp.float32)

    @pl.when(zh != zl)
    def _():
        arrived(flip_recv.at[k], trecv.at[1 + k])
        flip_sum[k] = flip_recv[k].astype(jnp.float32)

    arrived(flip_recv.at[1 - k], trecv.at[2 - k])
    flip_sum[1 - k] = flip_recv[1 - k].astype(jnp.float32)
    tile = (swap_sum[...] + jnp.concatenate([flip_sum[0], flip_sum[1]], axis=1)).astype(jnp.bfloat16)

    gr[zl, y] = tile
    gc[zh, k, x] = tile

    def row_move(buf, ssem, rsem, dzl, hop_zl, hop_y):
        piece = buf((zl + dzl) % 4, y)
        kind = hop_zl if hop_zl else 3 + hop_y
        there = ((dzl - hop_zl) % 4, (0 - hop_y) % 4)
        send(piece, piece, ssem.at[kind, dzl], rsem.at[there[0], there[1]], at(dzl=hop_zl, dy=hop_y))

    def gr_at(zp, yp):
        return gr.at[zp, yp]

    def gc_move(dz, hop_z, hop_x):
        piece = gc.at[(zh + dz) % 4, k, x]
        kind = 7 + (hop_z if hop_z else 3 + hop_x)
        there = ((dz - hop_z) % 4, (0 - hop_x) % 4)
        send(piece, piece, gsend.at[kind, dz], grecv.at[4 + there[0], there[1]], at(dzh=hop_z, dx=hop_x))

    for d in (1, 3, 2):
        gc_move(0, d, 0)
        row_move(gr_at, gsend, grecv, 0, d, 0)
    for d in (1, 3, 2):
        gc_move(0, 0, d)
        row_move(gr_at, gsend, grecv, 0, 0, d)
    for n in (3, 1, 2):
        arrived(gr.at[(zl + n) % 4, y], grecv.at[n, 0])
        for d in (1, 3, 2):
            row_move(gr_at, gsend, grecv, n, 0, d)
    for n in (3, 1, 2):
        arrived(gc.at[(zh + n) % 4, k, x], grecv.at[4 + n, 0])
        for d in (1, 3, 2):
            gc_move(n, 0, d)
    for n in (0, 3, 1, 2):
        zp = (zh + n) % 4
        for d in (1, 3, 2):
            arrived(gc.at[zp, k, (x + d) % 4], grecv.at[4 + n, d])
        send(gc.at[zp, k], gc.at[zp, k], gsend.at[14, n], grecv.at[8, n], at(dk=1))
    for n in range(4):
        for d in (1, 3, 2):
            arrived(gr.at[(zl + n) % 4, (y + d) % 4], grecv.at[n, d])
    for n in range(4):
        zp = (zh + n) % 4
        arrived(gc.at[zp, 1 - k], grecv.at[8, n])

    square = jnp.zeros((H, B), jnp.float32)
    for zp in range(4):
        for xp in range(4):
            right = jnp.concatenate([gc[zp, 0, xp], gc[zp, 1, xp]], axis=0)
            square = square + nn_dot(gr[zp, xp], right)
    zwait(2, 1 - half)
    zwait(2, 3 - half)
    pr[zl, k, y] = (coef_b * gr[zl, y].astype(jnp.float32) + coef_c * square).astype(jnp.bfloat16)

    def pr_at(zp, yp):
        return pr.at[zp, k, yp]

    for d in (1, 3, 2):
        row_move(pr_at, psend, precv, 0, d, 0)
    for d in (1, 3, 2):
        row_move(pr_at, psend, precv, 0, 0, d)
    x_spread(2, 0)
    x_spread(2, 1)
    x_forward(1, 1)
    x_forward(3, 0)
    for n in (3, 1, 2):
        arrived(pr_at((zl + n) % 4, y), precv.at[n, 0])
        for d in (1, 3, 2):
            row_move(pr_at, psend, precv, n, 0, d)
    for n in (0, 3, 1, 2):
        zp = (zl + n) % 4
        for d in (1, 3, 2):
            arrived(pr_at(zp, (y + d) % 4), precv.at[n, d])
        send(pr.at[zp, k], pr.at[zp, k], psend.at[7, n], precv.at[4, n], at(dk=1))

    x_forward(2, 0)
    x_forward(2, 1)
    for dz in (1, 3, 2):
        x_rest(dz)

    for n, d in enumerate((0, 3, 1, 2)):
        zp = (zl + d) % 4
        arrived(pr.at[zp, 1 - k], precv.at[4, d])

        def step(xp, carry, zp=zp, first=n == 0):
            left = jnp.concatenate([pr[zp, 0, xp], pr[zp, 1, xp]], axis=0)
            acc[...] += nn_dot(left, unpack(zp, xp))
            return carry

        if n == 0:
            acc[...] = coef_a * x_ref[...].astype(jnp.float32)
        lax.fori_loop(0, 4, step, 0)
    o_ref[...] = (factor * acc[...]).astype(jnp.bfloat16)

    for copy in started:
        copy.wait_send()
    for dz in range(4):
        d, copy = sum3(dz)

        @pl.when(d != 0)
        def _(copy=copy):
            copy.wait_send()

    flip_copy(1 - k).wait_send()

    @pl.when(zh != zl)
    def _():
        flip_copy(k).wait_send()

    @pl.when(x != y)
    def _():
        swap_copy.wait_send()


def on_device(momentum):
    bf16, f32 = jnp.bfloat16, jnp.float32
    dma = pltpu.SemaphoreType.DMA
    return pl.pallas_call(
        kernel,
        out_shape=jax.ShapeDtypeStruct((B, W), bf16),
        in_specs=[pl.BlockSpec(memory_space=pltpu.VMEM)],
        out_specs=pl.BlockSpec(memory_space=pltpu.VMEM),
        scratch_shapes=[
            pltpu.VMEM((4, 4, PACK, 128), bf16),
            pltpu.VMEM((4, 4, B, B), f32),
            pltpu.VMEM((4, 4, H, B), bf16),
            pltpu.VMEM((4, 4, H, B), bf16),
            pltpu.VMEM((4, 3, H, B), bf16),
            pltpu.VMEM((4, 3, H, B), bf16),
            pltpu.VMEM((4, H, B), f32),
            pltpu.VMEM((4, H, B), bf16),
            pltpu.VMEM((4, H, B), bf16),
            pltpu.VMEM((H, B), bf16),
            pltpu.VMEM((H, B), bf16),
            pltpu.VMEM((2, H, H), bf16),
            pltpu.VMEM((2, H, H), bf16),
            pltpu.VMEM((H, B), f32),
            pltpu.VMEM((2, H, H), f32),
            pltpu.VMEM((4, 4, H, B), bf16),
            pltpu.VMEM((4, 2, 4, H, B), bf16),
            pltpu.VMEM((4, 2, 4, H, B), bf16),
            pltpu.VMEM((B, W), f32),
            dma((4, 5)),
            dma((4, 5)),
            dma((3, 4, 2)),
            dma((4, 4, 2)),
            dma((5, 4)),
            dma((5, 4)),
            dma((3,)),
            dma((3,)),
            dma((15, 4)),
            dma((9, 4)),
            dma((8, 4)),
            dma((5, 4)),
        ],
        compiler_params=pltpu.CompilerParams(
            collective_id=0, has_side_effects=True, vmem_limit_bytes=48 * 2**20
        ),
        cost_estimate=pl.CostEstimate(flops=4 * 10**9, bytes_accessed=2 * 10**7, transcendentals=0),
    )(momentum)


def solution(mesh):
    return jax.shard_map(
        on_device, mesh=mesh, in_specs=(P("row", "col"),), out_specs=P("row", "col"), check_vma=False
    )
```

```python
import jax
import jax.numpy as jnp
from jax import lax
from jax.experimental import pallas as pl
from jax.experimental.pallas import tpu as pltpu
from jax.sharding import PartitionSpec as P

NR = 3584
NC = 18432

coef_a = 3.4445
coef_b = -4.775
coef_c = 2.0315
factor = 0.2 * max(NR, NC) ** 0.5

MESH = pl.DeviceIdType.MESH

B = 224
H = 112
W = 576
TILES = 4
PACK = TILES * B + H
LOW = (0, 2 * B)
HIGH = (2 * B, 2 * B + H)
FIRST = (0, 64)
SECOND = (64, 48)
REST = (TILES * B, H)


def nt_dot(a, b):
    return lax.dot_general(a, b, (((1,), (1,)), ((), ())), preferred_element_type=jnp.float32)


def nn_dot(a, b):
    return lax.dot_general(a, b, (((1,), (0,)), ((), ())), preferred_element_type=jnp.float32)


def kernel(
    x_hbm,
    o_ref,
    x_ref,
    xs,
    part,
    send1,
    recv1,
    send2,
    recv2,
    sum2,
    send3,
    recv3,
    swap_send,
    swap_recv,
    flip_send,
    flip_recv,
    swap_sum,
    flip_sum,
    gr,
    gc,
    pr,
    acc,
    load_sem,
    zsend,
    zrecv,
    xsend,
    xrecv,
    x2send,
    x2recv,
    rsend,
    rrecv,
    tsend,
    trecv,
    gsend,
    grecv,
    csend,
    crecv,
    psend,
    precv,
):
    row = lax.axis_index("row")
    col = lax.axis_index("col")
    x, zh = row // 4, row % 4
    y, zl, k = col // 8, (col // 2) % 4, col % 2
    sign = 1 + 2 * (zl % 2)

    def place(x_, zh_, y_, zl_, k_):
        return (x_ * 4 + zh_, y_ * 8 + zl_ * 2 + k_)

    def at(dx=0, dzh=0, dy=0, dzl=0, dk=0):
        return place((x + dx) % 4, (zh + dzh) % 4, (y + dy) % 4, (zl + dzl) % 4, (k + dk) % 2)

    def station(dz):
        return (zh + sign * dz) % 4

    started = []

    def send(src, dst, ssem, rsem, device):
        copy = pltpu.make_async_remote_copy(
            src_ref=src, dst_ref=dst, send_sem=ssem, recv_sem=rsem, device_id=device, device_id_type=MESH
        )
        copy.start()
        started.append(copy)

    def arrived(dst, rsem):
        pltpu.make_async_copy(dst, dst, rsem).wait()

    def rest(zp, xp):
        last = xs[zp, xp, pl.ds(TILES * B, H), :]
        return jnp.concatenate([last[:, :64], last[:, 64:]], axis=0)

    def tile_of(zp, xp, t):
        return xs[zp, xp, pl.ds(pl.multiple_of(t * B, 16), B), :]

    def unpack(zp, xp):
        return jnp.concatenate([tile_of(zp, xp, t) for t in range(TILES)] + [rest(zp, xp)], axis=1)

    load = pltpu.make_async_copy(x_hbm, x_ref, load_sem)
    load.start()
    barrier = pltpu.get_barrier_semaphore()
    peers = [at(dx=d) for d in (1, 2, 3)] + [at(dzh=d) for d in (1, 2, 3)]
    peers += [at(dy=d) for d in (1, 2, 3)] + [at(dzl=d) for d in (1, 2, 3)] + [at(dk=1)]
    swap_peer = place(y, zh, x, zl, k)
    flip_peers = [place(x, zl, y, zh, n) for n in range(2)]
    for peer in peers:
        pl.semaphore_signal(barrier, 1, device_id=peer, device_id_type=MESH)

    @pl.when(x != y)
    def _():
        pl.semaphore_signal(barrier, 1, device_id=swap_peer, device_id_type=MESH)

    @pl.when(zh != zl)
    def _():
        for peer in flip_peers:
            pl.semaphore_signal(barrier, 1, device_id=peer, device_id_type=MESH)

    load.wait()
    for t in range(TILES):
        xs[zh, x, pl.ds(t * B, B), :] = x_ref[:, pl.ds(t * 128, 128)]
    xs[zh, x, pl.ds(TILES * B, H), :] = jnp.concatenate(
        [x_ref[pl.ds(0, H), pl.ds(TILES * 128, 64)], x_ref[pl.ds(H, H), pl.ds(TILES * 128, 64)]], axis=1
    )
    pl.semaphore_wait(barrier, len(peers) + jnp.where(x != y, 1, 0) + jnp.where(zh != zl, 2, 0))

    def rows(dz, dx, start, size):
        return xs.at[station(dz), (x + dx) % 4, pl.ds(start, size)]

    def zmove(sem, dz, start, size, hop, rsem):
        piece = rows(dz, 0, start, size)
        send(piece, piece, zsend.at[sem], rsem, at(dzh=sign * hop))

    def xmove(kind, dz, dx, part_, hop):
        piece = rows(dz, dx, *(LOW, HIGH)[part_])
        send(piece, piece, xsend.at[kind, dz, part_], xrecv.at[dz, (dx - hop) % 4, part_], at(dx=hop))

    def xwait(dz, dx, part_):
        arrived(rows(dz, dx, *(LOW, HIGH)[part_]), xrecv.at[dz, dx, part_])

    def x_spread(dz, part_):
        xmove(0, dz, 0, part_, 1)
        xmove(1, dz, 0, part_, 3)

    def x_forward(dz, part_):
        source, hop = ((3, 1), (1, 3))[part_]
        xwait(dz, source, part_)
        xmove(2, dz, source, part_, hop)

    def x_rest(dz):
        for part_, source in ((0, 1), (1, 3)):
            xwait(dz, source, part_)
            xwait(dz, 2, part_)

    def tile_rows(t):
        return pl.multiple_of(t * B, 16)

    def zwait(dz, t):
        arrived(rows(dz, 0, tile_rows(t), B), zrecv.at[dz, t])

    def zwait_rest(dz):
        arrived(rows(dz, 0, *REST), zrecv.at[dz, 4])

    def x2_rows(dx, t):
        return rows(2, dx, *(REST if t is None else (tile_rows(t), B)))

    def x2_move(kind, dx, t, hop):
        piece, sem = x2_rows(dx, t), 4 if t is None else t
        send(piece, piece, x2send.at[kind, sem], x2recv.at[(dx - hop) % 4, sem], at(dx=hop))

    def x2_wait(dx, t):
        arrived(x2_rows(dx, t), x2recv.at[dx, 4 if t is None else t])

    def x2_spread(t):
        x2_move(0, 0, t, 1)
        x2_move(1, 0, t, 3)

    def x2_forward(t, up):
        source, hop = (3, 1) if up else (1, 3)
        x2_wait(source, t)
        x2_move(2, source, t, hop)

    def x2_rest(t, up):
        x2_wait(1 if up else 3, t)
        x2_wait(2, t)

    half = zh // 2
    half_before = ((zh + 4 - sign) % 4) // 2
    half_after = ((zh + sign) % 4) // 2

    def gram(dz):
        zp = station(dz)

        def step(xp, carry):
            if dz == 0:
                left, right = unpack(zh, xp), unpack(zh, x)
                value = 0.5 * nt_dot(left, right)
            elif dz == 1:
                left, right = [jnp.concatenate([tile_of(*b, t) for t in (0, 1)], axis=1) for b in ((zh, xp), (zp, x))]
                value = nt_dot(left, right)
            elif dz == 3:
                left, right = [
                    jnp.concatenate([tile_of(*b, t) for t in (2, 3)] + [rest(*b)], axis=1) for b in ((zh, xp), (zp, x))
                ]
                value = nt_dot(left, right)
            else:
                left, right = [
                    jnp.concatenate([tile_of(*b, half), tile_of(*b, 2 + half)], axis=1) for b in ((zh, xp), (zp, x))
                ]
                value = nt_dot(left, right) + 0.5 * nt_dot(rest(zh, xp), rest(zp, x))
            part[dz, xp] = value
            send1[dz, xp] = part[dz, xp, pl.ds(pl.multiple_of((1 - k) * H, 16), H), :].astype(jnp.bfloat16)
            return carry

        lax.fori_loop(0, 4, step, 0)
        send(send1.at[dz], recv1.at[dz], rsend.at[0, dz], rrecv.at[0, dz], at(dk=1))

    def reduce_core(dz):
        arrived(recv1.at[dz], rrecv.at[0, dz])

        def both(xp):
            return part[dz, xp, pl.ds(pl.multiple_of(k * H, 16), H), :] + recv1[dz, xp].astype(jnp.float32)

        for dy in (2, 1, 3):
            send2[dz, dy - 1] = both((y + dy) % 4).astype(jnp.bfloat16)
            send(send2.at[dz, dy - 1], recv2.at[dz, dy - 1], rsend.at[dy, dz], rrecv.at[dy, dz], at(dy=dy))
        sum2[dz] = both(y)

    def sum3(dz):
        owner = station(dz)
        d = (owner + 4 - zl) % 4
        copy = pltpu.make_async_remote_copy(
            src_ref=send3.at[dz],
            dst_ref=recv3.at[d],
            send_sem=rsend.at[4, dz],
            recv_sem=rrecv.at[4, d],
            device_id=place(x, zh, y, owner, k),
            device_id_type=MESH,
        )
        return d, copy

    def reduce_y(dz):
        for dy in (1, 3, 2):
            arrived(recv2.at[dz, dy - 1], rrecv.at[dy, dz])
        total = sum2[dz]
        for dy in (1, 2, 3):
            total = total + recv2[dz, dy - 1].astype(jnp.float32)
        sum2[dz] = total
        send3[dz] = total.astype(jnp.bfloat16)
        d, copy = sum3(dz)

        @pl.when(d != 0)
        def _():
            copy.start()

    for t in (0, 1):
        zmove((0, t), 0, t * B, B, 3, zrecv.at[1, t])
        zmove((0, 2 + t), 0, (2 + t) * B, B, 1, zrecv.at[3, 2 + t])
        xmove(t, 0, 0, t, 1 + 2 * t)
    zmove((0, 4), 0, *REST, 1, zrecv.at[3, 4])
    for t in (0, 1):
        xmove(1 - t, 0, 0, t, 3 - 2 * t)
    x_forward(0, 0)
    x_forward(0, 1)
    zwait(1, half_before)
    zmove((2, 0), 1, tile_rows(half_before), B, 3, zrecv.at[2, half_before])
    zwait(3, 2 + half_after)
    zmove((2, 1), 3, tile_rows(2 + half_after), B, 1, zrecv.at[2, 2 + half_after])
    zwait_rest(3)
    zmove((2, 2), 3, *REST, 1, zrecv.at[2, 4])
    x_rest(0)
    gram(0)
    zwait(1, 1 - half_before)
    gram(1)
    x_spread(1, 0)
    reduce_core(0)
    zwait(3, 3 - half_after)
    gram(3)
    x_spread(3, 1)
    reduce_core(1)
    reduce_core(3)
    reduce_y(0)
    zwait(2, half)
    zwait(2, 2 + half)
    zwait_rest(2)
    gram(2)
    zmove((1, 0), 0, *HIGH, 3, zrecv.at[1, 2])
    zmove((1, 1), 0, *LOW, 1, zrecv.at[3, 0])
    early = ((half, True), (2 + half, False), (None, True))
    late = ((1 - half, True), (3 - half, False))
    for t, up in early:
        x2_spread(t)
    reduce_y(1)
    reduce_core(2)
    reduce_y(3)
    x_forward(1, 0)
    x_forward(3, 1)
    reduce_y(2)

    total = sum2[(sign * (zl + 4 - zh)) % 4]
    for d in (1, 2, 3):
        arrived(recv3.at[d], rrecv.at[4, d])
        total = total + recv3[d].astype(jnp.float32)

    swap_send[...] = total.astype(jnp.bfloat16)
    flipped = total.T
    for n in range(2):
        flip_send[n] = flipped[n * H : (n + 1) * H, :].astype(jnp.bfloat16)
    swap_copy = pltpu.make_async_remote_copy(
        src_ref=swap_send,
        dst_ref=swap_recv,
        send_sem=tsend.at[0],
        recv_sem=trecv.at[0],
        device_id=swap_peer,
        device_id_type=MESH,
    )

    def flip_copy(n):
        return pltpu.make_async_remote_copy(
            src_ref=flip_send.at[n],
            dst_ref=flip_recv.at[k],
            send_sem=tsend.at[1 + n],
            recv_sem=trecv.at[1 + k],
            device_id=place(x, zl, y, zh, n),
            device_id_type=MESH,
        )

    @pl.when(x != y)
    def _():
        swap_copy.start()

    @pl.when(x == y)
    def _():
        swap_sum[...] = total

    flip_copy(1 - k).start()

    @pl.when(zh != zl)
    def _():
        flip_copy(k).start()

    @pl.when(zh == zl)
    def _():
        swap_send2 = jnp.where(k == 0, flipped[:H, :], flipped[H:, :])
        flip_sum[k] = swap_send2

    for t, up in early:
        x2_forward(t, up)
    arrived(rows(1, 0, *HIGH), zrecv.at[1, 2])
    x_spread(1, 1)
    arrived(rows(3, 0, *LOW), zrecv.at[3, 0])
    x_spread(3, 0)

    @pl.when(x != y)
    def _():
        arrived(swap_recv, trecv.at[0])
        swap_sum[...] = swap_recv[...].astype(jnp.float32)

    @pl.when(zh != zl)
    def _():
        arrived(flip_recv.at[k], trecv.at[1 + k])
        flip_sum[k] = flip_recv[k].astype(jnp.float32)

    arrived(flip_recv.at[1 - k], trecv.at[2 - k])
    flip_sum[1 - k] = flip_recv[1 - k].astype(jnp.float32)
    tile = (swap_sum[...] + jnp.concatenate([flip_sum[0], flip_sum[1]], axis=1)).astype(jnp.bfloat16)

    gr[zl, y] = tile
    gc[zh, k, x] = tile

    def cut(ref, piece):
        return ref.at[pl.ds(*piece)]

    def y_spread(buf, ssem, rsem, n):
        piece = buf((zl + n) % 4, y)
        for i, hop in enumerate((1, 3)):
            send(piece, piece, ssem.at[n, i], rsem.at[n, 4 - hop], at(dy=hop))

    def y_forward(buf, ssem, rsem, n):
        for i, (source, hop, rows_) in enumerate(((3, 1, FIRST), (1, 3, SECOND))):
            whole = buf((zl + n) % 4, (y + source) % 4)
            arrived(whole, rsem.at[n, source])
            send(cut(whole, rows_), cut(whole, rows_), ssem.at[n, 2 + i], rsem.at[n, 2 + 2 * i], at(dy=hop))

    def y_rest(buf, rsem, n):
        for i, rows_ in enumerate((FIRST, SECOND)):
            arrived(cut(buf((zl + n) % 4, (y + 2) % 4), rows_), rsem.at[n, 2 + 2 * i])

    def zl_spread(buf, ssem, rsem):
        piece = buf(zl, y)
        for d in (1, 3, 2):
            send(piece, piece, ssem.at[d, 4], rsem.at[4 - d, 0], at(dzl=d))

    def zl_wait(buf, rsem, n):
        arrived(buf((zl + n) % 4, y), rsem.at[n, 0])

    def x_gc_spread(n):
        piece = gc.at[(zh + n) % 4, k, x]
        for i, hop in enumerate((1, 3)):
            send(piece, piece, csend.at[n, i], crecv.at[n, 4 - hop], at(dx=hop))

    def x_gc_forward(n):
        for i, (source, hop, rows_) in enumerate(((3, 1, FIRST), (1, 3, SECOND))):
            whole = gc.at[(zh + n) % 4, k, (x + source) % 4]
            arrived(whole, crecv.at[n, source])
            send(cut(whole, rows_), cut(whole, rows_), csend.at[n, 2 + i], crecv.at[n, 2 + 2 * i], at(dx=hop))

    def x_gc_core(n):
        zp = (zh + n) % 4
        for i, rows_ in enumerate((FIRST, SECOND)):
            arrived(cut(gc.at[zp, k, (x + 2) % 4], rows_), crecv.at[n, 2 + 2 * i])
        send(gc.at[zp, k], gc.at[zp, k], csend.at[n, 4], crecv.at[n, 6], at(dk=1))

    def z_gc_spread():
        piece = gc.at[zh, k, x]
        for i, hop in enumerate((1, 3)):
            send(piece, piece, csend.at[2 * i, 5], crecv.at[4 - hop, 0], at(dzh=hop))

    def z_gc_forward():
        for i, (source, hop, rows_) in enumerate(((3, 1, FIRST), (1, 3, SECOND))):
            whole = gc.at[(zh + source) % 4, k, x]
            arrived(whole, crecv.at[source, 0])
            send(cut(whole, rows_), cut(whole, rows_), csend.at[1 + 2 * i, 5], crecv.at[2, 5 * i], at(dzh=hop))
            x_gc_spread(source)

    def gr_at(zp, yp):
        return gr.at[zp, yp]

    gsems = (gr_at, gsend, grecv)
    z_gc_spread()
    zl_spread(*gsems)
    x_gc_spread(0)
    y_spread(*gsems, 0)
    y_forward(*gsems, 0)
    x_gc_forward(0)
    for n in (3, 1, 2):
        zl_wait(gr_at, grecv, n)
        y_spread(*gsems, n)
    z_gc_forward()
    x_gc_core(0)
    x_forward(1, 1)
    x_forward(3, 0)
    for n in (3, 1, 2):
        y_forward(*gsems, n)
    for i, rows_ in enumerate((FIRST, SECOND)):
        arrived(cut(gc.at[(zh + 2) % 4, k, x], rows_), crecv.at[2, 5 * i])
    x_gc_spread(2)
    zmove((3, 0), 1, tile_rows(1 - half_before), B, 3, zrecv.at[2, 1 - half_before])
    zmove((3, 1), 3, tile_rows(3 - half_after), B, 1, zrecv.at[2, 3 - half_after])
    x_gc_forward(3)
    x_gc_forward(1)
    x_gc_core(3)
    x_gc_core(1)
    x_gc_forward(2)
    for n in range(4):
        y_rest(gr_at, grecv, n)
    x_gc_core(2)
    for n in (0, 3, 1, 2):
        zp = (zh + n) % 4
        arrived(gc.at[zp, 1 - k], crecv.at[n, 6])

    square = jnp.zeros((H, B), jnp.float32)
    for zp in range(4):
        for xp in range(4):
            right = jnp.concatenate([gc[zp, 0, xp], gc[zp, 1, xp]], axis=0)
            square = square + nn_dot(gr[zp, xp], right)
    pr[zl, k, y] = (coef_b * gr[zl, y].astype(jnp.float32) + coef_c * square).astype(jnp.bfloat16)

    def pr_at(zp, yp):
        return pr.at[zp, k, yp]

    def p_core(n):
        y_rest(pr_at, precv, n)
        zp = (zl + n) % 4
        send(pr.at[zp, k], pr.at[zp, k], psend.at[n, 5], precv.at[n, 5], at(dk=1))

    def product(n):
        zp = (zl + n) % 4
        arrived(pr.at[zp, 1 - k], precv.at[n, 5])

        def one(xp):
            return nn_dot(jnp.concatenate([pr[zp, 0, xp], pr[zp, 1, xp]], axis=0), unpack(zp, xp))

        acc[...] += (one(0) + one(1)) + (one(2) + one(3))

    psems = (pr_at, psend, precv)
    zl_spread(*psems)
    y_spread(*psems, 0)
    acc[...] = coef_a * x_ref[...].astype(jnp.float32)
    y_forward(*psems, 0)
    for n in (3, 1, 2):
        zl_wait(pr_at, precv, n)
        y_spread(*psems, n)
    for t, up in late:
        zwait(2, t)
        x2_spread(t)
    p_core(0)
    for n in (3, 1, 2):
        y_forward(*psems, n)
    for t, up in late:
        x2_forward(t, up)
    x_rest(1)
    x_rest(3)
    p_core(3)
    for t, up in early + late:
        x2_rest(t, up)
    product(0)
    p_core(1)
    product(3)
    p_core(2)
    product(1)
    product(2)
    o_ref[...] = (factor * acc[...]).astype(jnp.bfloat16)

    for copy in started:
        copy.wait_send()
    for dz in range(4):
        d, copy = sum3(dz)

        @pl.when(d != 0)
        def _(copy=copy):
            copy.wait_send()

    flip_copy(1 - k).wait_send()

    @pl.when(zh != zl)
    def _():
        flip_copy(k).wait_send()

    @pl.when(x != y)
    def _():
        swap_copy.wait_send()


def on_device(momentum):
    bf16, f32 = jnp.bfloat16, jnp.float32
    dma = pltpu.SemaphoreType.DMA
    return pl.pallas_call(
        kernel,
        out_shape=jax.ShapeDtypeStruct((B, W), bf16),
        in_specs=[pl.BlockSpec(memory_space=pl.ANY)],
        out_specs=pl.BlockSpec(memory_space=pltpu.VMEM),
        scratch_shapes=[
            pltpu.VMEM((B, W), bf16),
            pltpu.VMEM((4, 4, PACK, 128), bf16),
            pltpu.VMEM((4, 4, B, B), f32),
            pltpu.VMEM((4, 4, H, B), bf16),
            pltpu.VMEM((4, 4, H, B), bf16),
            pltpu.VMEM((4, 3, H, B), bf16),
            pltpu.VMEM((4, 3, H, B), bf16),
            pltpu.VMEM((4, H, B), f32),
            pltpu.VMEM((4, H, B), bf16),
            pltpu.VMEM((4, H, B), bf16),
            pltpu.VMEM((H, B), bf16),
            pltpu.VMEM((H, B), bf16),
            pltpu.VMEM((2, H, H), bf16),
            pltpu.VMEM((2, H, H), bf16),
            pltpu.VMEM((H, B), f32),
            pltpu.VMEM((2, H, H), f32),
            pltpu.VMEM((4, 4, H, B), bf16),
            pltpu.VMEM((4, 2, 4, H, B), bf16),
            pltpu.VMEM((4, 2, 4, H, B), bf16),
            pltpu.VMEM((B, W), f32),
            dma,
            dma((4, 5)),
            dma((4, 5)),
            dma((3, 4, 2)),
            dma((4, 4, 2)),
            dma((3, 5)),
            dma((4, 5)),
            dma((5, 4)),
            dma((5, 4)),
            dma((3,)),
            dma((3,)),
            dma((4, 5)),
            dma((4, 5)),
            dma((4, 6)),
            dma((4, 7)),
            dma((4, 6)),
            dma((4, 6)),
        ],
        compiler_params=pltpu.CompilerParams(
            collective_id=0, has_side_effects=True, vmem_limit_bytes=48 * 2**20
        ),
        cost_estimate=pl.CostEstimate(flops=4 * 10**9, bytes_accessed=2 * 10**7, transcendentals=0),
    )(momentum)


def solution(mesh):
    return jax.shard_map(
        on_device, mesh=mesh, in_specs=(P("row", "col"),), out_specs=P("row", "col"), check_vma=False
    )
```

```python
import jax
import jax.numpy as jnp
from jax import lax
from jax.experimental import pallas as pl
from jax.experimental.pallas import tpu as pltpu
from jax.sharding import PartitionSpec as P

NR = 3584
NC = 18432

coef_a = 3.4445
coef_b = -4.775
coef_c = 2.0315
factor = 0.2 * max(NR, NC) ** 0.5

MESH = pl.DeviceIdType.MESH

B = 224
H = 112
W = 576
TILES = 4
PACK = TILES * B + H
LOW = (0, 2 * B)
HIGH = (2 * B, 2 * B + H)
FIRST = (0, 64)
SECOND = (64, 48)
REST = (TILES * B, H)


def nt_dot(a, b):
    return lax.dot_general(a, b, (((1,), (1,)), ((), ())), preferred_element_type=jnp.float32)


def nn_dot(a, b):
    return lax.dot_general(a, b, (((1,), (0,)), ((), ())), preferred_element_type=jnp.float32)


def kernel(
    x_hbm,
    o_ref,
    x_ref,
    xs,
    part,
    send1,
    recv1,
    send2,
    recv2,
    sum2,
    send3,
    recv3,
    swap_send,
    swap_recv,
    flip_send,
    flip_recv,
    swap_sum,
    flip_sum,
    gr,
    gc,
    pr,
    acc,
    load_sem,
    zsend,
    zrecv,
    xsend,
    xrecv,
    x2send,
    x2recv,
    rsend,
    rrecv,
    tsend,
    trecv,
    gsend,
    grecv,
    csend,
    crecv,
    psend,
    precv,
):
    row = lax.axis_index("row")
    col = lax.axis_index("col")
    x, zh = row // 4, row % 4
    y, zl, k = col // 8, (col // 2) % 4, col % 2
    sign = 1 + 2 * (zl % 2)

    def place(x_, zh_, y_, zl_, k_):
        return (x_ * 4 + zh_, y_ * 8 + zl_ * 2 + k_)

    def at(dx=0, dzh=0, dy=0, dzl=0, dk=0):
        return place((x + dx) % 4, (zh + dzh) % 4, (y + dy) % 4, (zl + dzl) % 4, (k + dk) % 2)

    def station(dz):
        return (zh + sign * dz) % 4

    started = []

    def send(src, dst, ssem, rsem, device):
        copy = pltpu.make_async_remote_copy(
            src_ref=src, dst_ref=dst, send_sem=ssem, recv_sem=rsem, device_id=device, device_id_type=MESH
        )
        copy.start()
        started.append(copy)

    def arrived(dst, rsem):
        pltpu.make_async_copy(dst, dst, rsem).wait()

    def rest(zp, xp):
        last = xs[zp, xp, pl.ds(TILES * B, H), :]
        return jnp.concatenate([last[:, :64], last[:, 64:]], axis=0)

    def tile_of(zp, xp, t):
        return xs[zp, xp, pl.ds(pl.multiple_of(t * B, 16), B), :]

    def unpack(zp, xp):
        return jnp.concatenate([tile_of(zp, xp, t) for t in range(TILES)] + [rest(zp, xp)], axis=1)

    load = pltpu.make_async_copy(x_hbm, x_ref, load_sem)
    load.start()
    barrier = pltpu.get_barrier_semaphore()
    peers = [at(dx=d) for d in (1, 2, 3)] + [at(dzh=d) for d in (1, 3)]
    peers += [at(dy=d) for d in (1, 2, 3)] + [at(dzl=d) for d in (1, 2, 3)] + [at(dk=1)]
    swap_peer = place(y, zh, x, zl, k)
    flip_peers = [place(x, zl, y, zh, n) for n in range(2)]
    for peer in peers:
        pl.semaphore_signal(barrier, 1, device_id=peer, device_id_type=MESH)

    load.wait()
    for t in range(TILES):
        xs[zh, x, pl.ds(t * B, B), :] = x_ref[:, pl.ds(t * 128, 128)]
    xs[zh, x, pl.ds(TILES * B, H), :] = jnp.concatenate(
        [x_ref[pl.ds(0, H), pl.ds(TILES * 128, 64)], x_ref[pl.ds(H, H), pl.ds(TILES * 128, 64)]], axis=1
    )
    pl.semaphore_wait(barrier, len(peers))

    def rows(dz, dx, start, size):
        return xs.at[station(dz), (x + dx) % 4, pl.ds(start, size)]

    def zmove(sem, dz, start, size, hop, rsem):
        piece = rows(dz, 0, start, size)
        send(piece, piece, zsend.at[sem], rsem, at(dzh=sign * hop))

    def xmove(kind, dz, dx, part_, hop):
        piece = rows(dz, dx, *(LOW, HIGH)[part_])
        send(piece, piece, xsend.at[kind, dz, part_], xrecv.at[dz, (dx - hop) % 4, part_], at(dx=hop))

    def xwait(dz, dx, part_):
        arrived(rows(dz, dx, *(LOW, HIGH)[part_]), xrecv.at[dz, dx, part_])

    def x_spread(dz, part_):
        xmove(0, dz, 0, part_, 1)
        xmove(1, dz, 0, part_, 3)

    def x_forward(dz, part_):
        source, hop = ((3, 1), (1, 3))[part_]
        xwait(dz, source, part_)
        xmove(2, dz, source, part_, hop)

    def x_rest(dz):
        for part_, source in ((0, 1), (1, 3)):
            xwait(dz, source, part_)
            xwait(dz, 2, part_)

    def tile_rows(t):
        return pl.multiple_of(t * B, 16)

    def zwait(dz, t):
        arrived(rows(dz, 0, tile_rows(t), B), zrecv.at[dz, t])

    def zwait_rest(dz):
        arrived(rows(dz, 0, *REST), zrecv.at[dz, 4])

    def x2_rows(dx, t):
        return rows(2, dx, *(REST if t is None else (tile_rows(t), B)))

    def x2_move(kind, dx, t, hop):
        piece, sem = x2_rows(dx, t), 4 if t is None else t
        send(piece, piece, x2send.at[kind, sem], x2recv.at[(dx - hop) % 4, sem], at(dx=hop))

    def x2_wait(dx, t):
        arrived(x2_rows(dx, t), x2recv.at[dx, 4 if t is None else t])

    def x2_spread(t):
        x2_move(0, 0, t, 1)
        x2_move(1, 0, t, 3)

    def x2_forward(t, up):
        source, hop = (3, 1) if up else (1, 3)
        x2_wait(source, t)
        x2_move(2, source, t, hop)

    def x2_rest(t, up):
        x2_wait(1 if up else 3, t)
        x2_wait(2, t)

    half = zh // 2
    half_before = ((zh + 4 - sign) % 4) // 2
    half_after = ((zh + sign) % 4) // 2

    def gram(dz):
        zp = station(dz)

        def step(xp, carry):
            if dz == 0:
                left, right = unpack(zh, xp), unpack(zh, x)
                value = 0.5 * nt_dot(left, right)
            elif dz == 1:
                left, right = [jnp.concatenate([tile_of(*b, t) for t in (0, 1)], axis=1) for b in ((zh, xp), (zp, x))]
                value = nt_dot(left, right)
            elif dz == 3:
                left, right = [
                    jnp.concatenate([tile_of(*b, t) for t in (2, 3)] + [rest(*b)], axis=1) for b in ((zh, xp), (zp, x))
                ]
                value = nt_dot(left, right)
            else:
                left, right = [
                    jnp.concatenate([tile_of(*b, half), tile_of(*b, 2 + half)], axis=1) for b in ((zh, xp), (zp, x))
                ]
                value = nt_dot(left, right) + 0.5 * nt_dot(rest(zh, xp), rest(zp, x))
            part[dz, xp] = value
            send1[dz, xp] = part[dz, xp, pl.ds(pl.multiple_of((1 - k) * H, 16), H), :].astype(jnp.bfloat16)
            return carry

        lax.fori_loop(0, 4, step, 0)
        send(send1.at[dz], recv1.at[dz], rsend.at[0, dz], rrecv.at[0, dz], at(dk=1))

    def reduce_core(dz):
        arrived(recv1.at[dz], rrecv.at[0, dz])

        def both(xp):
            return part[dz, xp, pl.ds(pl.multiple_of(k * H, 16), H), :] + recv1[dz, xp].astype(jnp.float32)

        for dy in (2, 1, 3):
            send2[dz, dy - 1] = both((y + dy) % 4).astype(jnp.bfloat16)
            send(send2.at[dz, dy - 1], recv2.at[dz, dy - 1], rsend.at[dy, dz], rrecv.at[dy, dz], at(dy=dy))
        sum2[dz] = both(y)

    def sum3(dz):
        owner = station(dz)
        d = (owner + 4 - zl) % 4
        copy = pltpu.make_async_remote_copy(
            src_ref=send3.at[dz],
            dst_ref=recv3.at[d],
            send_sem=rsend.at[4, dz],
            recv_sem=rrecv.at[4, d],
            device_id=place(x, zh, y, owner, k),
            device_id_type=MESH,
        )
        return d, copy

    def reduce_y(dz):
        for dy in (1, 3, 2):
            arrived(recv2.at[dz, dy - 1], rrecv.at[dy, dz])
        total = sum2[dz]
        for dy in (1, 2, 3):
            total = total + recv2[dz, dy - 1].astype(jnp.float32)
        sum2[dz] = total
        send3[dz] = total.astype(jnp.bfloat16)
        d, copy = sum3(dz)

        @pl.when(d != 0)
        def _():
            copy.start()

    for t in (0, 1):
        zmove((0, t), 0, t * B, B, 3, zrecv.at[1, t])
        zmove((0, 2 + t), 0, (2 + t) * B, B, 1, zrecv.at[3, 2 + t])
        xmove(t, 0, 0, t, 1 + 2 * t)
    zmove((0, 4), 0, *REST, 1, zrecv.at[3, 4])
    for t in (0, 1):
        xmove(1 - t, 0, 0, t, 3 - 2 * t)
    x_forward(0, 0)
    x_forward(0, 1)
    zwait(1, half_before)
    zmove((2, 0), 1, tile_rows(half_before), B, 3, zrecv.at[2, half_before])
    zwait(3, 2 + half_after)
    zmove((2, 1), 3, tile_rows(2 + half_after), B, 1, zrecv.at[2, 2 + half_after])
    zwait_rest(3)
    zmove((2, 2), 3, *REST, 1, zrecv.at[2, 4])
    x_rest(0)
    gram(0)
    zwait(1, 1 - half_before)
    gram(1)
    x_spread(1, 0)
    reduce_core(0)
    zwait(3, 3 - half_after)
    gram(3)
    x_spread(3, 1)
    reduce_core(1)
    reduce_core(3)
    reduce_y(0)
    zwait(2, half)
    zwait(2, 2 + half)
    zwait_rest(2)
    gram(2)
    zmove((1, 0), 0, *HIGH, 3, zrecv.at[1, 2])
    zmove((1, 1), 0, *LOW, 1, zrecv.at[3, 0])
    early = ((half, True), (2 + half, False), (None, True))
    late = ((1 - half, True), (3 - half, False))
    for t, up in early:
        x2_spread(t)
    reduce_y(1)
    reduce_core(2)
    reduce_y(3)
    x_forward(1, 0)
    x_forward(3, 1)
    reduce_y(2)

    total = sum2[(sign * (zl + 4 - zh)) % 4]
    for d in (1, 2, 3):
        arrived(recv3.at[d], rrecv.at[4, d])
        total = total + recv3[d].astype(jnp.float32)

    swap_send[...] = total.astype(jnp.bfloat16)
    flipped = total.T
    for n in range(2):
        flip_send[n] = flipped[n * H : (n + 1) * H, :].astype(jnp.bfloat16)
    swap_copy = pltpu.make_async_remote_copy(
        src_ref=swap_send,
        dst_ref=swap_recv,
        send_sem=tsend.at[0],
        recv_sem=trecv.at[0],
        device_id=swap_peer,
        device_id_type=MESH,
    )

    def flip_copy(n):
        return pltpu.make_async_remote_copy(
            src_ref=flip_send.at[n],
            dst_ref=flip_recv.at[k],
            send_sem=tsend.at[1 + n],
            recv_sem=trecv.at[1 + k],
            device_id=(flip_peers[0][0], y * 8 + zh * 2 + n),
            device_id_type=MESH,
        )

    @pl.when(x != y)
    def _():
        swap_copy.start()

    @pl.when(x == y)
    def _():
        swap_sum[...] = total

    flip_copy(1 - k).start()

    @pl.when(zh != zl)
    def _():
        flip_copy(k).start()

    @pl.when(zh == zl)
    def _():
        swap_send2 = jnp.where(k == 0, flipped[:H, :], flipped[H:, :])
        flip_sum[k] = swap_send2

    for t, up in early:
        x2_forward(t, up)
    arrived(rows(1, 0, *HIGH), zrecv.at[1, 2])
    x_spread(1, 1)
    arrived(rows(3, 0, *LOW), zrecv.at[3, 0])
    x_spread(3, 0)

    @pl.when(x != y)
    def _():
        arrived(swap_recv, trecv.at[0])
        swap_sum[...] = swap_recv[...].astype(jnp.float32)

    @pl.when(zh != zl)
    def _():
        arrived(flip_recv.at[k], trecv.at[1 + k])
        flip_sum[k] = flip_recv[k].astype(jnp.float32)

    arrived(flip_recv.at[1 - k], trecv.at[2 - k])
    flip_sum[1 - k] = flip_recv[1 - k].astype(jnp.float32)
    tile = (swap_sum[...] + jnp.concatenate([flip_sum[0], flip_sum[1]], axis=1)).astype(jnp.bfloat16)

    gr[zl, y] = tile
    gc[zh, k, x] = tile

    def cut(ref, piece):
        return ref.at[pl.ds(*piece)]

    def y_spread(buf, ssem, rsem, n):
        piece = buf((zl + n) % 4, y)
        for i, hop in enumerate((1, 3)):
            send(piece, piece, ssem.at[n, i], rsem.at[n, 4 - hop], at(dy=hop))

    def y_forward(buf, ssem, rsem, n):
        for i, (source, hop, rows_) in enumerate(((3, 1, FIRST), (1, 3, SECOND))):
            whole = buf((zl + n) % 4, (y + source) % 4)
            arrived(whole, rsem.at[n, source])
            send(cut(whole, rows_), cut(whole, rows_), ssem.at[n, 2 + i], rsem.at[n, 2 + 2 * i], at(dy=hop))

    def y_rest(buf, rsem, n):
        for i, rows_ in enumerate((FIRST, SECOND)):
            arrived(cut(buf((zl + n) % 4, (y + 2) % 4), rows_), rsem.at[n, 2 + 2 * i])

    def zl_spread(buf, ssem, rsem):
        piece = buf(zl, y)
        for d in (1, 3, 2):
            send(piece, piece, ssem.at[d, 4], rsem.at[4 - d, 0], at(dzl=d))

    def zl_wait(buf, rsem, n):
        arrived(buf((zl + n) % 4, y), rsem.at[n, 0])

    def y_all(n):
        piece = gr.at[(zl + n) % 4, y]
        for d in (2, 1, 3):
            send(piece, piece, gsend.at[n, d], grecv.at[n, 4 - d], at(dy=d))

    def x_all(n):
        piece = gc.at[(zh + n) % 4, k, x]
        for d in (2, 1, 3):
            send(piece, piece, csend.at[n, d], crecv.at[n, 4 - d], at(dx=d))

    def x_gc_core(n):
        zp = (zh + n) % 4
        for d in (1, 3, 2):
            arrived(gc.at[zp, k, (x + d) % 4], crecv.at[n, d])
        send(gc.at[zp, k], gc.at[zp, k], csend.at[n, 4], crecv.at[n, 6], at(dk=1))

    def gr_at(zp, yp):
        return gr.at[zp, yp]

    for i, hop in enumerate((1, 3)):
        send(gc.at[zh, k, x], gc.at[zh, k, x], csend.at[2 * i, 5], crecv.at[4 - hop, 0], at(dzh=hop))
    x_all(0)
    y_all(0)
    x_gc_core(0)
    zl_spread(gr_at, gsend, grecv)
    x_forward(1, 1)
    x_forward(3, 0)
    for i, (source, hop, rows_) in enumerate(((3, 1, FIRST), (1, 3, SECOND))):
        whole = gc.at[(zh + source) % 4, k, x]
        arrived(whole, crecv.at[source, 0])
        send(cut(whole, rows_), cut(whole, rows_), csend.at[1 + 2 * i, 5], crecv.at[2, 5 * i], at(dzh=hop))
        x_all(source)
    for n in (3, 1, 2):
        zl_wait(gr_at, grecv, n)
        y_all(n)
    x_gc_core(3)
    x_gc_core(1)
    for i, rows_ in enumerate((FIRST, SECOND)):
        arrived(cut(gc.at[(zh + 2) % 4, k, x], rows_), crecv.at[2, 5 * i])
    x_all(2)
    zmove((3, 0), 1, tile_rows(1 - half_before), B, 3, zrecv.at[2, 1 - half_before])
    zmove((3, 1), 3, tile_rows(3 - half_after), B, 1, zrecv.at[2, 3 - half_after])
    for n in range(4):
        for d in (1, 3, 2):
            arrived(gr.at[(zl + n) % 4, (y + d) % 4], grecv.at[n, d])
    x_gc_core(2)
    for n in (0, 3, 1, 2):
        zp = (zh + n) % 4
        arrived(gc.at[zp, 1 - k], crecv.at[n, 6])

    square = jnp.zeros((H, B), jnp.float32)
    for zp in range(4):
        for xp in range(4):
            right = jnp.concatenate([gc[zp, 0, xp], gc[zp, 1, xp]], axis=0)
            square = square + nn_dot(gr[zp, xp], right)
    pr[zl, k, y] = (coef_b * gr[zl, y].astype(jnp.float32) + coef_c * square).astype(jnp.bfloat16)

    def pr_at(zp, yp):
        return pr.at[zp, k, yp]

    def p_core(n):
        y_rest(pr_at, precv, n)
        zp = (zl + n) % 4
        send(pr.at[zp, k], pr.at[zp, k], psend.at[n, 5], precv.at[n, 5], at(dk=1))

    def product(n):
        zp = (zl + n) % 4
        arrived(pr.at[zp, 1 - k], precv.at[n, 5])

        def one(xp):
            return nn_dot(jnp.concatenate([pr[zp, 0, xp], pr[zp, 1, xp]], axis=0), unpack(zp, xp))

        acc[...] += (one(0) + one(1)) + (one(2) + one(3))

    psems = (pr_at, psend, precv)
    zl_spread(*psems)
    y_spread(*psems, 0)
    acc[...] = coef_a * x_ref[...].astype(jnp.float32)
    y_forward(*psems, 0)
    for n in (3, 1, 2):
        zl_wait(pr_at, precv, n)
        y_spread(*psems, n)
    for t, up in late:
        zwait(2, t)
        x2_spread(t)
    p_core(0)
    for n in (3, 1, 2):
        y_forward(*psems, n)
    for t, up in late:
        x2_forward(t, up)
    x_rest(1)
    x_rest(3)
    p_core(3)
    for t, up in early + late:
        x2_rest(t, up)
    product(0)
    p_core(1)
    product(3)
    p_core(2)
    product(1)
    product(2)
    o_ref[...] = (factor * acc[...]).astype(jnp.bfloat16)

    for copy in started:
        copy.wait_send()
    for dz in range(4):
        d, copy = sum3(dz)

        @pl.when(d != 0)
        def _(copy=copy):
            copy.wait_send()

    flip_copy(1 - k).wait_send()

    @pl.when(zh != zl)
    def _():
        flip_copy(k).wait_send()

    @pl.when(x != y)
    def _():
        swap_copy.wait_send()


def on_device(momentum):
    bf16, f32 = jnp.bfloat16, jnp.float32
    dma = pltpu.SemaphoreType.DMA
    return pl.pallas_call(
        kernel,
        out_shape=jax.ShapeDtypeStruct((B, W), bf16),
        in_specs=[pl.BlockSpec(memory_space=pltpu.HBM)],
        out_specs=pl.BlockSpec(memory_space=pltpu.VMEM),
        scratch_shapes=[
            pltpu.VMEM((B, W), bf16),
            pltpu.VMEM((4, 4, PACK, 128), bf16),
            pltpu.VMEM((4, 4, B, B), f32),
            pltpu.VMEM((4, 4, H, B), bf16),
            pltpu.VMEM((4, 4, H, B), bf16),
            pltpu.VMEM((4, 3, H, B), bf16),
            pltpu.VMEM((4, 3, H, B), bf16),
            pltpu.VMEM((4, H, B), f32),
            pltpu.VMEM((4, H, B), bf16),
            pltpu.VMEM((4, H, B), bf16),
            pltpu.VMEM((H, B), bf16),
            pltpu.VMEM((H, B), bf16),
            pltpu.VMEM((2, H, H), bf16),
            pltpu.VMEM((2, H, H), bf16),
            pltpu.VMEM((H, B), f32),
            pltpu.VMEM((2, H, H), f32),
            pltpu.VMEM((4, 4, H, B), bf16),
            pltpu.VMEM((4, 2, 4, H, B), bf16),
            pltpu.VMEM((4, 2, 4, H, B), bf16),
            pltpu.VMEM((B, W), f32),
            dma,
            dma((4, 5)),
            dma((4, 5)),
            dma((3, 4, 2)),
            dma((4, 4, 2)),
            dma((3, 5)),
            dma((4, 5)),
            dma((5, 4)),
            dma((5, 4)),
            dma((3,)),
            dma((3,)),
            dma((4, 5)),
            dma((4, 5)),
            dma((4, 6)),
            dma((4, 7)),
            dma((4, 6)),
            dma((4, 6)),
        ],
        compiler_params=pltpu.CompilerParams(
            collective_id=0, has_side_effects=True, vmem_limit_bytes=60 * 2**20
        ),
        cost_estimate=pl.CostEstimate(flops=4 * 10**9, bytes_accessed=2 * 10**7, transcendentals=0),
    )(momentum)


def solution(mesh):
    return jax.shard_map(
        on_device, mesh=mesh, in_specs=(P("row", "col"),), out_specs=P("row", "col"), check_vma=False
    )
```

```python
import jax
import jax.numpy as jnp
from jax import lax
from jax.experimental import pallas as pl
from jax.experimental.pallas import tpu as pltpu
from jax.sharding import PartitionSpec as P

NR = 3584
NC = 18432

coef_a = 3.4445
coef_b = -4.775
coef_c = 2.0315
factor = 0.2 * max(NR, NC) ** 0.5

MESH = pl.DeviceIdType.MESH

B = 224
H = 112
W = 576
TILES = 4
PACK = TILES * B + H
LOW = (0, 2 * B)
HIGH = (2 * B, 2 * B + H)
FIRST = (0, 64)
SECOND = (64, 48)
REST = (TILES * B, H)


def nt_dot(a, b):
    return lax.dot_general(a, b, (((1,), (1,)), ((), ())), preferred_element_type=jnp.float32)


def nn_dot(a, b):
    return lax.dot_general(a, b, (((1,), (0,)), ((), ())), preferred_element_type=jnp.float32)


def kernel(
    x_hbm,
    o_ref,
    x_ref,
    xs,
    part,
    send1,
    recv1,
    send2,
    recv2,
    sum2,
    send3,
    recv3,
    swap_send,
    swap_recv,
    flip_send,
    flip_recv,
    swap_sum,
    flip_sum,
    gr,
    gc,
    pr,
    acc,
    load_sem,
    zsend,
    zrecv,
    xsend,
    xrecv,
    x2send,
    x2recv,
    rsend,
    rrecv,
    tsend,
    trecv,
    gsend,
    grecv,
    csend,
    crecv,
    psend,
    precv,
):
    row = lax.axis_index("row")
    col = lax.axis_index("col")
    x, zh = row // 4, row % 4
    y, zl, k = col // 8, (col // 2) % 4, col % 2
    sign = 1 + 2 * (zl % 2)

    def place(x_, zh_, y_, zl_, k_):
        return (x_ * 4 + zh_, y_ * 8 + zl_ * 2 + k_)

    def at(dx=0, dzh=0, dy=0, dzl=0, dk=0):
        return place((x + dx) % 4, (zh + dzh) % 4, (y + dy) % 4, (zl + dzl) % 4, (k + dk) % 2)

    def station(dz):
        return (zh + sign * dz) % 4

    started = []

    def send(src, dst, ssem, rsem, device):
        copy = pltpu.make_async_remote_copy(
            src_ref=src, dst_ref=dst, send_sem=ssem, recv_sem=rsem, device_id=device, device_id_type=MESH
        )
        copy.start()
        started.append(copy)

    def arrived(dst, rsem):
        pltpu.make_async_copy(dst, dst, rsem).wait()

    def rest(zp, xp):
        last = xs[zp, xp, pl.ds(TILES * B, H), :]
        return jnp.concatenate([last[:, :64], last[:, 64:]], axis=0)

    def tile_of(zp, xp, t):
        return xs[zp, xp, pl.ds(pl.multiple_of(t * B, 16), B), :]

    def unpack(zp, xp):
        return jnp.concatenate([tile_of(zp, xp, t) for t in range(TILES)] + [rest(zp, xp)], axis=1)

    load = pltpu.make_async_copy(x_hbm, x_ref, load_sem)
    load.start()
    barrier = pltpu.get_barrier_semaphore()
    peers = [at(dx=d) for d in (1, 2, 3)] + [at(dzh=d) for d in (1, 3)]
    peers += [at(dy=d) for d in (1, 2, 3)] + [at(dzl=d) for d in (1, 2, 3)] + [at(dk=1)]
    swap_peer = place(y, zh, x, zl, k)
    flip_peers = [place(x, zl, y, zh, n) for n in range(2)]
    for peer in peers:
        pl.semaphore_signal(barrier, 1, device_id=peer, device_id_type=MESH)

    load.wait()
    for t in range(TILES):
        xs[zh, x, pl.ds(t * B, B), :] = x_ref[:, pl.ds(t * 128, 128)]
    xs[zh, x, pl.ds(TILES * B, H), :] = jnp.concatenate(
        [x_ref[pl.ds(0, H), pl.ds(TILES * 128, 64)], x_ref[pl.ds(H, H), pl.ds(TILES * 128, 64)]], axis=1
    )
    pl.semaphore_wait(barrier, len(peers))

    def rows(dz, dx, start, size):
        return xs.at[station(dz), (x + dx) % 4, pl.ds(start, size)]

    def zmove(sem, dz, start, size, hop, rsem):
        piece = rows(dz, 0, start, size)
        send(piece, piece, zsend.at[sem], rsem, at(dzh=sign * hop))

    def xmove(kind, dz, dx, part_, hop):
        piece = rows(dz, dx, *(LOW, HIGH)[part_])
        send(piece, piece, xsend.at[kind, dz, part_], xrecv.at[dz, (dx - hop) % 4, part_], at(dx=hop))

    def xwait(dz, dx, part_):
        arrived(rows(dz, dx, *(LOW, HIGH)[part_]), xrecv.at[dz, dx, part_])

    def x_spread(dz, part_):
        xmove(0, dz, 0, part_, 1)
        xmove(1, dz, 0, part_, 3)

    def x_forward(dz, part_):
        source, hop = ((3, 1), (1, 3))[part_]
        xwait(dz, source, part_)
        xmove(2, dz, source, part_, hop)

    def x_rest(dz):
        for part_, source in ((0, 1), (1, 3)):
            xwait(dz, source, part_)
            xwait(dz, 2, part_)

    def tile_rows(t):
        return pl.multiple_of(t * B, 16)

    def zwait(dz, t):
        arrived(rows(dz, 0, tile_rows(t), B), zrecv.at[dz, t])

    def zwait_rest(dz):
        arrived(rows(dz, 0, *REST), zrecv.at[dz, 4])

    def x2_rows(dx, t):
        return rows(2, dx, *(REST if t is None else (tile_rows(t), B)))

    def x2_move(kind, dx, t, hop):
        piece, sem = x2_rows(dx, t), 4 if t is None else t
        send(piece, piece, x2send.at[kind, sem], x2recv.at[(dx - hop) % 4, sem], at(dx=hop))

    def x2_wait(dx, t):
        arrived(x2_rows(dx, t), x2recv.at[dx, 4 if t is None else t])

    def x2_spread(t):
        x2_move(0, 0, t, 1)
        x2_move(1, 0, t, 3)

    def x2_forward(t, up):
        source, hop = (3, 1) if up else (1, 3)
        x2_wait(source, t)
        x2_move(2, source, t, hop)

    def x2_rest(t, up):
        x2_wait(1 if up else 3, t)
        x2_wait(2, t)

    half = zh // 2
    half_before = ((zh + 4 - sign) % 4) // 2
    half_after = ((zh + sign) % 4) // 2

    def gram(dz):
        zp = station(dz)

        def stack(piece):
            return jnp.concatenate([piece(zh, xp) for xp in range(4)], axis=0)

        def dot(pieces):
            return nt_dot(
                jnp.concatenate([stack(piece) for piece in pieces], axis=1),
                jnp.concatenate([piece(zp, x) for piece in pieces], axis=1),
            )

        tiles = [lambda z_, x_, t=t: tile_of(z_, x_, t) for t in (0, 1, 2, 3, half, 2 + half)]
        if dz == 0:
            value = 0.5 * dot(tiles[:4] + [rest])
        elif dz == 1:
            value = dot(tiles[:2])
        elif dz == 3:
            value = dot(tiles[2:4] + [rest])
        else:
            value = dot(tiles[4:]) + 0.5 * dot([rest])
        part[dz] = value
        for xp in range(4):
            mine = pl.multiple_of(xp * B + (1 - k) * H, 16)
            send1[dz, xp] = part[dz, pl.ds(mine, H), :].astype(jnp.bfloat16)
        send(send1.at[dz], recv1.at[dz], rsend.at[0, dz], rrecv.at[0, dz], at(dk=1))

    def reduce_core(dz):
        arrived(recv1.at[dz], rrecv.at[0, dz])

        def both(xp):
            mine = pl.multiple_of(xp * B + k * H, 16)
            return part[dz, pl.ds(mine, H), :] + recv1[dz, xp].astype(jnp.float32)

        for dy in (2, 1, 3):
            send2[dz, dy - 1] = both((y + dy) % 4).astype(jnp.bfloat16)
            send(send2.at[dz, dy - 1], recv2.at[dz, dy - 1], rsend.at[dy, dz], rrecv.at[dy, dz], at(dy=dy))
        sum2[dz] = both(y)

    def sum3(dz):
        owner = station(dz)
        d = (owner + 4 - zl) % 4
        copy = pltpu.make_async_remote_copy(
            src_ref=send3.at[dz],
            dst_ref=recv3.at[d],
            send_sem=rsend.at[4, dz],
            recv_sem=rrecv.at[4, d],
            device_id=place(x, zh, y, owner, k),
            device_id_type=MESH,
        )
        return d, copy

    def reduce_y(dz):
        for dy in (1, 3, 2):
            arrived(recv2.at[dz, dy - 1], rrecv.at[dy, dz])
        total = sum2[dz]
        for dy in (1, 2, 3):
            total = total + recv2[dz, dy - 1].astype(jnp.float32)
        sum2[dz] = total
        send3[dz] = total.astype(jnp.bfloat16)
        d, copy = sum3(dz)

        @pl.when(d != 0)
        def _():
            copy.start()

    for t in (0, 1):
        zmove((0, t), 0, t * B, B, 3, zrecv.at[1, t])
        zmove((0, 2 + t), 0, (2 + t) * B, B, 1, zrecv.at[3, 2 + t])
        xmove(t, 0, 0, t, 1 + 2 * t)
    zmove((0, 4), 0, *REST, 1, zrecv.at[3, 4])
    for t in (0, 1):
        xmove(1 - t, 0, 0, t, 3 - 2 * t)
    x_forward(0, 0)
    x_forward(0, 1)
    zwait(1, half_before)
    zmove((2, 0), 1, tile_rows(half_before), B, 3, zrecv.at[2, half_before])
    zwait(3, 2 + half_after)
    zmove((2, 1), 3, tile_rows(2 + half_after), B, 1, zrecv.at[2, 2 + half_after])
    zwait_rest(3)
    zmove((2, 2), 3, *REST, 1, zrecv.at[2, 4])
    x_rest(0)
    gram(0)
    zwait(1, 1 - half_before)
    gram(1)
    x_spread(1, 0)
    reduce_core(0)
    zwait(3, 3 - half_after)
    gram(3)
    x_spread(3, 1)
    reduce_core(1)
    reduce_core(3)
    reduce_y(0)
    zwait(2, half)
    zwait(2, 2 + half)
    zwait_rest(2)
    gram(2)
    zmove((1, 0), 0, *HIGH, 3, zrecv.at[1, 2])
    zmove((1, 1), 0, *LOW, 1, zrecv.at[3, 0])
    early = ((half, True), (2 + half, False), (None, True))
    late = ((1 - half, True), (3 - half, False))
    for t, up in early:
        x2_spread(t)
    reduce_y(1)
    reduce_core(2)
    reduce_y(3)
    x_forward(1, 0)
    x_forward(3, 1)
    reduce_y(2)

    total = sum2[(sign * (zl + 4 - zh)) % 4]
    for d in (1, 2, 3):
        arrived(recv3.at[d], rrecv.at[4, d])
        total = total + recv3[d].astype(jnp.float32)

    swap_send[...] = total.astype(jnp.bfloat16)
    flipped = total.T
    for n in range(2):
        flip_send[n] = flipped[n * H : (n + 1) * H, :].astype(jnp.bfloat16)
    swap_copy = pltpu.make_async_remote_copy(
        src_ref=swap_send,
        dst_ref=swap_recv,
        send_sem=tsend.at[0],
        recv_sem=trecv.at[0],
        device_id=swap_peer,
        device_id_type=MESH,
    )

    def flip_copy(n):
        return pltpu.make_async_remote_copy(
            src_ref=flip_send.at[n],
            dst_ref=flip_recv.at[k],
            send_sem=tsend.at[1 + n],
            recv_sem=trecv.at[1 + k],
            device_id=(flip_peers[0][0], y * 8 + zh * 2 + n),
            device_id_type=MESH,
        )

    @pl.when(x != y)
    def _():
        swap_copy.start()

    @pl.when(x == y)
    def _():
        swap_sum[...] = total

    flip_copy(1 - k).start()

    @pl.when(zh != zl)
    def _():
        flip_copy(k).start()

    @pl.when(zh == zl)
    def _():
        swap_send2 = jnp.where(k == 0, flipped[:H, :], flipped[H:, :])
        flip_sum[k] = swap_send2

    for t, up in early:
        x2_forward(t, up)
    arrived(rows(1, 0, *HIGH), zrecv.at[1, 2])
    x_spread(1, 1)
    arrived(rows(3, 0, *LOW), zrecv.at[3, 0])
    x_spread(3, 0)

    @pl.when(x != y)
    def _():
        arrived(swap_recv, trecv.at[0])
        swap_sum[...] = swap_recv[...].astype(jnp.float32)

    @pl.when(zh != zl)
    def _():
        arrived(flip_recv.at[k], trecv.at[1 + k])
        flip_sum[k] = flip_recv[k].astype(jnp.float32)

    arrived(flip_recv.at[1 - k], trecv.at[2 - k])
    flip_sum[1 - k] = flip_recv[1 - k].astype(jnp.float32)
    tile = (swap_sum[...] + jnp.concatenate([flip_sum[0], flip_sum[1]], axis=1)).astype(jnp.bfloat16)

    gr[zl, y] = tile
    gc[zh, k, x] = tile

    def cut(ref, piece):
        return ref.at[pl.ds(*piece)]

    def y_spread(buf, ssem, rsem, n):
        piece = buf((zl + n) % 4, y)
        for i, hop in enumerate((1, 3)):
            send(piece, piece, ssem.at[n, i], rsem.at[n, 4 - hop], at(dy=hop))

    def y_forward(buf, ssem, rsem, n):
        for i, (source, hop, rows_) in enumerate(((3, 1, FIRST), (1, 3, SECOND))):
            whole = buf((zl + n) % 4, (y + source) % 4)
            arrived(whole, rsem.at[n, source])
            send(cut(whole, rows_), cut(whole, rows_), ssem.at[n, 2 + i], rsem.at[n, 2 + 2 * i], at(dy=hop))

    def y_rest(buf, rsem, n):
        for i, rows_ in enumerate((FIRST, SECOND)):
            arrived(cut(buf((zl + n) % 4, (y + 2) % 4), rows_), rsem.at[n, 2 + 2 * i])

    def zl_spread(buf, ssem, rsem):
        piece = buf(zl, y)
        for d in (1, 3, 2):
            send(piece, piece, ssem.at[d, 4], rsem.at[4 - d, 0], at(dzl=d))

    def zl_wait(buf, rsem, n):
        arrived(buf((zl + n) % 4, y), rsem.at[n, 0])

    def y_all(n):
        piece = gr.at[(zl + n) % 4, y]
        for d in (2, 1, 3):
            send(piece, piece, gsend.at[n, d], grecv.at[n, 4 - d], at(dy=d))

    def x_all(n):
        piece = gc.at[(zh + n) % 4, k, x]
        for d in (2, 1, 3):
            send(piece, piece, csend.at[n, d], crecv.at[n, 4 - d], at(dx=d))

    def x_gc_core(n):
        zp = (zh + n) % 4
        for d in (1, 3, 2):
            arrived(gc.at[zp, k, (x + d) % 4], crecv.at[n, d])
        send(gc.at[zp, k], gc.at[zp, k], csend.at[n, 4], crecv.at[n, 6], at(dk=1))

    def gr_at(zp, yp):
        return gr.at[zp, yp]

    for i, hop in enumerate((1, 3)):
        send(gc.at[zh, k, x], gc.at[zh, k, x], csend.at[2 * i, 5], crecv.at[4 - hop, 0], at(dzh=hop))
    x_all(0)
    y_all(0)
    x_gc_core(0)
    zl_spread(gr_at, gsend, grecv)
    x_forward(1, 1)
    x_forward(3, 0)
    for i, (source, hop, rows_) in enumerate(((3, 1, FIRST), (1, 3, SECOND))):
        whole = gc.at[(zh + source) % 4, k, x]
        arrived(whole, crecv.at[source, 0])
        send(cut(whole, rows_), cut(whole, rows_), csend.at[1 + 2 * i, 5], crecv.at[2, 5 * i], at(dzh=hop))
        x_all(source)
    for n in (3, 1, 2):
        zl_wait(gr_at, grecv, n)
        y_all(n)
    x_gc_core(3)
    x_gc_core(1)
    for i, rows_ in enumerate((FIRST, SECOND)):
        arrived(cut(gc.at[(zh + 2) % 4, k, x], rows_), crecv.at[2, 5 * i])
    x_all(2)
    zmove((3, 0), 1, tile_rows(1 - half_before), B, 3, zrecv.at[2, 1 - half_before])
    zmove((3, 1), 3, tile_rows(3 - half_after), B, 1, zrecv.at[2, 3 - half_after])
    x_gc_core(2)
    for n in range(4):
        for d in (1, 3, 2):
            arrived(gr.at[(zl + n) % 4, (y + d) % 4], grecv.at[n, d])

    square = jnp.zeros((H, B), jnp.float32)
    for n in (0, 3, 1, 2):
        zp = (zh + n) % 4
        arrived(gc.at[zp, 1 - k], crecv.at[n, 6])
        for xp in range(4):
            right = jnp.concatenate([gc[zp, 0, xp], gc[zp, 1, xp]], axis=0)
            square = square + nn_dot(gr[zp, xp], right)
    pr[zl, k, y] = (coef_b * gr[zl, y].astype(jnp.float32) + coef_c * square).astype(jnp.bfloat16)

    def pr_at(zp, yp):
        return pr.at[zp, k, yp]

    def p_all(n):
        piece = pr_at((zl + n) % 4, y)
        for d in (2, 1, 3):
            send(piece, piece, psend.at[n, d], precv.at[n, 4 - d], at(dy=d))

    def p_core(n):
        if n == 2:
            for d in (1, 3, 2):
                arrived(pr_at((zl + n) % 4, (y + d) % 4), precv.at[n, d])
        else:
            y_rest(pr_at, precv, n)
        zp = (zl + n) % 4
        send(pr.at[zp, k], pr.at[zp, k], psend.at[n, 5], precv.at[n, 5], at(dk=1))

    def product(n):
        zp = (zl + n) % 4
        arrived(pr.at[zp, 1 - k], precv.at[n, 5])

        def one(xp):
            return nn_dot(jnp.concatenate([pr[zp, 0, xp], pr[zp, 1, xp]], axis=0), unpack(zp, xp))

        acc[...] += (one(0) + one(1)) + (one(2) + one(3))

    psems = (pr_at, psend, precv)
    zl_spread(*psems)
    y_spread(*psems, 0)
    acc[...] = coef_a * x_ref[...].astype(jnp.float32)
    y_forward(*psems, 0)
    for n in (3, 1):
        zl_wait(pr_at, precv, n)
        y_spread(*psems, n)
    zl_wait(pr_at, precv, 2)
    p_all(2)
    for t, up in late:
        zwait(2, t)
        x2_spread(t)
    p_core(0)
    for n in (3, 1):
        y_forward(*psems, n)
    for t, up in late:
        x2_forward(t, up)
    x_rest(1)
    x_rest(3)
    p_core(3)
    for t, up in early + late:
        x2_rest(t, up)
    product(0)
    p_core(1)
    product(3)
    p_core(2)
    product(1)
    product(2)
    o_ref[...] = (factor * acc[...]).astype(jnp.bfloat16)

    for copy in started:
        copy.wait_send()
    for dz in range(4):
        d, copy = sum3(dz)

        @pl.when(d != 0)
        def _(copy=copy):
            copy.wait_send()

    flip_copy(1 - k).wait_send()

    @pl.when(zh != zl)
    def _():
        flip_copy(k).wait_send()

    @pl.when(x != y)
    def _():
        swap_copy.wait_send()


def on_device(momentum):
    bf16, f32 = jnp.bfloat16, jnp.float32
    dma = pltpu.SemaphoreType.DMA
    return pl.pallas_call(
        kernel,
        out_shape=jax.ShapeDtypeStruct((B, W), bf16),
        in_specs=[pl.BlockSpec(memory_space=pltpu.HBM)],
        out_specs=pl.BlockSpec(memory_space=pltpu.VMEM),
        scratch_shapes=[
            pltpu.VMEM((B, W), bf16),
            pltpu.VMEM((4, 4, PACK, 128), bf16),
            pltpu.VMEM((4, 4 * B, B), f32),
            pltpu.VMEM((4, 4, H, B), bf16),
            pltpu.VMEM((4, 4, H, B), bf16),
            pltpu.VMEM((4, 3, H, B), bf16),
            pltpu.VMEM((4, 3, H, B), bf16),
            pltpu.VMEM((4, H, B), f32),
            pltpu.VMEM((4, H, B), bf16),
            pltpu.VMEM((4, H, B), bf16),
            pltpu.VMEM((H, B), bf16),
            pltpu.VMEM((H, B), bf16),
            pltpu.VMEM((2, H, H), bf16),
            pltpu.VMEM((2, H, H), bf16),
            pltpu.VMEM((H, B), f32),
            pltpu.VMEM((2, H, H), f32),
            pltpu.VMEM((4, 4, H, B), bf16),
            pltpu.VMEM((4, 2, 4, H, B), bf16),
            pltpu.VMEM((4, 2, 4, H, B), bf16),
            pltpu.VMEM((B, W), f32),
            dma,
            dma((4, 5)),
            dma((4, 5)),
            dma((3, 4, 2)),
            dma((4, 4, 2)),
            dma((3, 5)),
            dma((4, 5)),
            dma((5, 4)),
            dma((5, 4)),
            dma((3,)),
            dma((3,)),
            dma((4, 5)),
            dma((4, 5)),
            dma((4, 6)),
            dma((4, 7)),
            dma((4, 6)),
            dma((4, 6)),
        ],
        compiler_params=pltpu.CompilerParams(
            collective_id=0, has_side_effects=True, vmem_limit_bytes=60 * 2**20
        ),
        cost_estimate=pl.CostEstimate(flops=4 * 10**9, bytes_accessed=2 * 10**7, transcendentals=0),
    )(momentum)


def solution(mesh):
    return jax.shard_map(
        on_device, mesh=mesh, in_specs=(P("row", "col"),), out_specs=P("row", "col"), check_vma=False
    )
```

```python
import jax
import jax.numpy as jnp
from jax import lax
from jax.experimental import pallas as pl
from jax.experimental.pallas import tpu as pltpu
from jax.sharding import PartitionSpec as P

NR = 3584
NC = 18432

coef_a = 3.4445
coef_b = -4.775
coef_c = 2.0315
factor = 0.2 * max(NR, NC) ** 0.5

MESH = pl.DeviceIdType.MESH

B = 224
H = 112
W = 576
TILES = 4
PACK = TILES * B + H
LOW = (0, 2 * B)
HIGH = (2 * B, 2 * B + H)
FIRST = (0, 64)
SECOND = (64, 48)
LATE_LOW = ((B, B), (0, B))
LATE_HIGH = ((3 * B, B + H), (2 * B, B))
REST = (TILES * B, H)


def nt_dot(a, b):
    return lax.dot_general(a, b, (((1,), (1,)), ((), ())), preferred_element_type=jnp.float32)


def nn_dot(a, b):
    return lax.dot_general(a, b, (((1,), (0,)), ((), ())), preferred_element_type=jnp.float32)


def kernel(
    x_hbm,
    o_ref,
    x_ref,
    xs,
    part,
    send1,
    recv1,
    send2,
    recv2,
    sum2,
    send3,
    recv3,
    swap_send,
    swap_recv,
    flip_send,
    flip_recv,
    swap_sum,
    flip_sum,
    gr,
    gc,
    pr,
    acc,
    load_sem,
    zsend,
    zrecv,
    xsend,
    xrecv,
    x2send,
    x2recv,
    rsend,
    rrecv,
    tsend,
    trecv,
    gsend,
    grecv,
    csend,
    crecv,
    psend,
    precv,
):
    row = lax.axis_index("row")
    col = lax.axis_index("col")
    x, zh = row // 4, row % 4
    y, zl, k = col // 8, (col // 2) % 4, col % 2
    sign = 1 + 2 * (zl % 2)

    def place(x_, zh_, y_, zl_, k_):
        return (x_ * 4 + zh_, y_ * 8 + zl_ * 2 + k_)

    def at(dx=0, dzh=0, dy=0, dzl=0, dk=0):
        return place((x + dx) % 4, (zh + dzh) % 4, (y + dy) % 4, (zl + dzl) % 4, (k + dk) % 2)

    def station(dz):
        return (zh + sign * dz) % 4

    started = []

    def send(src, dst, ssem, rsem, device):
        copy = pltpu.make_async_remote_copy(
            src_ref=src, dst_ref=dst, send_sem=ssem, recv_sem=rsem, device_id=device, device_id_type=MESH
        )
        copy.start()
        started.append(copy)

    def arrived(dst, rsem):
        pltpu.make_async_copy(dst, dst, rsem).wait()

    def rest(zp, xp):
        last = xs[zp, xp, pl.ds(TILES * B, H), :]
        return jnp.concatenate([last[:, :64], last[:, 64:]], axis=0)

    def tile_of(zp, xp, t):
        return xs[zp, xp, pl.ds(pl.multiple_of(t * B, 16), B), :]

    def unpack(zp, xp):
        return jnp.concatenate([tile_of(zp, xp, t) for t in range(TILES)] + [rest(zp, xp)], axis=1)

    load = pltpu.make_async_copy(x_hbm, x_ref, load_sem)
    load.start()
    barrier = pltpu.get_barrier_semaphore()
    peers = [at(dx=d) for d in (1, 2, 3)] + [at(dzh=d) for d in (1, 3)]
    peers += [at(dy=d) for d in (1, 2, 3)] + [at(dzl=d) for d in (1, 2, 3)] + [at(dk=1)]
    swap_peer = place(y, zh, x, zl, k)
    flip_peers = [place(x, zl, y, zh, n) for n in range(2)]
    for peer in peers:
        pl.semaphore_signal(barrier, 1, device_id=peer, device_id_type=MESH)

    load.wait()
    for t in range(TILES):
        xs[zh, x, pl.ds(t * B, B), :] = x_ref[:, pl.ds(t * 128, 128)]
    xs[zh, x, pl.ds(TILES * B, H), :] = jnp.concatenate(
        [x_ref[pl.ds(0, H), pl.ds(TILES * 128, 64)], x_ref[pl.ds(H, H), pl.ds(TILES * 128, 64)]], axis=1
    )
    pl.semaphore_wait(barrier, len(peers))

    def rows(dz, dx, start, size):
        return xs.at[station(dz), (x + dx) % 4, pl.ds(start, size)]

    def zmove(sem, dz, start, size, hop, rsem):
        piece = rows(dz, 0, start, size)
        send(piece, piece, zsend.at[sem], rsem, at(dzh=sign * hop))

    def xmove(kind, dz, dx, part_, hop):
        piece = rows(dz, dx, *(LOW, HIGH)[part_])
        send(piece, piece, xsend.at[kind, dz, part_], xrecv.at[dz, (dx - hop) % 4, part_], at(dx=hop))

    def xwait(dz, dx, part_):
        arrived(rows(dz, dx, *(LOW, HIGH)[part_]), xrecv.at[dz, dx, part_])

    def x_spread(dz, part_):
        xmove(0, dz, 0, part_, 1)
        xmove(1, dz, 0, part_, 3)

    def x_forward(dz, part_):
        source, hop = ((3, 1), (1, 3))[part_]
        xwait(dz, source, part_)
        xmove(2, dz, source, part_, hop)

    def x_rest(dz):
        for part_, source in ((0, 1), (1, 3)):
            xwait(dz, source, part_)
            xwait(dz, 2, part_)

    def tile_rows(t):
        return pl.multiple_of(t * B, 16)

    def zwait(dz, t):
        arrived(rows(dz, 0, tile_rows(t), B), zrecv.at[dz, t])

    def zwait_rest(dz):
        arrived(rows(dz, 0, *REST), zrecv.at[dz, 4])

    def x2_rows(dx, t):
        return rows(2, dx, *(REST if t is None else (tile_rows(t), B)))

    def x2_move(kind, dx, t, hop):
        piece, sem = x2_rows(dx, t), 4 if t is None else t
        send(piece, piece, x2send.at[kind, sem], x2recv.at[(dx - hop) % 4, sem], at(dx=hop))

    def x2_wait(dx, t):
        arrived(x2_rows(dx, t), x2recv.at[dx, 4 if t is None else t])

    def x2_spread(t):
        x2_move(0, 0, t, 1)
        x2_move(1, 0, t, 3)

    def x2_forward(t, up):
        source, hop = (3, 1) if up else (1, 3)
        x2_wait(source, t)
        x2_move(2, source, t, hop)

    def x2_rest(t, up):
        x2_wait(1 if up else 3, t)
        x2_wait(2, t)

    half = zh // 2
    half_before = ((zh + 4 - sign) % 4) // 2
    half_after = ((zh + sign) % 4) // 2

    def gram(dz):
        zp = station(dz)

        def stack(piece):
            return jnp.concatenate([piece(zh, xp) for xp in range(4)], axis=0)

        def dot(pieces):
            return nt_dot(
                jnp.concatenate([stack(piece) for piece in pieces], axis=1),
                jnp.concatenate([piece(zp, x) for piece in pieces], axis=1),
            )

        tiles = [lambda z_, x_, t=t: tile_of(z_, x_, t) for t in (0, 1, 2, 3, half, 2 + half)]
        if dz == 0:
            value = 0.5 * dot(tiles[:4] + [rest])
        elif dz == 1:
            value = dot(tiles[:2])
        elif dz == 3:
            value = dot(tiles[2:4] + [rest])
        else:
            value = dot(tiles[4:]) + 0.5 * dot([rest])
        part[dz] = value
        for xp in range(4):
            mine = pl.multiple_of(xp * B + (1 - k) * H, 16)
            send1[dz, xp] = part[dz, pl.ds(mine, H), :].astype(jnp.bfloat16)
        send(send1.at[dz], recv1.at[dz], rsend.at[0, dz], rrecv.at[0, dz], at(dk=1))

    def reduce_core(dz):
        arrived(recv1.at[dz], rrecv.at[0, dz])

        def both(xp):
            mine = pl.multiple_of(xp * B + k * H, 16)
            return part[dz, pl.ds(mine, H), :] + recv1[dz, xp].astype(jnp.float32)

        for dy in (2, 1, 3):
            send2[dz, dy - 1] = both((y + dy) % 4).astype(jnp.bfloat16)
            send(send2.at[dz, dy - 1], recv2.at[dz, dy - 1], rsend.at[dy, dz], rrecv.at[dy, dz], at(dy=dy))
        sum2[dz] = both(y)

    def sum3(dz):
        owner = station(dz)
        d = (owner + 4 - zl) % 4
        copy = pltpu.make_async_remote_copy(
            src_ref=send3.at[dz],
            dst_ref=recv3.at[d],
            send_sem=rsend.at[4, dz],
            recv_sem=rrecv.at[4, d],
            device_id=place(x, zh, y, owner, k),
            device_id_type=MESH,
        )
        return d, copy

    def reduce_y(dz):
        for dy in (1, 3, 2):
            arrived(recv2.at[dz, dy - 1], rrecv.at[dy, dz])
        total = sum2[dz]
        for dy in (1, 2, 3):
            total = total + recv2[dz, dy - 1].astype(jnp.float32)
        sum2[dz] = total
        send3[dz] = total.astype(jnp.bfloat16)
        d, copy = sum3(dz)

        @pl.when(d != 0)
        def _():
            copy.start()

    for t in (0, 1):
        zmove((0, t), 0, t * B, B, 3, zrecv.at[1, t])
        zmove((0, 2 + t), 0, (2 + t) * B, B, 1, zrecv.at[3, 2 + t])
        xmove(t, 0, 0, t, 1 + 2 * t)
    zmove((0, 4), 0, *REST, 1, zrecv.at[3, 4])
    for t in (0, 1):
        xmove(1 - t, 0, 0, t, 3 - 2 * t)
    x_forward(0, 0)
    x_forward(0, 1)
    zwait(1, half_before)
    zmove((2, 0), 1, tile_rows(half_before), B, 3, zrecv.at[2, half_before])
    zwait(3, 2 + half_after)
    zmove((2, 1), 3, tile_rows(2 + half_after), B, 1, zrecv.at[2, 2 + half_after])
    zwait_rest(3)
    zmove((2, 2), 3, *REST, 1, zrecv.at[2, 4])
    x_rest(0)
    gram(0)
    zwait(1, 1 - half_before)
    gram(1)
    x_spread(1, 0)
    reduce_core(0)
    zwait(3, 3 - half_after)
    gram(3)
    x_spread(3, 1)
    reduce_core(1)
    reduce_core(3)
    reduce_y(0)
    zwait(2, half)
    zwait(2, 2 + half)
    zwait_rest(2)
    gram(2)
    zmove((1, 0), 0, *LATE_HIGH[0], 3, zrecv.at[1, 3])
    zmove((1, 1), 0, *LATE_LOW[0], 1, zrecv.at[3, 1])
    early = ((half, True), (2 + half, False), (None, True))
    late = ((1 - half, True), (3 - half, False))
    for t, up in early:
        x2_spread(t)
    reduce_y(1)
    reduce_core(2)
    reduce_y(3)
    x_forward(1, 0)
    x_forward(3, 1)
    reduce_y(2)

    total = sum2[(sign * (zl + 4 - zh)) % 4]
    for d in (1, 2, 3):
        arrived(recv3.at[d], rrecv.at[4, d])
        total = total + recv3[d].astype(jnp.float32)

    swap_send[...] = total.astype(jnp.bfloat16)
    flipped = total.T
    for n in range(2):
        flip_send[n] = flipped[n * H : (n + 1) * H, :].astype(jnp.bfloat16)
    swap_copy = pltpu.make_async_remote_copy(
        src_ref=swap_send,
        dst_ref=swap_recv,
        send_sem=tsend.at[0],
        recv_sem=trecv.at[0],
        device_id=swap_peer,
        device_id_type=MESH,
    )

    def flip_copy(n):
        return pltpu.make_async_remote_copy(
            src_ref=flip_send.at[n],
            dst_ref=flip_recv.at[k],
            send_sem=tsend.at[1 + n],
            recv_sem=trecv.at[1 + k],
            device_id=(flip_peers[0][0], y * 8 + zh * 2 + n),
            device_id_type=MESH,
        )

    @pl.when(x != y)
    def _():
        swap_copy.start()

    @pl.when(x == y)
    def _():
        swap_sum[...] = total

    flip_copy(1 - k).start()

    @pl.when(zh != zl)
    def _():
        flip_copy(k).start()

    @pl.when(zh == zl)
    def _():
        swap_send2 = jnp.where(k == 0, flipped[:H, :], flipped[H:, :])
        flip_sum[k] = swap_send2

    zmove((1, 2), 0, *LATE_HIGH[1], 3, zrecv.at[1, 2])
    zmove((1, 3), 0, *LATE_LOW[1], 1, zrecv.at[3, 0])
    for t, up in early:
        x2_forward(t, up)

    @pl.when(x != y)
    def _():
        arrived(swap_recv, trecv.at[0])
        swap_sum[...] = swap_recv[...].astype(jnp.float32)

    @pl.when(zh != zl)
    def _():
        arrived(flip_recv.at[k], trecv.at[1 + k])
        flip_sum[k] = flip_recv[k].astype(jnp.float32)

    arrived(flip_recv.at[1 - k], trecv.at[2 - k])
    flip_sum[1 - k] = flip_recv[1 - k].astype(jnp.float32)
    tile = (swap_sum[...] + jnp.concatenate([flip_sum[0], flip_sum[1]], axis=1)).astype(jnp.bfloat16)

    gr[zl, y] = tile
    gc[zh, k, x] = tile

    def cut(ref, piece):
        return ref.at[pl.ds(*piece)]

    def y_spread(buf, ssem, rsem, n):
        piece = buf((zl + n) % 4, y)
        for i, hop in enumerate((1, 3)):
            send(piece, piece, ssem.at[n, i], rsem.at[n, 4 - hop], at(dy=hop))

    def y_forward(buf, ssem, rsem, n):
        for i, (source, hop, rows_) in enumerate(((3, 1, FIRST), (1, 3, SECOND))):
            whole = buf((zl + n) % 4, (y + source) % 4)
            arrived(whole, rsem.at[n, source])
            send(cut(whole, rows_), cut(whole, rows_), ssem.at[n, 2 + i], rsem.at[n, 2 + 2 * i], at(dy=hop))

    def y_rest(buf, rsem, n):
        for i, rows_ in enumerate((FIRST, SECOND)):
            arrived(cut(buf((zl + n) % 4, (y + 2) % 4), rows_), rsem.at[n, 2 + 2 * i])

    def zl_spread(buf, ssem, rsem):
        piece = buf(zl, y)
        for d in (1, 3, 2):
            send(piece, piece, ssem.at[d, 4], rsem.at[4 - d, 0], at(dzl=d))

    def zl_wait(buf, rsem, n):
        arrived(buf((zl + n) % 4, y), rsem.at[n, 0])

    def y_all(n):
        piece = gr.at[(zl + n) % 4, y]
        for d in (2, 1, 3):
            send(piece, piece, gsend.at[n, d], grecv.at[n, 4 - d], at(dy=d))

    def x_all(n):
        piece = gc.at[(zh + n) % 4, k, x]
        for d in (2, 1, 3):
            send(piece, piece, csend.at[n, d], crecv.at[n, 4 - d], at(dx=d))

    def x_gc_spread(n):
        piece = gc.at[(zh + n) % 4, k, x]
        for i, hop in enumerate((1, 3)):
            send(piece, piece, csend.at[n, i], crecv.at[n, 4 - hop], at(dx=hop))

    def x_gc_forward(n):
        for i, (source, hop, rows_) in enumerate(((3, 1, FIRST), (1, 3, SECOND))):
            whole = gc.at[(zh + n) % 4, k, (x + source) % 4]
            arrived(whole, crecv.at[n, source])
            send(cut(whole, rows_), cut(whole, rows_), csend.at[n, 2 + i], crecv.at[n, 2 + 2 * i], at(dx=hop))

    def x_gc_core(n):
        zp = (zh + n) % 4
        if n % 2:
            for i, rows_ in enumerate((FIRST, SECOND)):
                arrived(cut(gc.at[zp, k, (x + 2) % 4], rows_), crecv.at[n, 2 + 2 * i])
        else:
            for d in (1, 3, 2):
                arrived(gc.at[zp, k, (x + d) % 4], crecv.at[n, d])
        send(gc.at[zp, k], gc.at[zp, k], csend.at[n, 4], crecv.at[n, 6], at(dk=1))

    def gr_at(zp, yp):
        return gr.at[zp, yp]

    for i, hop in enumerate((1, 3)):
        send(gc.at[zh, k, x], gc.at[zh, k, x], csend.at[2 * i, 5], crecv.at[4 - hop, 0], at(dzh=hop))
    x_all(0)
    y_all(0)
    x_gc_core(0)
    zl_spread(gr_at, gsend, grecv)
    for i, (source, hop, rows_) in enumerate(((3, 1, FIRST), (1, 3, SECOND))):
        whole = gc.at[(zh + source) % 4, k, x]
        arrived(whole, crecv.at[source, 0])
        send(cut(whole, rows_), cut(whole, rows_), csend.at[1 + 2 * i, 5], crecv.at[2, 5 * i], at(dzh=hop))
        x_gc_spread(source)
    for n in (3, 1, 2):
        zl_wait(gr_at, grecv, n)
        y_all(n)
    x_gc_forward(3)
    x_gc_forward(1)
    for i, rows_ in enumerate((FIRST, SECOND)):
        arrived(cut(gc.at[(zh + 2) % 4, k, x], rows_), crecv.at[2, 5 * i])
    x_all(2)
    zmove((3, 0), 1, tile_rows(1 - half_before), B, 3, zrecv.at[2, 1 - half_before])
    zmove((3, 1), 3, tile_rows(3 - half_after), B, 1, zrecv.at[2, 3 - half_after])
    for dz, part_, pieces in ((1, 1, LATE_HIGH), (3, 0, LATE_LOW)):
        for n, piece in enumerate(pieces):
            arrived(rows(dz, 0, *piece), zrecv.at[dz, (1 - n) + 2 * part_])
        x_spread(dz, part_)
    x_gc_core(3)
    x_gc_core(1)
    x_gc_core(2)
    for n in range(4):
        for d in (1, 3, 2):
            arrived(gr.at[(zl + n) % 4, (y + d) % 4], grecv.at[n, d])

    square = jnp.zeros((H, B), jnp.float32)
    for n in (0, 3, 1, 2):
        zp = (zh + n) % 4
        arrived(gc.at[zp, 1 - k], crecv.at[n, 6])
        for xp in range(4):
            right = jnp.concatenate([gc[zp, 0, xp], gc[zp, 1, xp]], axis=0)
            square = square + nn_dot(gr[zp, xp], right)
    pr[zl, k, y] = (coef_b * gr[zl, y].astype(jnp.float32) + coef_c * square).astype(jnp.bfloat16)

    def pr_at(zp, yp):
        return pr.at[zp, k, yp]

    def p_all(n):
        piece = pr_at((zl + n) % 4, y)
        for d in (2, 1, 3):
            send(piece, piece, psend.at[n, d], precv.at[n, 4 - d], at(dy=d))

    def p_core(n):
        if n == 2:
            for d in (1, 3, 2):
                arrived(pr_at((zl + n) % 4, (y + d) % 4), precv.at[n, d])
        else:
            y_rest(pr_at, precv, n)
        zp = (zl + n) % 4
        send(pr.at[zp, k], pr.at[zp, k], psend.at[n, 5], precv.at[n, 5], at(dk=1))

    def product(n):
        zp = (zl + n) % 4
        arrived(pr.at[zp, 1 - k], precv.at[n, 5])

        def one(xp):
            return nn_dot(jnp.concatenate([pr[zp, 0, xp], pr[zp, 1, xp]], axis=0), unpack(zp, xp))

        acc[...] += (one(0) + one(1)) + (one(2) + one(3))

    psems = (pr_at, psend, precv)
    zl_spread(*psems)
    y_spread(*psems, 0)
    acc[...] = coef_a * x_ref[...].astype(jnp.float32)
    y_forward(*psems, 0)
    for n in (3, 1):
        zl_wait(pr_at, precv, n)
        y_spread(*psems, n)
    zl_wait(pr_at, precv, 2)
    p_all(2)
    x_forward(1, 1)
    x_forward(3, 0)
    for t, up in late:
        zwait(2, t)
        x2_spread(t)
    p_core(0)
    for n in (3, 1):
        y_forward(*psems, n)
    for t, up in late:
        x2_forward(t, up)
    x_rest(1)
    x_rest(3)
    p_core(3)
    for t, up in early + late:
        x2_rest(t, up)
    product(0)
    p_core(1)
    product(3)
    p_core(2)
    product(1)
    product(2)
    o_ref[...] = (factor * acc[...]).astype(jnp.bfloat16)

    for copy in started:
        copy.wait_send()
    for dz in range(4):
        d, copy = sum3(dz)

        @pl.when(d != 0)
        def _(copy=copy):
            copy.wait_send()

    flip_copy(1 - k).wait_send()

    @pl.when(zh != zl)
    def _():
        flip_copy(k).wait_send()

    @pl.when(x != y)
    def _():
        swap_copy.wait_send()


def on_device(momentum):
    bf16, f32 = jnp.bfloat16, jnp.float32
    dma = pltpu.SemaphoreType.DMA
    return pl.pallas_call(
        kernel,
        out_shape=jax.ShapeDtypeStruct((B, W), bf16),
        in_specs=[pl.BlockSpec(memory_space=pltpu.HBM)],
        out_specs=pl.BlockSpec(memory_space=pltpu.VMEM),
        scratch_shapes=[
            pltpu.VMEM((B, W), bf16),
            pltpu.VMEM((4, 4, PACK, 128), bf16),
            pltpu.VMEM((4, 4 * B, B), f32),
            pltpu.VMEM((4, 4, H, B), bf16),
            pltpu.VMEM((4, 4, H, B), bf16),
            pltpu.VMEM((4, 3, H, B), bf16),
            pltpu.VMEM((4, 3, H, B), bf16),
            pltpu.VMEM((4, H, B), f32),
            pltpu.VMEM((4, H, B), bf16),
            pltpu.VMEM((4, H, B), bf16),
            pltpu.VMEM((H, B), bf16),
            pltpu.VMEM((H, B), bf16),
            pltpu.VMEM((2, H, H), bf16),
            pltpu.VMEM((2, H, H), bf16),
            pltpu.VMEM((H, B), f32),
            pltpu.VMEM((2, H, H), f32),
            pltpu.VMEM((4, 4, H, B), bf16),
            pltpu.VMEM((4, 2, 4, H, B), bf16),
            pltpu.VMEM((4, 2, 4, H, B), bf16),
            pltpu.VMEM((B, W), f32),
            dma,
            dma((4, 5)),
            dma((4, 5)),
            dma((3, 4, 2)),
            dma((4, 4, 2)),
            dma((3, 5)),
            dma((4, 5)),
            dma((5, 4)),
            dma((5, 4)),
            dma((3,)),
            dma((3,)),
            dma((4, 5)),
            dma((4, 5)),
            dma((4, 6)),
            dma((4, 7)),
            dma((4, 6)),
            dma((4, 6)),
        ],
        compiler_params=pltpu.CompilerParams(
            collective_id=0, has_side_effects=True, vmem_limit_bytes=60 * 2**20
        ),
        cost_estimate=pl.CostEstimate(flops=4 * 10**9, bytes_accessed=2 * 10**7, transcendentals=0),
    )(momentum)


def solution(mesh):
    return jax.shard_map(
        on_device, mesh=mesh, in_specs=(P("row", "col"),), out_specs=P("row", "col"), check_vma=False
    )
```

```python
import jax
import jax.numpy as jnp
from jax import lax
from jax.experimental import pallas as pl
from jax.experimental.pallas import tpu as pltpu
from jax.sharding import PartitionSpec as P

NR = 3584
NC = 18432

coef_a = 3.4445
coef_b = -4.775
coef_c = 2.0315
factor = 0.2 * max(NR, NC) ** 0.5

MESH = pl.DeviceIdType.MESH

B = 224
H = 112
W = 576
TILES = 4
PACK = TILES * B + H
LOW = (0, 2 * B)
HIGH = (2 * B, 2 * B + H)
FIRST = (0, 64)
SECOND = (64, 48)
REST = (TILES * B, H)


def nt_dot(a, b):
    return lax.dot_general(a, b, (((1,), (1,)), ((), ())), preferred_element_type=jnp.float32)


def nn_dot(a, b):
    return lax.dot_general(a, b, (((1,), (0,)), ((), ())), preferred_element_type=jnp.float32)


def kernel(
    x_hbm,
    o_ref,
    x_ref,
    xs,
    part,
    send1,
    recv1,
    send2,
    recv2,
    sum2,
    send3,
    recv3,
    swap_send,
    swap_recv,
    flip_send,
    flip_recv,
    swap_sum,
    flip_sum,
    gr,
    gc,
    pr,
    acc,
    load_sem,
    zsend,
    zrecv,
    xsend,
    xrecv,
    x2send,
    x2recv,
    rsend,
    rrecv,
    tsend,
    trecv,
    gsend,
    grecv,
    csend,
    crecv,
    psend,
    precv,
):
    row = lax.axis_index("row")
    col = lax.axis_index("col")
    x, zh = row // 4, row % 4
    y, zl, k = col // 8, (col // 2) % 4, col % 2
    sign = 1 + 2 * (zl % 2)

    def place(x_, zh_, y_, zl_, k_):
        return (x_ * 4 + zh_, y_ * 8 + zl_ * 2 + k_)

    def at(dx=0, dzh=0, dy=0, dzl=0, dk=0):
        return place((x + dx) % 4, (zh + dzh) % 4, (y + dy) % 4, (zl + dzl) % 4, (k + dk) % 2)

    def station(dz):
        return (zh + sign * dz) % 4

    started = []

    def send(src, dst, ssem, rsem, device):
        copy = pltpu.make_async_remote_copy(
            src_ref=src, dst_ref=dst, send_sem=ssem, recv_sem=rsem, device_id=device, device_id_type=MESH
        )
        copy.start()
        started.append(copy)

    def arrived(dst, rsem):
        pltpu.make_async_copy(dst, dst, rsem).wait()

    def rest(zp, xp):
        last = xs[zp, xp, pl.ds(TILES * B, H), :]
        return jnp.concatenate([last[:, :64], last[:, 64:]], axis=0)

    def tile_of(zp, xp, t):
        return xs[zp, xp, pl.ds(pl.multiple_of(t * B, 16), B), :]

    def unpack(zp, xp):
        return jnp.concatenate([tile_of(zp, xp, t) for t in range(TILES)] + [rest(zp, xp)], axis=1)

    load = pltpu.make_async_copy(x_hbm, x_ref, load_sem)
    load.start()
    barrier = pltpu.get_barrier_semaphore()
    peers = [at(dx=d) for d in (1, 2, 3)] + [at(dzh=d) for d in (1, 3)]
    peers += [at(dy=d) for d in (1, 2, 3)] + [at(dzl=d) for d in (1, 2, 3)] + [at(dk=1)]
    swap_peer = place(y, zh, x, zl, k)
    flip_peers = [place(x, zl, y, zh, n) for n in range(2)]
    for peer in peers:
        pl.semaphore_signal(barrier, 1, device_id=peer, device_id_type=MESH)

    load.wait()
    for t in range(TILES):
        xs[zh, x, pl.ds(t * B, B), :] = x_ref[:, pl.ds(t * 128, 128)]
    xs[zh, x, pl.ds(TILES * B, H), :] = jnp.concatenate(
        [x_ref[pl.ds(0, H), pl.ds(TILES * 128, 64)], x_ref[pl.ds(H, H), pl.ds(TILES * 128, 64)]], axis=1
    )
    pl.semaphore_wait(barrier, len(peers))

    def rows(dz, dx, start, size):
        return xs.at[station(dz), (x + dx) % 4, pl.ds(start, size)]

    def zmove(sem, dz, start, size, hop, rsem):
        piece = rows(dz, 0, start, size)
        send(piece, piece, zsend.at[sem], rsem, at(dzh=sign * hop))

    def xmove(kind, dz, dx, part_, hop):
        piece = rows(dz, dx, *(LOW, HIGH)[part_])
        send(piece, piece, xsend.at[kind, dz, part_], xrecv.at[dz, (dx - hop) % 4, part_], at(dx=hop))

    def xwait(dz, dx, part_):
        arrived(rows(dz, dx, *(LOW, HIGH)[part_]), xrecv.at[dz, dx, part_])

    def x_spread(dz, part_):
        xmove(0, dz, 0, part_, 1)
        xmove(1, dz, 0, part_, 3)

    def x_forward(dz, part_):
        source, hop = ((3, 1), (1, 3))[part_]
        xwait(dz, source, part_)
        xmove(2, dz, source, part_, hop)

    def x_rest(dz):
        for part_, source in ((0, 1), (1, 3)):
            xwait(dz, source, part_)
            xwait(dz, 2, part_)

    def tile_rows(t):
        return pl.multiple_of(t * B, 16)

    def zwait(dz, t):
        arrived(rows(dz, 0, tile_rows(t), B), zrecv.at[dz, t])

    def zwait_rest(dz):
        arrived(rows(dz, 0, *REST), zrecv.at[dz, 4])

    def x2_rows(dx, t):
        return rows(2, dx, *(REST if t is None else (tile_rows(t), B)))

    def x2_move(kind, dx, t, hop):
        piece, sem = x2_rows(dx, t), 4 if t is None else t
        send(piece, piece, x2send.at[kind, sem], x2recv.at[(dx - hop) % 4, sem], at(dx=hop))

    def x2_wait(dx, t):
        arrived(x2_rows(dx, t), x2recv.at[dx, 4 if t is None else t])

    def x2_spread(t):
        x2_move(0, 0, t, 1)
        x2_move(1, 0, t, 3)

    def x2_forward(t, up):
        source, hop = (3, 1) if up else (1, 3)
        x2_wait(source, t)
        x2_move(2, source, t, hop)

    def x2_rest(t, up):
        x2_wait(1 if up else 3, t)
        x2_wait(2, t)

    half = zh // 2
    half_before = ((zh + 4 - sign) % 4) // 2
    half_after = ((zh + sign) % 4) // 2

    def gram(dz):
        zp = station(dz)

        def stack(piece):
            return jnp.concatenate([piece(zh, xp) for xp in range(4)], axis=0)

        def dot(pieces):
            return nt_dot(
                jnp.concatenate([stack(piece) for piece in pieces], axis=1),
                jnp.concatenate([piece(zp, x) for piece in pieces], axis=1),
            )

        tiles = [lambda z_, x_, t=t: tile_of(z_, x_, t) for t in (0, 1, 2, 3, half, 2 + half)]
        if dz == 0:
            value = 0.5 * dot(tiles[:4] + [rest])
        elif dz == 1:
            value = dot(tiles[:2])
        elif dz == 3:
            value = dot(tiles[2:4] + [rest])
        else:
            value = dot(tiles[4:]) + 0.5 * dot([rest])
        part[dz] = value
        for xp in range(4):
            mine = pl.multiple_of(xp * B + (1 - k) * H, 16)
            send1[dz, xp] = part[dz, pl.ds(mine, H), :].astype(jnp.bfloat16)
        send(send1.at[dz], recv1.at[dz], rsend.at[0, dz], rrecv.at[0, dz], at(dk=1))

    def reduce_core(dz):
        arrived(recv1.at[dz], rrecv.at[0, dz])

        def both(xp):
            mine = pl.multiple_of(xp * B + k * H, 16)
            return part[dz, pl.ds(mine, H), :] + recv1[dz, xp].astype(jnp.float32)

        for dy in (2, 1, 3):
            send2[dz, dy - 1] = both((y + dy) % 4).astype(jnp.bfloat16)
            send(send2.at[dz, dy - 1], recv2.at[dz, dy - 1], rsend.at[dy, dz], rrecv.at[dy, dz], at(dy=dy))
        sum2[dz] = both(y)

    def sum3(dz):
        owner = station(dz)
        d = (owner + 4 - zl) % 4
        copy = pltpu.make_async_remote_copy(
            src_ref=send3.at[dz],
            dst_ref=recv3.at[d],
            send_sem=rsend.at[4, dz],
            recv_sem=rrecv.at[4, d],
            device_id=place(x, zh, y, owner, k),
            device_id_type=MESH,
        )
        return d, copy

    def reduce_y(dz):
        for dy in (1, 3, 2):
            arrived(recv2.at[dz, dy - 1], rrecv.at[dy, dz])
        total = sum2[dz]
        for dy in (1, 2, 3):
            total = total + recv2[dz, dy - 1].astype(jnp.float32)
        sum2[dz] = total
        send3[dz] = total.astype(jnp.bfloat16)
        d, copy = sum3(dz)

        @pl.when(d != 0)
        def _():
            copy.start()

    for t in (0, 1):
        zmove((0, t), 0, t * B, B, 3, zrecv.at[1, t])
        zmove((0, 2 + t), 0, (2 + t) * B, B, 1, zrecv.at[3, 2 + t])
        xmove(t, 0, 0, t, 1 + 2 * t)
    zmove((0, 4), 0, *REST, 1, zrecv.at[3, 4])
    for t in (0, 1):
        xmove(1 - t, 0, 0, t, 3 - 2 * t)
    x_forward(0, 0)
    x_forward(0, 1)
    zwait(1, half_before)
    zmove((2, 0), 1, tile_rows(half_before), B, 3, zrecv.at[2, half_before])
    zwait(3, 2 + half_after)
    zmove((2, 1), 3, tile_rows(2 + half_after), B, 1, zrecv.at[2, 2 + half_after])
    zwait_rest(3)
    zmove((2, 2), 3, *REST, 1, zrecv.at[2, 4])
    x_rest(0)
    gram(0)
    zwait(1, 1 - half_before)
    gram(1)
    x_spread(1, 0)
    reduce_core(0)
    zwait(3, 3 - half_after)
    gram(3)
    x_spread(3, 1)
    reduce_core(1)
    reduce_core(3)
    reduce_y(0)
    zwait(2, half)
    zwait(2, 2 + half)
    zwait_rest(2)
    gram(2)
    zmove((1, 0), 0, *HIGH, 3, zrecv.at[1, 2])
    zmove((1, 1), 0, *LOW, 1, zrecv.at[3, 0])
    early = ((half, True), (2 + half, False), (None, True))
    late = ((1 - half, True), (3 - half, False))
    for t, up in early:
        x2_spread(t)
    reduce_y(1)
    reduce_core(2)
    reduce_y(3)
    x_forward(1, 0)
    x_forward(3, 1)
    reduce_y(2)

    total = sum2[(sign * (zl + 4 - zh)) % 4]
    for d in (1, 2, 3):
        arrived(recv3.at[d], rrecv.at[4, d])
        total = total + recv3[d].astype(jnp.float32)

    swap_send[...] = total.astype(jnp.bfloat16)
    flipped = total.T
    for n in range(2):
        flip_send[n] = flipped[n * H : (n + 1) * H, :].astype(jnp.bfloat16)
    swap_copy = pltpu.make_async_remote_copy(
        src_ref=swap_send,
        dst_ref=swap_recv,
        send_sem=tsend.at[0],
        recv_sem=trecv.at[0],
        device_id=swap_peer,
        device_id_type=MESH,
    )

    def flip_copy(n):
        return pltpu.make_async_remote_copy(
            src_ref=flip_send.at[n],
            dst_ref=flip_recv.at[k],
            send_sem=tsend.at[1 + n],
            recv_sem=trecv.at[1 + k],
            device_id=(flip_peers[0][0], y * 8 + zh * 2 + n),
            device_id_type=MESH,
        )

    @pl.when(x != y)
    def _():
        swap_copy.start()

    @pl.when(x == y)
    def _():
        swap_sum[...] = total

    flip_copy(1 - k).start()

    @pl.when(zh != zl)
    def _():
        flip_copy(k).start()

    @pl.when(zh == zl)
    def _():
        swap_send2 = jnp.where(k == 0, flipped[:H, :], flipped[H:, :])
        flip_sum[k] = swap_send2

    for t, up in early:
        x2_forward(t, up)
    arrived(rows(1, 0, *HIGH), zrecv.at[1, 2])
    x_spread(1, 1)
    arrived(rows(3, 0, *LOW), zrecv.at[3, 0])
    x_spread(3, 0)

    @pl.when(x != y)
    def _():
        arrived(swap_recv, trecv.at[0])
        swap_sum[...] = swap_recv[...].astype(jnp.float32)

    @pl.when(zh != zl)
    def _():
        arrived(flip_recv.at[k], trecv.at[1 + k])
        flip_sum[k] = flip_recv[k].astype(jnp.float32)

    arrived(flip_recv.at[1 - k], trecv.at[2 - k])
    flip_sum[1 - k] = flip_recv[1 - k].astype(jnp.float32)
    tile = (swap_sum[...] + jnp.concatenate([flip_sum[0], flip_sum[1]], axis=1)).astype(jnp.bfloat16)

    gr[zl, y] = tile
    gc[zh, k, x] = tile

    def cut(ref, piece):
        return ref.at[pl.ds(*piece)]

    def zl_spread(buf, ssem, rsem):
        piece = buf(zl, y)
        for d in (1, 3, 2):
            send(piece, piece, ssem.at[d, 4], rsem.at[4 - d, 0], at(dzl=d))

    def zl_wait(buf, rsem, n):
        arrived(buf((zl + n) % 4, y), rsem.at[n, 0])

    def y_all(n):
        piece = gr.at[(zl + n) % 4, y]
        for d in (2, 1, 3):
            send(piece, piece, gsend.at[n, d], grecv.at[n, 4 - d], at(dy=d))

    def x_all(n):
        piece = gc.at[(zh + n) % 4, k, x]
        for d in (2, 1, 3):
            send(piece, piece, csend.at[n, d], crecv.at[n, 4 - d], at(dx=d))

    def x_gc_core(n):
        zp = (zh + n) % 4
        for d in (1, 3, 2):
            arrived(gc.at[zp, k, (x + d) % 4], crecv.at[n, d])
        send(gc.at[zp, k], gc.at[zp, k], csend.at[n, 4], crecv.at[n, 6], at(dk=1))

    def gr_at(zp, yp):
        return gr.at[zp, yp]

    for i, hop in enumerate((1, 3)):
        send(gc.at[zh, k, x], gc.at[zh, k, x], csend.at[2 * i, 5], crecv.at[4 - hop, 0], at(dzh=hop))
    x_all(0)
    y_all(0)
    x_gc_core(0)
    zl_spread(gr_at, gsend, grecv)
    x_forward(1, 1)
    x_forward(3, 0)
    for i, (source, hop, rows_) in enumerate(((3, 1, FIRST), (1, 3, SECOND))):
        whole = gc.at[(zh + source) % 4, k, x]
        arrived(whole, crecv.at[source, 0])
        send(cut(whole, rows_), cut(whole, rows_), csend.at[1 + 2 * i, 5], crecv.at[2, 5 * i], at(dzh=hop))
        x_all(source)
    for n in (3, 1, 2):
        zl_wait(gr_at, grecv, n)
        y_all(n)
    x_gc_core(3)
    x_gc_core(1)
    for i, rows_ in enumerate((FIRST, SECOND)):
        arrived(cut(gc.at[(zh + 2) % 4, k, x], rows_), crecv.at[2, 5 * i])
    x_all(2)
    zmove((3, 0), 1, tile_rows(1 - half_before), B, 3, zrecv.at[2, 1 - half_before])
    zmove((3, 1), 3, tile_rows(3 - half_after), B, 1, zrecv.at[2, 3 - half_after])
    x_gc_core(2)
    for n in range(4):
        for d in (1, 3, 2):
            arrived(gr.at[(zl + n) % 4, (y + d) % 4], grecv.at[n, d])

    square = jnp.zeros((H, B), jnp.float32)
    for n in (0, 3, 1, 2):
        zp = (zh + n) % 4
        arrived(gc.at[zp, 1 - k], crecv.at[n, 6])
        for xp in range(4):
            right = jnp.concatenate([gc[zp, 0, xp], gc[zp, 1, xp]], axis=0)
            square = square + nn_dot(gr[zp, xp], right)
    pr[zl, k, y] = (coef_b * gr[zl, y].astype(jnp.float32) + coef_c * square).astype(jnp.bfloat16)

    def pr_at(zp, yp):
        return pr.at[zp, k, yp]

    def p_all(n):
        piece = pr_at((zl + n) % 4, y)
        for d in (2, 1, 3):
            send(piece, piece, psend.at[n, d], precv.at[n, 4 - d], at(dy=d))

    def p_core(n):
        for d in (1, 3, 2):
            arrived(pr_at((zl + n) % 4, (y + d) % 4), precv.at[n, d])
        zp = (zl + n) % 4
        send(pr.at[zp, k], pr.at[zp, k], psend.at[n, 5], precv.at[n, 5], at(dk=1))

    def product(n):
        zp = (zl + n) % 4
        arrived(pr.at[zp, 1 - k], precv.at[n, 5])

        def one(xp):
            return nn_dot(jnp.concatenate([pr[zp, 0, xp], pr[zp, 1, xp]], axis=0), unpack(zp, xp))

        acc[...] += (one(0) + one(1)) + (one(2) + one(3))

    zl_spread(pr_at, psend, precv)
    p_all(0)
    acc[...] = coef_a * x_ref[...].astype(jnp.float32)
    for n in (3, 1, 2):
        zl_wait(pr_at, precv, n)
        p_all(n)
    for t, up in late:
        zwait(2, t)
        x2_spread(t)
    p_core(0)
    for t, up in late:
        x2_forward(t, up)
    x_rest(1)
    x_rest(3)
    p_core(3)
    for t, up in early + late:
        x2_rest(t, up)
    product(0)
    p_core(1)
    product(3)
    p_core(2)
    product(1)
    product(2)
    o_ref[...] = (factor * acc[...]).astype(jnp.bfloat16)

    for copy in started:
        copy.wait_send()
    for dz in range(4):
        d, copy = sum3(dz)

        @pl.when(d != 0)
        def _(copy=copy):
            copy.wait_send()

    flip_copy(1 - k).wait_send()

    @pl.when(zh != zl)
    def _():
        flip_copy(k).wait_send()

    @pl.when(x != y)
    def _():
        swap_copy.wait_send()


def on_device(momentum):
    bf16, f32 = jnp.bfloat16, jnp.float32
    dma = pltpu.SemaphoreType.DMA
    return pl.pallas_call(
        kernel,
        out_shape=jax.ShapeDtypeStruct((B, W), bf16),
        in_specs=[pl.BlockSpec(memory_space=pltpu.HBM)],
        out_specs=pl.BlockSpec(memory_space=pltpu.VMEM),
        scratch_shapes=[
            pltpu.VMEM((B, W), bf16),
            pltpu.VMEM((4, 4, PACK, 128), bf16),
            pltpu.VMEM((4, 4 * B, B), f32),
            pltpu.VMEM((4, 4, H, B), bf16),
            pltpu.VMEM((4, 4, H, B), bf16),
            pltpu.VMEM((4, 3, H, B), bf16),
            pltpu.VMEM((4, 3, H, B), bf16),
            pltpu.VMEM((4, H, B), f32),
            pltpu.VMEM((4, H, B), bf16),
            pltpu.VMEM((4, H, B), bf16),
            pltpu.VMEM((H, B), bf16),
            pltpu.VMEM((H, B), bf16),
            pltpu.VMEM((2, H, H), bf16),
            pltpu.VMEM((2, H, H), bf16),
            pltpu.VMEM((H, B), f32),
            pltpu.VMEM((2, H, H), f32),
            pltpu.VMEM((4, 4, H, B), bf16),
            pltpu.VMEM((4, 2, 4, H, B), bf16),
            pltpu.VMEM((4, 2, 4, H, B), bf16),
            pltpu.VMEM((B, W), f32),
            dma,
            dma((4, 5)),
            dma((4, 5)),
            dma((3, 4, 2)),
            dma((4, 4, 2)),
            dma((3, 5)),
            dma((4, 5)),
            dma((5, 4)),
            dma((5, 4)),
            dma((3,)),
            dma((3,)),
            dma((4, 5)),
            dma((4, 5)),
            dma((4, 6)),
            dma((4, 7)),
            dma((4, 6)),
            dma((4, 6)),
        ],
        compiler_params=pltpu.CompilerParams(
            collective_id=0, has_side_effects=True, vmem_limit_bytes=60 * 2**20
        ),
        cost_estimate=pl.CostEstimate(flops=4 * 10**9, bytes_accessed=2 * 10**7, transcendentals=0),
    )(momentum)


def solution(mesh):
    return jax.shard_map(
        on_device, mesh=mesh, in_specs=(P("row", "col"),), out_specs=P("row", "col"), check_vma=False
    )
```

```python
import jax
import jax.numpy as jnp
from jax import lax
from jax.experimental import pallas as pl
from jax.experimental.pallas import tpu as pltpu
from jax.sharding import PartitionSpec as P

NR = 3584
NC = 18432

coef_a = 3.4445
coef_b = -4.775
coef_c = 2.0315
factor = 0.2 * max(NR, NC) ** 0.5

MESH = pl.DeviceIdType.MESH

B = 224
H = 112
W = 576
TILES = 4
PACK = TILES * B + H
LOW = (0, 2 * B)
HIGH = (2 * B, 2 * B + H)
FIRST = (0, 64)
SECOND = (64, 48)
REST = (TILES * B, H)


def nt_dot(a, b):
    return lax.dot_general(a, b, (((1,), (1,)), ((), ())), preferred_element_type=jnp.float32)


def nn_dot(a, b):
    return lax.dot_general(a, b, (((1,), (0,)), ((), ())), preferred_element_type=jnp.float32)


def kernel(
    x_hbm,
    o_ref,
    x_ref,
    xs,
    part,
    send1,
    recv1,
    send2,
    recv2,
    sum2,
    send3,
    recv3,
    swap_send,
    swap_recv,
    flip_send,
    flip_recv,
    swap_sum,
    flip_sum,
    gr,
    gc,
    pr,
    acc,
    load_sem,
    zsend,
    zrecv,
    xsend,
    xrecv,
    x2send,
    x2recv,
    rsend,
    rrecv,
    tsend,
    trecv,
    gsend,
    grecv,
    csend,
    crecv,
    psend,
    precv,
):
    row = lax.axis_index("row")
    col = lax.axis_index("col")
    x, zh = row // 4, row % 4
    y, zl, k = col // 8, (col // 2) % 4, col % 2
    sign = 1 + 2 * (zl % 2)

    def place(x_, zh_, y_, zl_, k_):
        return (x_ * 4 + zh_, y_ * 8 + zl_ * 2 + k_)

    def at(dx=0, dzh=0, dy=0, dzl=0, dk=0):
        return place((x + dx) % 4, (zh + dzh) % 4, (y + dy) % 4, (zl + dzl) % 4, (k + dk) % 2)

    def station(dz):
        return (zh + sign * dz) % 4

    started = []

    def send(src, dst, ssem, rsem, device):
        copy = pltpu.make_async_remote_copy(
            src_ref=src, dst_ref=dst, send_sem=ssem, recv_sem=rsem, device_id=device, device_id_type=MESH
        )
        copy.start()
        started.append(copy)

    def arrived(dst, rsem):
        pltpu.make_async_copy(dst, dst, rsem).wait()

    def rest(zp, xp):
        last = xs[zp, xp, pl.ds(TILES * B, H), :]
        return jnp.concatenate([last[:, :64], last[:, 64:]], axis=0)

    def tile_of(zp, xp, t):
        return xs[zp, xp, pl.ds(pl.multiple_of(t * B, 16), B), :]

    def unpack(zp, xp):
        return jnp.concatenate([tile_of(zp, xp, t) for t in range(TILES)] + [rest(zp, xp)], axis=1)

    load = pltpu.make_async_copy(x_hbm, x_ref, load_sem)
    load.start()
    barrier = pltpu.get_barrier_semaphore()
    peers = [at(dx=d) for d in (1, 2, 3)] + [at(dzh=d) for d in (1, 3)]
    peers += [at(dy=d) for d in (1, 2, 3)] + [at(dzl=d) for d in (1, 2, 3)] + [at(dk=1)]
    swap_peer = place(y, zh, x, zl, k)
    flip_peers = [place(x, zl, y, zh, n) for n in range(2)]
    for peer in peers:
        pl.semaphore_signal(barrier, 1, device_id=peer, device_id_type=MESH)

    load.wait()
    for t in range(TILES):
        xs[zh, x, pl.ds(t * B, B), :] = x_ref[:, pl.ds(t * 128, 128)]
    xs[zh, x, pl.ds(TILES * B, H), :] = jnp.concatenate(
        [x_ref[pl.ds(0, H), pl.ds(TILES * 128, 64)], x_ref[pl.ds(H, H), pl.ds(TILES * 128, 64)]], axis=1
    )
    pl.semaphore_wait(barrier, len(peers))

    def rows(dz, dx, start, size):
        return xs.at[station(dz), (x + dx) % 4, pl.ds(start, size)]

    def zmove(sem, dz, start, size, hop, rsem):
        piece = rows(dz, 0, start, size)
        send(piece, piece, zsend.at[sem], rsem, at(dzh=sign * hop))

    def xmove(kind, dz, dx, part_, hop):
        piece = rows(dz, dx, *(LOW, HIGH)[part_])
        send(piece, piece, xsend.at[kind, dz, part_], xrecv.at[dz, (dx - hop) % 4, part_], at(dx=hop))

    def xwait(dz, dx, part_):
        arrived(rows(dz, dx, *(LOW, HIGH)[part_]), xrecv.at[dz, dx, part_])

    def x_spread(dz, part_):
        xmove(0, dz, 0, part_, 1)
        xmove(1, dz, 0, part_, 3)

    def x_forward(dz, part_):
        source, hop = ((3, 1), (1, 3))[part_]
        xwait(dz, source, part_)
        xmove(2, dz, source, part_, hop)

    def x_rest(dz):
        for part_, source in ((0, 1), (1, 3)):
            xwait(dz, source, part_)
            xwait(dz, 2, part_)

    def tile_rows(t):
        return pl.multiple_of(t * B, 16)

    def zwait(dz, t):
        arrived(rows(dz, 0, tile_rows(t), B), zrecv.at[dz, t])

    def zwait_rest(dz):
        arrived(rows(dz, 0, *REST), zrecv.at[dz, 4])

    def x2_rows(dx, t):
        return rows(2, dx, *(REST if t is None else (tile_rows(t), B)))

    def x2_move(kind, dx, t, hop):
        piece, sem = x2_rows(dx, t), 4 if t is None else t
        send(piece, piece, x2send.at[kind, sem], x2recv.at[(dx - hop) % 4, sem], at(dx=hop))

    def x2_wait(dx, t):
        arrived(x2_rows(dx, t), x2recv.at[dx, 4 if t is None else t])

    def x2_spread(t):
        x2_move(0, 0, t, 1)
        x2_move(1, 0, t, 3)

    def x2_forward(t, up):
        source, hop = (3, 1) if up else (1, 3)
        x2_wait(source, t)
        x2_move(2, source, t, hop)

    def x2_rest(t, up):
        x2_wait(1 if up else 3, t)
        x2_wait(2, t)

    half = zh // 2
    half_before = ((zh + 4 - sign) % 4) // 2
    half_after = ((zh + sign) % 4) // 2

    def gram(dz):
        zp = station(dz)

        def stack(piece):
            return jnp.concatenate([piece(zh, xp) for xp in range(4)], axis=0)

        def dot(pieces):
            return nt_dot(
                jnp.concatenate([stack(piece) for piece in pieces], axis=1),
                jnp.concatenate([piece(zp, x) for piece in pieces], axis=1),
            )

        tiles = [lambda z_, x_, t=t: tile_of(z_, x_, t) for t in (0, 1, 2, 3, half, 2 + half)]
        if dz == 0:
            value = 0.5 * dot(tiles[:4] + [rest])
        elif dz == 1:
            value = dot(tiles[:2])
        elif dz == 3:
            value = dot(tiles[2:4] + [rest])
        else:
            value = dot(tiles[4:]) + 0.5 * dot([rest])
        part[dz] = value
        for xp in range(4):
            mine = pl.multiple_of(xp * B + (1 - k) * H, 16)
            send1[dz, xp] = part[dz, pl.ds(mine, H), :].astype(jnp.bfloat16)
        send(send1.at[dz], recv1.at[dz], rsend.at[0, dz], rrecv.at[0, dz], at(dk=1))

    def reduce_core(dz):
        arrived(recv1.at[dz], rrecv.at[0, dz])

        def both(xp):
            mine = pl.multiple_of(xp * B + k * H, 16)
            return part[dz, pl.ds(mine, H), :] + recv1[dz, xp].astype(jnp.float32)

        for dy in (2, 1, 3):
            send2[dz, dy - 1] = both((y + dy) % 4).astype(jnp.bfloat16)
            send(send2.at[dz, dy - 1], recv2.at[dz, dy - 1], rsend.at[dy, dz], rrecv.at[dy, dz], at(dy=dy))
        sum2[dz] = both(y)

    def sum3(dz):
        owner = station(dz)
        d = (owner + 4 - zl) % 4
        copy = pltpu.make_async_remote_copy(
            src_ref=send3.at[dz],
            dst_ref=recv3.at[d],
            send_sem=rsend.at[4, dz],
            recv_sem=rrecv.at[4, d],
            device_id=place(x, zh, y, owner, k),
            device_id_type=MESH,
        )
        return d, copy

    def reduce_y(dz):
        for dy in (1, 3, 2):
            arrived(recv2.at[dz, dy - 1], rrecv.at[dy, dz])
        total = sum2[dz]
        for dy in (1, 2, 3):
            total = total + recv2[dz, dy - 1].astype(jnp.float32)
        sum2[dz] = total
        send3[dz] = total.astype(jnp.bfloat16)
        d, copy = sum3(dz)

        @pl.when(d != 0)
        def _():
            copy.start()

    for t in (0, 1):
        zmove((0, t), 0, t * B, B, 3, zrecv.at[1, t])
        zmove((0, 2 + t), 0, (2 + t) * B, B, 1, zrecv.at[3, 2 + t])
        xmove(t, 0, 0, t, 1 + 2 * t)
    zmove((0, 4), 0, *REST, 1, zrecv.at[3, 4])
    for t in (0, 1):
        xmove(1 - t, 0, 0, t, 3 - 2 * t)
    x_forward(0, 0)
    x_forward(0, 1)
    zwait(1, half_before)
    zmove((2, 0), 1, tile_rows(half_before), B, 3, zrecv.at[2, half_before])
    zwait(3, 2 + half_after)
    zmove((2, 1), 3, tile_rows(2 + half_after), B, 1, zrecv.at[2, 2 + half_after])
    zwait_rest(3)
    zmove((2, 2), 3, *REST, 1, zrecv.at[2, 4])
    x_rest(0)
    gram(0)
    zwait(1, 1 - half_before)
    gram(1)
    x_spread(1, 0)
    reduce_core(0)
    zwait(3, 3 - half_after)
    gram(3)
    x_spread(3, 1)
    reduce_core(1)
    reduce_core(3)
    reduce_y(0)
    zwait(2, half)
    zwait(2, 2 + half)
    zwait_rest(2)
    gram(2)
    zmove((1, 0), 0, *HIGH, 3, zrecv.at[1, 2])
    zmove((1, 1), 0, *LOW, 1, zrecv.at[3, 0])
    early = ((half, True), (2 + half, False), (None, True))
    late = ((1 - half, True), (3 - half, False))
    for t, up in early:
        x2_spread(t)
    reduce_y(1)
    reduce_core(2)
    reduce_y(3)
    x_forward(1, 0)
    x_forward(3, 1)
    reduce_y(2)

    total = sum2[(sign * (zl + 4 - zh)) % 4]
    for d in (1, 2, 3):
        arrived(recv3.at[d], rrecv.at[4, d])
        total = total + recv3[d].astype(jnp.float32)

    swap_send[...] = total.astype(jnp.bfloat16)
    flipped = total.T
    for n in range(2):
        flip_send[n] = flipped[n * H : (n + 1) * H, :].astype(jnp.bfloat16)
    swap_copy = pltpu.make_async_remote_copy(
        src_ref=swap_send,
        dst_ref=swap_recv,
        send_sem=tsend.at[0],
        recv_sem=trecv.at[0],
        device_id=swap_peer,
        device_id_type=MESH,
    )

    def flip_copy(n):
        return pltpu.make_async_remote_copy(
            src_ref=flip_send.at[n],
            dst_ref=flip_recv.at[k],
            send_sem=tsend.at[1 + n],
            recv_sem=trecv.at[1 + k],
            device_id=(flip_peers[0][0], y * 8 + zh * 2 + n),
            device_id_type=MESH,
        )

    @pl.when(x != y)
    def _():
        swap_copy.start()

    @pl.when(x == y)
    def _():
        swap_sum[...] = total

    flip_copy(1 - k).start()

    @pl.when(zh != zl)
    def _():
        flip_copy(k).start()

    @pl.when(zh == zl)
    def _():
        swap_send2 = jnp.where(k == 0, flipped[:H, :], flipped[H:, :])
        flip_sum[k] = swap_send2

    for t, up in early:
        x2_forward(t, up)
    arrived(rows(1, 0, *HIGH), zrecv.at[1, 2])
    x_spread(1, 1)
    arrived(rows(3, 0, *LOW), zrecv.at[3, 0])
    x_spread(3, 0)

    @pl.when(x != y)
    def _():
        arrived(swap_recv, trecv.at[0])
        swap_sum[...] = swap_recv[...].astype(jnp.float32)

    @pl.when(zh != zl)
    def _():
        arrived(flip_recv.at[k], trecv.at[1 + k])
        flip_sum[k] = flip_recv[k].astype(jnp.float32)

    arrived(flip_recv.at[1 - k], trecv.at[2 - k])
    flip_sum[1 - k] = flip_recv[1 - k].astype(jnp.float32)
    tile = (swap_sum[...] + jnp.concatenate([flip_sum[0], flip_sum[1]], axis=1)).astype(jnp.bfloat16)

    gr[zl, y] = tile
    gc[zh, k, x] = tile

    def cut(ref, piece):
        return ref.at[pl.ds(*piece)]

    def zl_spread(buf, ssem, rsem):
        piece = buf(zl, y)
        for d in (1, 3, 2):
            send(piece, piece, ssem.at[d, 4], rsem.at[4 - d, 0], at(dzl=d))

    def zl_wait(buf, rsem, n):
        arrived(buf((zl + n) % 4, y), rsem.at[n, 0])

    def y_all(n):
        piece = gr.at[(zl + n) % 4, y]
        for d in (2, 1, 3):
            send(piece, piece, gsend.at[n, d], grecv.at[n, 4 - d], at(dy=d))

    def x_all(n):
        piece = gc.at[(zh + n) % 4, k, x]
        for d in (2, 1, 3):
            send(piece, piece, csend.at[n, d], crecv.at[n, 4 - d], at(dx=d))

    def x_gc_core(n):
        zp = (zh + n) % 4
        for d in (1, 3, 2):
            arrived(gc.at[zp, k, (x + d) % 4], crecv.at[n, d])
        send(gc.at[zp, k], gc.at[zp, k], csend.at[n, 4], crecv.at[n, 6], at(dk=1))

    def gr_at(zp, yp):
        return gr.at[zp, yp]

    for i, hop in enumerate((1, 3)):
        send(gc.at[zh, k, x], gc.at[zh, k, x], csend.at[2 * i, 5], crecv.at[4 - hop, 0], at(dzh=hop))
    x_all(0)
    y_all(0)
    x_gc_core(0)
    zl_spread(gr_at, gsend, grecv)
    x_forward(1, 1)
    x_forward(3, 0)
    for i, (source, hop, rows_) in enumerate(((3, 1, FIRST), (1, 3, SECOND))):
        whole = gc.at[(zh + source) % 4, k, x]
        arrived(whole, crecv.at[source, 0])
        send(cut(whole, rows_), cut(whole, rows_), csend.at[1 + 2 * i, 5], crecv.at[2, 5 * i], at(dzh=hop))
        x_all(source)
    for n in (3, 1, 2):
        zl_wait(gr_at, grecv, n)
        y_all(n)
    x_gc_core(3)
    x_gc_core(1)
    for i, rows_ in enumerate((FIRST, SECOND)):
        arrived(cut(gc.at[(zh + 2) % 4, k, x], rows_), crecv.at[2, 5 * i])
    x_all(2)
    zmove((3, 0), 1, tile_rows(1 - half_before), B, 3, zrecv.at[2, 1 - half_before])
    zmove((3, 1), 3, tile_rows(3 - half_after), B, 1, zrecv.at[2, 3 - half_after])
    x_gc_core(2)
    for n in range(4):
        for d in (1, 3, 2):
            arrived(gr.at[(zl + n) % 4, (y + d) % 4], grecv.at[n, d])

    square = jnp.zeros((H, B), jnp.float32)
    for n in (0, 3, 1, 2):
        zp = (zh + n) % 4
        arrived(gc.at[zp, 1 - k], crecv.at[n, 6])
        for xp in range(4):
            right = jnp.concatenate([gc[zp, 0, xp], gc[zp, 1, xp]], axis=0)
            square = square + nn_dot(gr[zp, xp], right)
    pr[zl, k, y] = (coef_b * gr[zl, y].astype(jnp.float32) + coef_c * square).astype(jnp.bfloat16)

    def pr_at(zp, yp):
        return pr.at[zp, k, yp]

    def p_all(n):
        piece = pr_at((zl + n) % 4, y)
        for d in (2, 1, 3):
            send(piece, piece, psend.at[n, d], precv.at[n, 4 - d], at(dy=d))

    def p_core(n):
        for d in (1, 3, 2):
            arrived(pr_at((zl + n) % 4, (y + d) % 4), precv.at[n, d])
        zp = (zl + n) % 4
        send(pr.at[zp, k], pr.at[zp, k], psend.at[n, 5], precv.at[n, 5], at(dk=1))

    def product(n):
        zp = (zl + n) % 4
        arrived(pr.at[zp, 1 - k], precv.at[n, 5])

        def one(xp):
            return nn_dot(jnp.concatenate([pr[zp, 0, xp], pr[zp, 1, xp]], axis=0), unpack(zp, xp))

        acc[...] += (one(0) + one(1)) + (one(2) + one(3))

    zl_spread(pr_at, psend, precv)
    p_all(0)
    acc[...] = coef_a * x_ref[...].astype(jnp.float32)
    for n in (3, 1, 2):
        zl_wait(pr_at, precv, n)
        p_all(n)
    for t, up in late:
        zwait(2, t)
        x2_spread(t)
    p_core(0)
    for t, up in late:
        x2_forward(t, up)
    x_rest(1)
    x_rest(3)
    p_core(3)
    p_core(1)
    for t, up in early + late:
        x2_rest(t, up)
    product(0)
    product(3)
    p_core(2)
    product(1)
    product(2)
    o_ref[...] = (factor * acc[...]).astype(jnp.bfloat16)

    for copy in started:
        copy.wait_send()
    for dz in range(4):
        d, copy = sum3(dz)

        @pl.when(d != 0)
        def _(copy=copy):
            copy.wait_send()

    flip_copy(1 - k).wait_send()

    @pl.when(zh != zl)
    def _():
        flip_copy(k).wait_send()

    @pl.when(x != y)
    def _():
        swap_copy.wait_send()


def on_device(momentum):
    bf16, f32 = jnp.bfloat16, jnp.float32
    dma = pltpu.SemaphoreType.DMA
    return pl.pallas_call(
        kernel,
        out_shape=jax.ShapeDtypeStruct((B, W), bf16),
        in_specs=[pl.BlockSpec(memory_space=pltpu.HBM)],
        out_specs=pl.BlockSpec(memory_space=pltpu.VMEM),
        scratch_shapes=[
            pltpu.VMEM((B, W), bf16),
            pltpu.VMEM((4, 4, PACK, 128), bf16),
            pltpu.VMEM((4, 4 * B, B), f32),
            pltpu.VMEM((4, 4, H, B), bf16),
            pltpu.VMEM((4, 4, H, B), bf16),
            pltpu.VMEM((4, 3, H, B), bf16),
            pltpu.VMEM((4, 3, H, B), bf16),
            pltpu.VMEM((4, H, B), f32),
            pltpu.VMEM((4, H, B), bf16),
            pltpu.VMEM((4, H, B), bf16),
            pltpu.VMEM((H, B), bf16),
            pltpu.VMEM((H, B), bf16),
            pltpu.VMEM((2, H, H), bf16),
            pltpu.VMEM((2, H, H), bf16),
            pltpu.VMEM((H, B), f32),
            pltpu.VMEM((2, H, H), f32),
            pltpu.VMEM((4, 4, H, B), bf16),
            pltpu.VMEM((4, 2, 4, H, B), bf16),
            pltpu.VMEM((4, 2, 4, H, B), bf16),
            pltpu.VMEM((B, W), f32),
            dma,
            dma((4, 5)),
            dma((4, 5)),
            dma((3, 4, 2)),
            dma((4, 4, 2)),
            dma((3, 5)),
            dma((4, 5)),
            dma((5, 4)),
            dma((5, 4)),
            dma((3,)),
            dma((3,)),
            dma((4, 5)),
            dma((4, 5)),
            dma((4, 6)),
            dma((4, 7)),
            dma((4, 6)),
            dma((4, 6)),
        ],
        compiler_params=pltpu.CompilerParams(
            collective_id=0, has_side_effects=True, vmem_limit_bytes=60 * 2**20
        ),
        cost_estimate=pl.CostEstimate(flops=4 * 10**9, bytes_accessed=2 * 10**7, transcendentals=0),
    )(momentum)


def solution(mesh):
    return jax.shard_map(
        on_device, mesh=mesh, in_specs=(P("row", "col"),), out_specs=P("row", "col"), check_vma=False
    )
```

```python
import jax
import jax.numpy as jnp
from jax import lax
from jax.experimental import pallas as pl
from jax.experimental.pallas import tpu as pltpu
from jax.sharding import PartitionSpec as P

NR = 3584
NC = 18432

coef_a = 3.4445
coef_b = -4.775
coef_c = 2.0315
factor = 0.2 * max(NR, NC) ** 0.5

MESH = pl.DeviceIdType.MESH

B = 224
H = 112
W = 576
TILES = 4
PACK = TILES * B + H
LOW = (0, 2 * B)
HIGH = (2 * B, 2 * B + H)
FIRST = (0, 64)
SECOND = (64, 48)
REST = (TILES * B, H)


def nt_dot(a, b):
    return lax.dot_general(a, b, (((1,), (1,)), ((), ())), preferred_element_type=jnp.float32)


def nn_dot(a, b):
    return lax.dot_general(a, b, (((1,), (0,)), ((), ())), preferred_element_type=jnp.float32)


def kernel(
    x_hbm,
    o_ref,
    x_ref,
    xs,
    part,
    send1,
    recv1,
    send2,
    recv2,
    sum2,
    send3,
    recv3,
    swap_send,
    swap_recv,
    flip_send,
    flip_recv,
    swap_sum,
    flip_sum,
    gr,
    gc,
    pr,
    acc,
    load_sem,
    zsend,
    zrecv,
    xsend,
    xrecv,
    x2send,
    x2recv,
    rsend,
    rrecv,
    tsend,
    trecv,
    gsend,
    grecv,
    csend,
    crecv,
    psend,
    precv,
):
    row = lax.axis_index("row")
    col = lax.axis_index("col")
    x, zh = row // 4, row % 4
    y, zl, k = col // 8, (col // 2) % 4, col % 2
    sign = 1 + 2 * (zl % 2)

    def place(x_, zh_, y_, zl_, k_):
        return (x_ * 4 + zh_, y_ * 8 + zl_ * 2 + k_)

    def at(dx=0, dzh=0, dy=0, dzl=0, dk=0):
        return place((x + dx) % 4, (zh + dzh) % 4, (y + dy) % 4, (zl + dzl) % 4, (k + dk) % 2)

    def station(dz):
        return (zh + sign * dz) % 4

    started = []

    def send(src, dst, ssem, rsem, device):
        copy = pltpu.make_async_remote_copy(
            src_ref=src, dst_ref=dst, send_sem=ssem, recv_sem=rsem, device_id=device, device_id_type=MESH
        )
        copy.start()
        started.append(copy)

    def arrived(dst, rsem):
        pltpu.make_async_copy(dst, dst, rsem).wait()

    def rest(zp, xp):
        last = xs[zp, xp, pl.ds(TILES * B, H), :]
        return jnp.concatenate([last[:, :64], last[:, 64:]], axis=0)

    def tile_of(zp, xp, t):
        return xs[zp, xp, pl.ds(pl.multiple_of(t * B, 16), B), :]

    def unpack(zp, xp):
        return jnp.concatenate([tile_of(zp, xp, t) for t in range(TILES)] + [rest(zp, xp)], axis=1)

    load = pltpu.make_async_copy(x_hbm, x_ref, load_sem)
    load.start()
    barrier = pltpu.get_barrier_semaphore()
    peers = [at(dx=d) for d in (1, 2, 3)] + [at(dzh=d) for d in (1, 3)]
    peers += [at(dy=d) for d in (1, 2, 3)] + [at(dzl=d) for d in (1, 2, 3)] + [at(dk=1)]
    swap_peer = place(y, zh, x, zl, k)
    flip_peers = [place(x, zl, y, zh, n) for n in range(2)]
    for peer in peers:
        pl.semaphore_signal(barrier, 1, device_id=peer, device_id_type=MESH)

    load.wait()
    for t in range(TILES):
        xs[zh, x, pl.ds(t * B, B), :] = x_ref[:, pl.ds(t * 128, 128)]
    xs[zh, x, pl.ds(TILES * B, H), :] = jnp.concatenate(
        [x_ref[pl.ds(0, H), pl.ds(TILES * 128, 64)], x_ref[pl.ds(H, H), pl.ds(TILES * 128, 64)]], axis=1
    )
    pl.semaphore_wait(barrier, len(peers))

    def rows(dz, dx, start, size):
        return xs.at[station(dz), (x + dx) % 4, pl.ds(start, size)]

    def zmove(sem, dz, start, size, hop, rsem):
        piece = rows(dz, 0, start, size)
        send(piece, piece, zsend.at[sem], rsem, at(dzh=sign * hop))

    def xmove(kind, dz, dx, part_, hop):
        piece = rows(dz, dx, *(LOW, HIGH)[part_])
        send(piece, piece, xsend.at[kind, dz, part_], xrecv.at[dz, (dx - hop) % 4, part_], at(dx=hop))

    def xwait(dz, dx, part_):
        arrived(rows(dz, dx, *(LOW, HIGH)[part_]), xrecv.at[dz, dx, part_])

    def x_spread(dz, part_):
        xmove(0, dz, 0, part_, 1)
        xmove(1, dz, 0, part_, 3)

    def x_forward(dz, part_):
        source, hop = ((3, 1), (1, 3))[part_]
        xwait(dz, source, part_)
        xmove(2, dz, source, part_, hop)

    def x_rest(dz):
        for part_, source in ((0, 1), (1, 3)):
            xwait(dz, source, part_)
            xwait(dz, 2, part_)

    def tile_rows(t):
        return pl.multiple_of(t * B, 16)

    def zwait(dz, t):
        arrived(rows(dz, 0, tile_rows(t), B), zrecv.at[dz, t])

    def zwait_rest(dz):
        arrived(rows(dz, 0, *REST), zrecv.at[dz, 4])

    def x2_rows(dx, t):
        return rows(2, dx, *(REST if t is None else (tile_rows(t), B)))

    def x2_move(kind, dx, t, hop):
        piece, sem = x2_rows(dx, t), 4 if t is None else t
        send(piece, piece, x2send.at[kind, sem], x2recv.at[(dx - hop) % 4, sem], at(dx=hop))

    def x2_wait(dx, t):
        arrived(x2_rows(dx, t), x2recv.at[dx, 4 if t is None else t])

    def x2_spread(t):
        x2_move(0, 0, t, 1)
        x2_move(1, 0, t, 3)

    def x2_forward(t, up):
        source, hop = (3, 1) if up else (1, 3)
        x2_wait(source, t)
        x2_move(2, source, t, hop)

    def x2_rest(t, up):
        x2_wait(1 if up else 3, t)
        x2_wait(2, t)

    half = zh // 2
    half_before = ((zh + 4 - sign) % 4) // 2
    half_after = ((zh + sign) % 4) // 2

    def gram(dz):
        zp = station(dz)

        def stack(piece):
            return jnp.concatenate([piece(zh, xp) for xp in range(4)], axis=0)

        def dot(pieces):
            return nt_dot(
                jnp.concatenate([stack(piece) for piece in pieces], axis=1),
                jnp.concatenate([piece(zp, x) for piece in pieces], axis=1),
            )

        tiles = [lambda z_, x_, t=t: tile_of(z_, x_, t) for t in (0, 1, 2, 3, half, 2 + half)]
        if dz == 0:
            value = 0.5 * dot(tiles[:4] + [rest])
        elif dz == 1:
            value = dot(tiles[:2])
        elif dz == 3:
            value = dot(tiles[2:4] + [rest])
        else:
            value = dot(tiles[4:]) + 0.5 * dot([rest])
        part[dz] = value
        for xp in range(4):
            mine = pl.multiple_of(xp * B + (1 - k) * H, 16)
            send1[dz, xp] = part[dz, pl.ds(mine, H), :].astype(jnp.bfloat16)
        send(send1.at[dz], recv1.at[dz], rsend.at[0, dz], rrecv.at[0, dz], at(dk=1))

    def reduce_core(dz):
        arrived(recv1.at[dz], rrecv.at[0, dz])

        def both(xp):
            mine = pl.multiple_of(xp * B + k * H, 16)
            return part[dz, pl.ds(mine, H), :] + recv1[dz, xp].astype(jnp.float32)

        for dy in (2, 1, 3):
            send2[dz, dy - 1] = both((y + dy) % 4).astype(jnp.bfloat16)
            send(send2.at[dz, dy - 1], recv2.at[dz, dy - 1], rsend.at[dy, dz], rrecv.at[dy, dz], at(dy=dy))
        sum2[dz] = both(y)

    def sum3(dz):
        owner = station(dz)
        d = (owner + 4 - zl) % 4
        copy = pltpu.make_async_remote_copy(
            src_ref=send3.at[dz],
            dst_ref=recv3.at[d],
            send_sem=rsend.at[4, dz],
            recv_sem=rrecv.at[4, d],
            device_id=place(x, zh, y, owner, k),
            device_id_type=MESH,
        )
        return d, copy

    def reduce_y(dz):
        for dy in (1, 3, 2):
            arrived(recv2.at[dz, dy - 1], rrecv.at[dy, dz])
        total = sum2[dz]
        for dy in (1, 2, 3):
            total = total + recv2[dz, dy - 1].astype(jnp.float32)
        sum2[dz] = total
        send3[dz] = total.astype(jnp.bfloat16)
        d, copy = sum3(dz)

        @pl.when(d != 0)
        def _():
            copy.start()

    for t in (0, 1):
        zmove((0, t), 0, t * B, B, 3, zrecv.at[1, t])
        zmove((0, 2 + t), 0, (2 + t) * B, B, 1, zrecv.at[3, 2 + t])
        xmove(t, 0, 0, t, 1 + 2 * t)
    zmove((0, 4), 0, *REST, 1, zrecv.at[3, 4])
    for t in (0, 1):
        xmove(1 - t, 0, 0, t, 3 - 2 * t)
    x_forward(0, 0)
    x_forward(0, 1)
    zwait(1, half_before)
    zmove((2, 0), 1, tile_rows(half_before), B, 3, zrecv.at[2, half_before])
    zwait(3, 2 + half_after)
    zmove((2, 1), 3, tile_rows(2 + half_after), B, 1, zrecv.at[2, 2 + half_after])
    zwait_rest(3)
    zmove((2, 2), 3, *REST, 1, zrecv.at[2, 4])
    x_rest(0)
    gram(0)
    zwait(1, 1 - half_before)
    gram(1)
    x_spread(1, 0)
    reduce_core(0)
    zwait(3, 3 - half_after)
    gram(3)
    x_spread(3, 1)
    reduce_core(1)
    reduce_core(3)
    reduce_y(0)
    zwait(2, half)
    zwait(2, 2 + half)
    zwait_rest(2)
    gram(2)
    zmove((1, 0), 0, *HIGH, 3, zrecv.at[1, 2])
    zmove((1, 1), 0, *LOW, 1, zrecv.at[3, 0])
    early = ((half, True), (2 + half, False), (None, True))
    late = ((1 - half, True), (3 - half, False))
    for t, up in early:
        x2_spread(t)
    reduce_y(1)
    reduce_core(2)
    reduce_y(3)
    x_forward(1, 0)
    x_forward(3, 1)
    reduce_y(2)

    total = sum2[(sign * (zl + 4 - zh)) % 4]
    for d in (1, 2, 3):
        arrived(recv3.at[d], rrecv.at[4, d])
        total = total + recv3[d].astype(jnp.float32)

    swap_send[...] = total.astype(jnp.bfloat16)
    flipped = total.T
    for n in range(2):
        flip_send[n] = flipped[n * H : (n + 1) * H, :].astype(jnp.bfloat16)
    swap_copy = pltpu.make_async_remote_copy(
        src_ref=swap_send,
        dst_ref=swap_recv,
        send_sem=tsend.at[0],
        recv_sem=trecv.at[0],
        device_id=swap_peer,
        device_id_type=MESH,
    )

    def flip_copy(n):
        return pltpu.make_async_remote_copy(
            src_ref=flip_send.at[n],
            dst_ref=flip_recv.at[k],
            send_sem=tsend.at[1 + n],
            recv_sem=trecv.at[1 + k],
            device_id=(flip_peers[0][0], y * 8 + zh * 2 + n),
            device_id_type=MESH,
        )

    @pl.when(x != y)
    def _():
        swap_copy.start()

    @pl.when(x == y)
    def _():
        swap_sum[...] = total

    flip_copy(1 - k).start()

    @pl.when(zh != zl)
    def _():
        flip_copy(k).start()

    @pl.when(zh == zl)
    def _():
        swap_send2 = jnp.where(k == 0, flipped[:H, :], flipped[H:, :])
        flip_sum[k] = swap_send2

    for t, up in early:
        x2_forward(t, up)
    arrived(rows(1, 0, *HIGH), zrecv.at[1, 2])
    x_spread(1, 1)
    arrived(rows(3, 0, *LOW), zrecv.at[3, 0])
    x_spread(3, 0)

    @pl.when(x != y)
    def _():
        arrived(swap_recv, trecv.at[0])
        swap_sum[...] = swap_recv[...].astype(jnp.float32)

    @pl.when(zh != zl)
    def _():
        arrived(flip_recv.at[k], trecv.at[1 + k])
        flip_sum[k] = flip_recv[k].astype(jnp.float32)

    arrived(flip_recv.at[1 - k], trecv.at[2 - k])
    flip_sum[1 - k] = flip_recv[1 - k].astype(jnp.float32)
    tile = (swap_sum[...] + jnp.concatenate([flip_sum[0], flip_sum[1]], axis=1)).astype(jnp.bfloat16)

    gr[zl, y] = tile
    gc[zh, k, x] = tile

    def cut(ref, piece):
        return ref.at[pl.ds(*piece)]

    def zl_spread(buf, ssem, rsem):
        piece = buf(zl, y)
        for d in (1, 3, 2):
            send(piece, piece, ssem.at[d, 4], rsem.at[4 - d, 0], at(dzl=d))

    def zl_wait(buf, rsem, n):
        arrived(buf((zl + n) % 4, y), rsem.at[n, 0])

    def y_all(n):
        piece = gr.at[(zl + n) % 4, y]
        for d in (2, 1, 3):
            send(piece, piece, gsend.at[n, d], grecv.at[n, 4 - d], at(dy=d))

    def x_all(n):
        piece = gc.at[(zh + n) % 4, k, x]
        for d in (2, 1, 3):
            send(piece, piece, csend.at[n, d], crecv.at[n, 4 - d], at(dx=d))

    def x_gc_core(n):
        zp = (zh + n) % 4
        for d in (1, 3, 2):
            arrived(gc.at[zp, k, (x + d) % 4], crecv.at[n, d])
        send(gc.at[zp, k], gc.at[zp, k], csend.at[n, 4], crecv.at[n, 6], at(dk=1))

    def gr_at(zp, yp):
        return gr.at[zp, yp]

    for i, hop in enumerate((1, 3)):
        send(gc.at[zh, k, x], gc.at[zh, k, x], csend.at[2 * i, 5], crecv.at[4 - hop, 0], at(dzh=hop))
    x_all(0)
    y_all(0)
    x_gc_core(0)
    zl_spread(gr_at, gsend, grecv)
    x_forward(1, 1)
    x_forward(3, 0)
    for i, (source, hop, rows_) in enumerate(((3, 1, FIRST), (1, 3, SECOND))):
        whole = gc.at[(zh + source) % 4, k, x]
        arrived(whole, crecv.at[source, 0])
        send(cut(whole, rows_), cut(whole, rows_), csend.at[1 + 2 * i, 5], crecv.at[2, 5 * i], at(dzh=hop))
        x_all(source)
    for n in (3, 1, 2):
        zl_wait(gr_at, grecv, n)
        y_all(n)
    x_gc_core(3)
    x_gc_core(1)
    for i, rows_ in enumerate((FIRST, SECOND)):
        arrived(cut(gc.at[(zh + 2) % 4, k, x], rows_), crecv.at[2, 5 * i])
    x_all(2)
    zmove((3, 0), 1, tile_rows(1 - half_before), B, 3, zrecv.at[2, 1 - half_before])
    zmove((3, 1), 3, tile_rows(3 - half_after), B, 1, zrecv.at[2, 3 - half_after])
    x_gc_core(2)
    for n in range(4):
        for d in (1, 3, 2):
            arrived(gr.at[(zl + n) % 4, (y + d) % 4], grecv.at[n, d])

    square = jnp.zeros((H, B), jnp.float32)
    for n in (0, 3, 1, 2):
        zp = (zh + n) % 4
        arrived(gc.at[zp, 1 - k], crecv.at[n, 6])
        for xp in range(4):
            right = jnp.concatenate([gc[zp, 0, xp], gc[zp, 1, xp]], axis=0)
            square = square + nn_dot(gr[zp, xp], right)
    pr[zl, k, y] = (coef_b * gr[zl, y].astype(jnp.float32) + coef_c * square).astype(jnp.bfloat16)

    def pr_at(zp, yp):
        return pr.at[zp, k, yp]

    def p_all(n):
        piece = pr_at((zl + n) % 4, y)
        for d in (2, 1, 3):
            send(piece, piece, psend.at[n, d], precv.at[n, 4 - d], at(dy=d))

    def p_core(n):
        for d in (1, 3, 2):
            arrived(pr_at((zl + n) % 4, (y + d) % 4), precv.at[n, d])
        zp = (zl + n) % 4
        send(pr.at[zp, k], pr.at[zp, k], psend.at[n, 5], precv.at[n, 5], at(dk=1))

    def product(n):
        zp = (zl + n) % 4
        arrived(pr.at[zp, 1 - k], precv.at[n, 5])

        def one(xp):
            return nn_dot(jnp.concatenate([pr[zp, 0, xp], pr[zp, 1, xp]], axis=0), unpack(zp, xp))

        acc[...] += (one(0) + one(1)) + (one(2) + one(3))

    zl_spread(pr_at, psend, precv)
    p_all(0)
    for t, up in late:
        zwait(2, t)
        x2_spread(t)
    acc[...] = coef_a * x_ref[...].astype(jnp.float32)
    for n in (3, 1, 2):
        zl_wait(pr_at, precv, n)
        p_all(n)
    p_core(0)
    for t, up in late:
        x2_forward(t, up)
    x_rest(1)
    x_rest(3)
    p_core(3)
    p_core(1)
    for t, up in early + late:
        x2_rest(t, up)
    product(0)
    product(3)
    p_core(2)
    product(1)
    product(2)
    o_ref[...] = (factor * acc[...]).astype(jnp.bfloat16)

    for copy in started:
        copy.wait_send()
    for dz in range(4):
        d, copy = sum3(dz)

        @pl.when(d != 0)
        def _(copy=copy):
            copy.wait_send()

    flip_copy(1 - k).wait_send()

    @pl.when(zh != zl)
    def _():
        flip_copy(k).wait_send()

    @pl.when(x != y)
    def _():
        swap_copy.wait_send()


def on_device(momentum):
    bf16, f32 = jnp.bfloat16, jnp.float32
    dma = pltpu.SemaphoreType.DMA
    return pl.pallas_call(
        kernel,
        out_shape=jax.ShapeDtypeStruct((B, W), bf16),
        in_specs=[pl.BlockSpec(memory_space=pltpu.HBM)],
        out_specs=pl.BlockSpec(memory_space=pltpu.VMEM),
        scratch_shapes=[
            pltpu.VMEM((B, W), bf16),
            pltpu.VMEM((4, 4, PACK, 128), bf16),
            pltpu.VMEM((4, 4 * B, B), f32),
            pltpu.VMEM((4, 4, H, B), bf16),
            pltpu.VMEM((4, 4, H, B), bf16),
            pltpu.VMEM((4, 3, H, B), bf16),
            pltpu.VMEM((4, 3, H, B), bf16),
            pltpu.VMEM((4, H, B), f32),
            pltpu.VMEM((4, H, B), bf16),
            pltpu.VMEM((4, H, B), bf16),
            pltpu.VMEM((H, B), bf16),
            pltpu.VMEM((H, B), bf16),
            pltpu.VMEM((2, H, H), bf16),
            pltpu.VMEM((2, H, H), bf16),
            pltpu.VMEM((H, B), f32),
            pltpu.VMEM((2, H, H), f32),
            pltpu.VMEM((4, 4, H, B), bf16),
            pltpu.VMEM((4, 2, 4, H, B), bf16),
            pltpu.VMEM((4, 2, 4, H, B), bf16),
            pltpu.VMEM((B, W), f32),
            dma,
            dma((4, 5)),
            dma((4, 5)),
            dma((3, 4, 2)),
            dma((4, 4, 2)),
            dma((3, 5)),
            dma((4, 5)),
            dma((5, 4)),
            dma((5, 4)),
            dma((3,)),
            dma((3,)),
            dma((4, 5)),
            dma((4, 5)),
            dma((4, 6)),
            dma((4, 7)),
            dma((4, 6)),
            dma((4, 6)),
        ],
        compiler_params=pltpu.CompilerParams(
            collective_id=0, has_side_effects=True, vmem_limit_bytes=60 * 2**20
        ),
        cost_estimate=pl.CostEstimate(flops=4 * 10**9, bytes_accessed=2 * 10**7, transcendentals=0),
    )(momentum)


def solution(mesh):
    return jax.shard_map(
        on_device, mesh=mesh, in_specs=(P("row", "col"),), out_specs=P("row", "col"), check_vma=False
    )
```

```python
import jax
import jax.numpy as jnp
from jax import lax
from jax.experimental import pallas as pl
from jax.experimental.pallas import tpu as pltpu
from jax.sharding import PartitionSpec as P

NR = 3584
NC = 18432

coef_a = 3.4445
coef_b = -4.775
coef_c = 2.0315
factor = 0.2 * max(NR, NC) ** 0.5

MESH = pl.DeviceIdType.MESH

B = 224
H = 112
W = 576
TILES = 4
PACK = TILES * B + H
LOW = (0, 2 * B)
HIGH = (2 * B, 2 * B + H)
FIRST = (0, 64)
SECOND = (64, 48)
REST = (TILES * B, H)


def nt_dot(a, b):
    return lax.dot_general(a, b, (((1,), (1,)), ((), ())), preferred_element_type=jnp.float32)


def nn_dot(a, b):
    return lax.dot_general(a, b, (((1,), (0,)), ((), ())), preferred_element_type=jnp.float32)


def kernel(
    x_hbm,
    o_ref,
    x_ref,
    xs,
    part,
    send1,
    recv1,
    send2,
    recv2,
    sum2,
    send3,
    recv3,
    swap_send,
    swap_recv,
    flip_send,
    flip_recv,
    swap_sum,
    flip_sum,
    gr,
    gc,
    pr,
    acc,
    load_sem,
    zsend,
    zrecv,
    xsend,
    xrecv,
    x2send,
    x2recv,
    rsend,
    rrecv,
    tsend,
    trecv,
    gsend,
    grecv,
    csend,
    crecv,
    psend,
    precv,
):
    row = lax.axis_index("row")
    col = lax.axis_index("col")
    x, zh = row // 4, row % 4
    y, zl, k = col // 8, (col // 2) % 4, col % 2
    sign = 1 + 2 * (zl % 2)

    def place(x_, zh_, y_, zl_, k_):
        return (x_ * 4 + zh_, y_ * 8 + zl_ * 2 + k_)

    def at(dx=0, dzh=0, dy=0, dzl=0, dk=0):
        return place((x + dx) % 4, (zh + dzh) % 4, (y + dy) % 4, (zl + dzl) % 4, (k + dk) % 2)

    def station(dz):
        return (zh + sign * dz) % 4

    started = []

    def send(src, dst, ssem, rsem, device):
        copy = pltpu.make_async_remote_copy(
            src_ref=src, dst_ref=dst, send_sem=ssem, recv_sem=rsem, device_id=device, device_id_type=MESH
        )
        copy.start()
        started.append(copy)

    def arrived(dst, rsem):
        pltpu.make_async_copy(dst, dst, rsem).wait()

    def rest(zp, xp):
        last = xs[zp, xp, pl.ds(TILES * B, H), :]
        return jnp.concatenate([last[:, :64], last[:, 64:]], axis=0)

    def tile_of(zp, xp, t):
        return xs[zp, xp, pl.ds(pl.multiple_of(t * B, 16), B), :]

    def unpack(zp, xp):
        return jnp.concatenate([tile_of(zp, xp, t) for t in range(TILES)] + [rest(zp, xp)], axis=1)

    load = pltpu.make_async_copy(x_hbm, x_ref, load_sem)
    load.start()
    barrier = pltpu.get_barrier_semaphore()
    peers = [at(dx=d) for d in (1, 2, 3)] + [at(dzh=d) for d in (1, 3)]
    peers += [at(dy=d) for d in (1, 2, 3)] + [at(dzl=d) for d in (1, 2, 3)] + [at(dk=1)]
    swap_peer = place(y, zh, x, zl, k)
    flip_peers = [place(x, zl, y, zh, n) for n in range(2)]
    for peer in peers:
        pl.semaphore_signal(barrier, 1, device_id=peer, device_id_type=MESH)

    load.wait()
    for t in range(TILES):
        xs[zh, x, pl.ds(t * B, B), :] = x_ref[:, pl.ds(t * 128, 128)]
    xs[zh, x, pl.ds(TILES * B, H), :] = jnp.concatenate(
        [x_ref[pl.ds(0, H), pl.ds(TILES * 128, 64)], x_ref[pl.ds(H, H), pl.ds(TILES * 128, 64)]], axis=1
    )
    pl.semaphore_wait(barrier, len(peers))

    def rows(dz, dx, start, size):
        return xs.at[station(dz), (x + dx) % 4, pl.ds(start, size)]

    def zmove(sem, dz, start, size, hop, rsem):
        piece = rows(dz, 0, start, size)
        send(piece, piece, zsend.at[sem], rsem, at(dzh=sign * hop))

    def xmove(kind, dz, dx, part_, hop):
        piece = rows(dz, dx, *(LOW, HIGH)[part_])
        send(piece, piece, xsend.at[kind, dz, part_], xrecv.at[dz, (dx - hop) % 4, part_], at(dx=hop))

    def xwait(dz, dx, part_):
        arrived(rows(dz, dx, *(LOW, HIGH)[part_]), xrecv.at[dz, dx, part_])

    def x_spread(dz, part_):
        xmove(0, dz, 0, part_, 1)
        xmove(1, dz, 0, part_, 3)

    def x_forward(dz, part_):
        source, hop = ((3, 1), (1, 3))[part_]
        xwait(dz, source, part_)
        xmove(2, dz, source, part_, hop)

    def x_rest(dz):
        for part_, source in ((0, 1), (1, 3)):
            xwait(dz, source, part_)
            xwait(dz, 2, part_)

    def tile_rows(t):
        return pl.multiple_of(t * B, 16)

    def zwait(dz, t):
        arrived(rows(dz, 0, tile_rows(t), B), zrecv.at[dz, t])

    def zwait_rest(dz):
        arrived(rows(dz, 0, *REST), zrecv.at[dz, 4])

    def x2_rows(dx, t):
        return rows(2, dx, *(REST if t is None else (tile_rows(t), B)))

    def x2_move(kind, dx, t, hop):
        piece, sem = x2_rows(dx, t), 4 if t is None else t
        send(piece, piece, x2send.at[kind, sem], x2recv.at[(dx - hop) % 4, sem], at(dx=hop))

    def x2_wait(dx, t):
        arrived(x2_rows(dx, t), x2recv.at[dx, 4 if t is None else t])

    def x2_spread(t):
        x2_move(0, 0, t, 1)
        x2_move(1, 0, t, 3)

    def x2_forward(t, up):
        source, hop = (3, 1) if up else (1, 3)
        x2_wait(source, t)
        x2_move(2, source, t, hop)

    def x2_rest(t, up):
        x2_wait(1 if up else 3, t)
        x2_wait(2, t)

    half = zh // 2
    half_before = ((zh + 4 - sign) % 4) // 2
    half_after = ((zh + sign) % 4) // 2

    def gram(dz):
        zp = station(dz)

        def stack(piece):
            return jnp.concatenate([piece(zh, xp) for xp in range(4)], axis=0)

        def dot(pieces):
            return nt_dot(
                jnp.concatenate([stack(piece) for piece in pieces], axis=1),
                jnp.concatenate([piece(zp, x) for piece in pieces], axis=1),
            )

        tiles = [lambda z_, x_, t=t: tile_of(z_, x_, t) for t in (0, 1, 2, 3, half, 2 + half)]
        if dz == 0:
            value = 0.5 * dot(tiles[:4] + [rest])
        elif dz == 1:
            value = dot(tiles[:2])
        elif dz == 3:
            value = dot(tiles[2:4] + [rest])
        else:
            value = dot(tiles[4:]) + 0.5 * dot([rest])
        part[dz] = value
        for xp in range(4):
            mine = pl.multiple_of(xp * B + (1 - k) * H, 16)
            send1[dz, xp] = part[dz, pl.ds(mine, H), :].astype(jnp.bfloat16)
        send(send1.at[dz], recv1.at[dz], rsend.at[0, dz], rrecv.at[0, dz], at(dk=1))

    def reduce_core(dz):
        arrived(recv1.at[dz], rrecv.at[0, dz])

        def both(xp):
            mine = pl.multiple_of(xp * B + k * H, 16)
            return part[dz, pl.ds(mine, H), :] + recv1[dz, xp].astype(jnp.float32)

        for dy in (2, 1, 3):
            send2[dz, dy - 1] = both((y + dy) % 4).astype(jnp.bfloat16)
            send(send2.at[dz, dy - 1], recv2.at[dz, dy - 1], rsend.at[dy, dz], rrecv.at[dy, dz], at(dy=dy))
        sum2[dz] = both(y)

    def sum3(dz):
        owner = station(dz)
        d = (owner + 4 - zl) % 4
        copy = pltpu.make_async_remote_copy(
            src_ref=send3.at[dz],
            dst_ref=recv3.at[d],
            send_sem=rsend.at[4, dz],
            recv_sem=rrecv.at[4, d],
            device_id=place(x, zh, y, owner, k),
            device_id_type=MESH,
        )
        return d, copy

    def reduce_y(dz):
        for dy in (1, 3, 2):
            arrived(recv2.at[dz, dy - 1], rrecv.at[dy, dz])
        total = sum2[dz]
        for dy in (1, 2, 3):
            total = total + recv2[dz, dy - 1].astype(jnp.float32)
        sum2[dz] = total
        send3[dz] = total.astype(jnp.bfloat16)
        d, copy = sum3(dz)

        @pl.when(d != 0)
        def _():
            copy.start()

    for t in (0, 1):
        zmove((0, t), 0, t * B, B, 3, zrecv.at[1, t])
        zmove((0, 2 + t), 0, (2 + t) * B, B, 1, zrecv.at[3, 2 + t])
        xmove(t, 0, 0, t, 1 + 2 * t)
    zmove((0, 4), 0, *REST, 1, zrecv.at[3, 4])
    for t in (0, 1):
        xmove(1 - t, 0, 0, t, 3 - 2 * t)
    x_forward(0, 0)
    x_forward(0, 1)
    zwait(1, half_before)
    zmove((2, 0), 1, tile_rows(half_before), B, 3, zrecv.at[2, half_before])
    zwait(3, 2 + half_after)
    zmove((2, 1), 3, tile_rows(2 + half_after), B, 1, zrecv.at[2, 2 + half_after])
    zwait_rest(3)
    zmove((2, 2), 3, *REST, 1, zrecv.at[2, 4])
    x_rest(0)
    gram(0)
    zwait(1, 1 - half_before)
    gram(1)
    x_spread(1, 0)
    reduce_core(0)
    zwait(3, 3 - half_after)
    gram(3)
    x_spread(3, 1)
    reduce_core(1)
    reduce_core(3)
    reduce_y(0)
    zwait(2, half)
    zwait(2, 2 + half)
    zwait_rest(2)
    gram(2)
    zmove((1, 0), 0, *HIGH, 3, zrecv.at[1, 2])
    zmove((1, 1), 0, *LOW, 1, zrecv.at[3, 0])
    early = ((half, True), (2 + half, False), (None, True))
    late = ((1 - half, True), (3 - half, False))
    for t, up in early:
        x2_spread(t)
    reduce_y(1)
    reduce_core(2)
    reduce_y(3)
    x_forward(1, 0)
    x_forward(3, 1)
    reduce_y(2)

    total = sum2[(sign * (zl + 4 - zh)) % 4]
    for d in (1, 2, 3):
        arrived(recv3.at[d], rrecv.at[4, d])
        total = total + recv3[d].astype(jnp.float32)

    swap_send[...] = total.astype(jnp.bfloat16)
    flipped = total.T
    for n in range(2):
        flip_send[n] = flipped[n * H : (n + 1) * H, :].astype(jnp.bfloat16)
    swap_copy = pltpu.make_async_remote_copy(
        src_ref=swap_send,
        dst_ref=swap_recv,
        send_sem=tsend.at[0],
        recv_sem=trecv.at[0],
        device_id=swap_peer,
        device_id_type=MESH,
    )

    def flip_copy(n):
        return pltpu.make_async_remote_copy(
            src_ref=flip_send.at[n],
            dst_ref=flip_recv.at[k],
            send_sem=tsend.at[1 + n],
            recv_sem=trecv.at[1 + k],
            device_id=(flip_peers[0][0], y * 8 + zh * 2 + n),
            device_id_type=MESH,
        )

    @pl.when(x != y)
    def _():
        swap_copy.start()

    @pl.when(x == y)
    def _():
        swap_sum[...] = total

    flip_copy(1 - k).start()

    @pl.when(zh != zl)
    def _():
        flip_copy(k).start()

    @pl.when(zh == zl)
    def _():
        swap_send2 = jnp.where(k == 0, flipped[:H, :], flipped[H:, :])
        flip_sum[k] = swap_send2

    for t, up in early:
        x2_forward(t, up)
    arrived(rows(1, 0, *HIGH), zrecv.at[1, 2])
    x_spread(1, 1)
    arrived(rows(3, 0, *LOW), zrecv.at[3, 0])
    x_spread(3, 0)

    @pl.when(x != y)
    def _():
        arrived(swap_recv, trecv.at[0])
        swap_sum[...] = swap_recv[...].astype(jnp.float32)

    @pl.when(zh != zl)
    def _():
        arrived(flip_recv.at[k], trecv.at[1 + k])
        flip_sum[k] = flip_recv[k].astype(jnp.float32)

    arrived(flip_recv.at[1 - k], trecv.at[2 - k])
    flip_sum[1 - k] = flip_recv[1 - k].astype(jnp.float32)
    tile = (swap_sum[...] + jnp.concatenate([flip_sum[0], flip_sum[1]], axis=1)).astype(jnp.bfloat16)

    gr[zl, y] = tile
    gc[zh, k, x] = tile

    def cut(ref, piece):
        return ref.at[pl.ds(*piece)]

    def zl_spread(buf, ssem, rsem):
        piece = buf(zl, y)
        for d in (1, 3, 2):
            send(piece, piece, ssem.at[d, 4], rsem.at[4 - d, 0], at(dzl=d))

    def zl_wait(buf, rsem, n):
        arrived(buf((zl + n) % 4, y), rsem.at[n, 0])

    def y_all(n):
        piece = gr.at[(zl + n) % 4, y]
        for d in (2, 1, 3):
            send(piece, piece, gsend.at[n, d], grecv.at[n, 4 - d], at(dy=d))

    def x_all(n):
        piece = gc.at[(zh + n) % 4, k, x]
        for d in (2, 1, 3):
            send(piece, piece, csend.at[n, d], crecv.at[n, 4 - d], at(dx=d))

    def x_gc_core(n):
        zp = (zh + n) % 4
        for d in (1, 3, 2):
            arrived(gc.at[zp, k, (x + d) % 4], crecv.at[n, d])
        send(gc.at[zp, k], gc.at[zp, k], csend.at[n, 4], crecv.at[n, 6], at(dk=1))

    def gr_at(zp, yp):
        return gr.at[zp, yp]

    for i, hop in enumerate((1, 3)):
        send(gc.at[zh, k, x], gc.at[zh, k, x], csend.at[2 * i, 5], crecv.at[4 - hop, 0], at(dzh=hop))
    x_all(0)
    y_all(0)
    x_gc_core(0)
    zl_spread(gr_at, gsend, grecv)
    x_forward(1, 1)
    x_forward(3, 0)
    for i, (source, hop, rows_) in enumerate(((3, 1, FIRST), (1, 3, SECOND))):
        whole = gc.at[(zh + source) % 4, k, x]
        arrived(whole, crecv.at[source, 0])
        send(cut(whole, rows_), cut(whole, rows_), csend.at[1 + 2 * i, 5], crecv.at[2, 5 * i], at(dzh=hop))
        x_all(source)
    for n in (3, 1, 2):
        zl_wait(gr_at, grecv, n)
        y_all(n)
    x_gc_core(3)
    x_gc_core(1)
    for i, rows_ in enumerate((FIRST, SECOND)):
        arrived(cut(gc.at[(zh + 2) % 4, k, x], rows_), crecv.at[2, 5 * i])
    x_all(2)
    zmove((3, 0), 1, tile_rows(1 - half_before), B, 3, zrecv.at[2, 1 - half_before])
    zmove((3, 1), 3, tile_rows(3 - half_after), B, 1, zrecv.at[2, 3 - half_after])
    x_gc_core(2)
    for n in range(4):
        for d in (1, 3, 2):
            arrived(gr.at[(zl + n) % 4, (y + d) % 4], grecv.at[n, d])

    square = jnp.zeros((H, B), jnp.float32)
    for n in (0, 3, 1, 2):
        zp = (zh + n) % 4
        arrived(gc.at[zp, 1 - k], crecv.at[n, 6])
        for xp in range(4):
            right = jnp.concatenate([gc[zp, 0, xp], gc[zp, 1, xp]], axis=0)
            square = square + nn_dot(gr[zp, xp], right)
    pr[zl, k, y] = (coef_b * gr[zl, y].astype(jnp.float32) + coef_c * square).astype(jnp.bfloat16)

    def pr_at(zp, yp):
        return pr.at[zp, k, yp]

    def p_all(n):
        piece = pr_at((zl + n) % 4, y)
        for d in (2, 1, 3):
            send(piece, piece, psend.at[n, d], precv.at[n, 4 - d], at(dy=d))

    def p_core(n):
        for d in (1, 3, 2):
            arrived(pr_at((zl + n) % 4, (y + d) % 4), precv.at[n, d])
        zp = (zl + n) % 4
        send(pr.at[zp, k], pr.at[zp, k], psend.at[n, 5], precv.at[n, 5], at(dk=1))

    def product(n):
        zp = (zl + n) % 4
        arrived(pr.at[zp, 1 - k], precv.at[n, 5])

        def one(xp):
            return nn_dot(jnp.concatenate([pr[zp, 0, xp], pr[zp, 1, xp]], axis=0), unpack(zp, xp))

        acc[...] += (one(0) + one(1)) + (one(2) + one(3))

    zl_spread(pr_at, psend, precv)
    p_all(0)
    for t, up in late:
        zwait(2, t)
        x2_spread(t)
    acc[...] = coef_a * x_ref[...].astype(jnp.float32)
    for n in (3, 1, 2):
        zl_wait(pr_at, precv, n)
        p_all(n)
    p_core(0)
    for t, up in late:
        x2_forward(t, up)
    x_rest(1)
    x_rest(3)
    p_core(3)
    p_core(1)
    for t, up in early + late:
        x2_rest(t, up)
    product(0)
    p_core(2)
    product(3)
    product(1)
    product(2)
    o_ref[...] = (factor * acc[...]).astype(jnp.bfloat16)

    for copy in started:
        copy.wait_send()
    for dz in range(4):
        d, copy = sum3(dz)

        @pl.when(d != 0)
        def _(copy=copy):
            copy.wait_send()

    flip_copy(1 - k).wait_send()

    @pl.when(zh != zl)
    def _():
        flip_copy(k).wait_send()

    @pl.when(x != y)
    def _():
        swap_copy.wait_send()


def on_device(momentum):
    bf16, f32 = jnp.bfloat16, jnp.float32
    dma = pltpu.SemaphoreType.DMA
    return pl.pallas_call(
        kernel,
        out_shape=jax.ShapeDtypeStruct((B, W), bf16),
        in_specs=[pl.BlockSpec(memory_space=pltpu.HBM)],
        out_specs=pl.BlockSpec(memory_space=pltpu.VMEM),
        scratch_shapes=[
            pltpu.VMEM((B, W), bf16),
            pltpu.VMEM((4, 4, PACK, 128), bf16),
            pltpu.VMEM((4, 4 * B, B), f32),
            pltpu.VMEM((4, 4, H, B), bf16),
            pltpu.VMEM((4, 4, H, B), bf16),
            pltpu.VMEM((4, 3, H, B), bf16),
            pltpu.VMEM((4, 3, H, B), bf16),
            pltpu.VMEM((4, H, B), f32),
            pltpu.VMEM((4, H, B), bf16),
            pltpu.VMEM((4, H, B), bf16),
            pltpu.VMEM((H, B), bf16),
            pltpu.VMEM((H, B), bf16),
            pltpu.VMEM((2, H, H), bf16),
            pltpu.VMEM((2, H, H), bf16),
            pltpu.VMEM((H, B), f32),
            pltpu.VMEM((2, H, H), f32),
            pltpu.VMEM((4, 4, H, B), bf16),
            pltpu.VMEM((4, 2, 4, H, B), bf16),
            pltpu.VMEM((4, 2, 4, H, B), bf16),
            pltpu.VMEM((B, W), f32),
            dma,
            dma((4, 5)),
            dma((4, 5)),
            dma((3, 4, 2)),
            dma((4, 4, 2)),
            dma((3, 5)),
            dma((4, 5)),
            dma((5, 4)),
            dma((5, 4)),
            dma((3,)),
            dma((3,)),
            dma((4, 5)),
            dma((4, 5)),
            dma((4, 6)),
            dma((4, 7)),
            dma((4, 6)),
            dma((4, 6)),
        ],
        compiler_params=pltpu.CompilerParams(
            collective_id=0, has_side_effects=True, vmem_limit_bytes=60 * 2**20
        ),
        cost_estimate=pl.CostEstimate(flops=4 * 10**9, bytes_accessed=2 * 10**7, transcendentals=0),
    )(momentum)


def solution(mesh):
    return jax.shard_map(
        on_device, mesh=mesh, in_specs=(P("row", "col"),), out_specs=P("row", "col"), check_vma=False
    )
```
